32 devices in a mesh: groups: 2 (over x), dev: 16 (over z, y, core).
Axes of the slice: x: 2, y: 2, z: 4, core: 2. Of those that a mesh axis runs over, the one named last changes fastest.
Arguments:
- image_rows: bfloat16 [512, 2560], P(('groups', 'dev')), parts along dimension 0, may hold values from -6 to 6
- text_hidden: bfloat16 [512, 4096], P('groups', 'dev'), parts along dimension 0, may hold values from -6 to 6
- caption_weight: bfloat16 [4096, 2560], P('dev'), may hold values from -0.09375 to 0.09375
- mod_scale: float32 [2560], replicated, may hold values from 0.5 to 1.5
- mod_shift: float32 [2560], replicated, may hold values from -3 to 3
- router_weight: float32 [2560, 4], replicated, may hold values from -0.125 to 0.125
- image_experts: int32 [512, 2], P(('groups', 'dev')), parts along dimension 0, may hold values from 0 to 3, all different within a row; in each aligned block of 16 rows (0 to 15, 16 to 31, ...) at most 12 rows name the same one
- caption_experts: int32 [512, 2], P(('groups', 'dev')), parts along dimension 0, may hold values from 0 to 3, all different within a row; in each aligned block of 16 rows (0 to 15, 16 to 31, ...) at most 9 rows name the same one
- prompt_lengths: int32 [4], P('groups'), parts along dimension 0, may hold values from 1 to 128, as said below
- w_gate: bfloat16 [2560, 27648], P(None, 'dev'), may hold values from -0.125 to 0.125
- w_up: bfloat16 [2560, 27648], P(None, 'dev'), may hold values from -0.125 to 0.125
- w_down: bfloat16 [27648, 2560], P('dev'), may hold values from -0.078125 to 0.078125
Outputs:
- image_out: bfloat16 [512, 2560], P(('groups', 'dev')), parts along dimension 0
- caption_out: bfloat16 [512, 2560], P(('groups', 'dev')), parts along dimension 0
The draws below stay inside these ranges and needn't reach their ends.
There are 2 independent parts, one for each index of `groups`. The reference program is written for one: setup_inputs(seed, part) draws one part's arguments, and reference() takes and returns one part's arrays. A program takes and returns all parts, laid end to end along the dimension named above; an argument that names none is the same for every part. Nothing has to cross between parts.
Inputs may be any that keep to these rules, and one draw needn't show every extreme that they name: `image_experts`: in each aligned block of 16 rows (the rows of one device) no expert is named by more than 12 rows, a bound that some block reaches; a row names two different experts. `caption_experts`: in each aligned block of 16 rows (the rows of one device) no expert is named by more than 9 rows, a bound that some block reaches; a row names two different experts. `prompt_lengths`: one prompt has exactly 128 live tokens.
All inputs are finite; a program needn't handle non-finite values.
Results may differ from the reference program's by a relative error of at most 0.018.
Values may be sent and summed in bfloat16 or wider, within the bound.
No kernel may reach another device: no remote copies, remote signals or barrier semaphores. Data moves between devices by JAX's collectives and lax.ppermute only.
A program may use at most 128 MiB of HBM per device.

```python
import math
import jax
import jax.numpy as jnp
import numpy as np
from jax import lax

D = 2560
LLAMA = 4096
FF = 6912
EXPERTS = 4
TOP = 2
PROMPTS = 2
PLEN = 128
IMG_DEV = 16
CAP_IMG = 12
IMAGE = 256
TEXT = 256
TXT_DEV = 16
TXT_CAP = 9
N_DEV = 16


def draw_prompt_lengths(key, part):
    key = jax.random.fold_in(key, 7)
    first_key, second_key = jax.random.split(key)
    drawn_lengths = jax.random.randint(first_key, (PROMPTS,), 1, PLEN + 1)
    longest = jax.random.randint(second_key, (), 0, PROMPTS)
    return jnp.where(jnp.arange(PROMPTS) == longest, PLEN, drawn_lengths).astype(jnp.int32)


def with_spikes(entries, key, source, target, shards_of, factor):
    owner, partner = [(jnp.arange(entries.shape[axis_at]) // (entries.shape[axis_at] // shards_of)).reshape([-1 if axis == axis_at else 1 for axis in range(entries.ndim)]) for axis_at in (source, target)]
    chosen = jax.random.permutation(key, shards_of)[partner]
    strong = (owner == chosen) | (owner == (partner + shards_of // 2) % shards_of)
    return jnp.where(strong, factor * entries, entries)


def steps_of(key, extent, cuts, least, top_value):
    level, own = 1.0, jax.random.fold_in(key, 6)
    for dim, parts in cuts:
        steps = jnp.exp(jax.random.uniform(jax.random.fold_in(own, dim), (parts,), jnp.float32, least / len(cuts), top_value / len(cuts)))
        level = level * jnp.repeat(steps, extent[dim] // parts).reshape([-1 if axis == dim else 1 for axis in range(len(extent))])
    return level


def routed_block(rng, own, number, rows, count, top, most, slope):
    ranking = jax.random.permutation(rng, count)
    crowded, common = portions_of(count, rows * top, most, slope, True), portions_of(count, rows * top, most, slope, False)
    places = jnp.arange(count)

    def named(tallies, offset_by):
        used = int((tallies > 0).sum())
        fixed = max(1, used // 4)
        shifted = fixed + (places - fixed + offset_by * (used - fixed)) % max(1, count - fixed)
        return jnp.zeros((count,), jnp.int32).at[ranking[jnp.where(places < fixed, places, shifted)]].set(jnp.asarray(tallies, jnp.int32))

    tallies = jnp.where(number % 4 == 0, named(crowded, number // 4), named(common, number - number // 4 - 1))
    mixed = jax.random.permutation(jax.random.fold_in(own, 3), count)
    donor, sink = mixed[0:count // 2 * 2:2], mixed[1:count // 2 * 2:2]
    room = jnp.minimum(tallies[donor] - 1, most - tallies[sink]) // 2
    room = jnp.where((donor == ranking[0]) | (sink == ranking[0]) | (tallies[sink] == 0), 0, jnp.maximum(room, 0))
    shifted = jax.random.randint(jax.random.fold_in(own, 4), (count // 2,), 0, 1 << 20) % (room + 1)
    tallies = tallies.at[donor].add(-shifted).at[sink].add(shifted)
    members = jnp.searchsorted(jnp.cumsum(tallies), jnp.arange(rows * top), side="right").astype(jnp.int32)
    grid = members.reshape(top, rows).T
    grid = grid[jax.random.permutation(jax.random.fold_in(own, 1), rows)]
    offset_by = jax.random.randint(jax.random.fold_in(own, 2), (rows, 1), 0, top)
    return jnp.take_along_axis(grid, (jnp.arange(top)[None, :] + offset_by) % top, axis=1)


def portions_of(count, total, bound, slope, full):
    weights = [(1 << 20) // math.isqrt(rank ** slope) + 1 for rank in range(1, count + 1)]
    largest = bound if full else min(bound, max(-(-total // count), total * weights[0] // sum(weights)))
    least = 1 if total - largest >= count - 1 else 0
    counts, rest = [largest] + [least] * (count - 1), total - largest - least * (count - 1)
    while rest > 0:
        candidates = [i for i in range(1, count) if counts[i] < largest] or [i for i in range(1, count) if counts[i] < bound]
        mass, left = sum([weights[i] for i in candidates]), rest
        for i in candidates:
            extra = min(bound - counts[i], max(1, left * weights[i] // mass), rest)
            counts[i] = counts[i] + extra
            rest = rest - extra
    return np.array(counts)


def gaussian(key, shape, scale, bound, cuts=(), kind=jnp.bfloat16):
    drawn = jax.random.normal(key, shape, jnp.float32) * scale
    if len(cuts) > 0:
        drawn = steps_of(key, shape, cuts, -0.22, 0.18) * drawn
    return jnp.clip(drawn, min=-bound, max=bound).astype(kind)


def gaussian_with(own_key, extent, scale, most, pieces, heavy, held_as=jnp.bfloat16):
    array = scale * jax.random.normal(own_key, extent, jnp.float32)
    if pieces:
        array = array * steps_of(own_key, extent, pieces, -0.22, 0.18)
    return jnp.clip(with_spikes(array, jax.random.fold_in(own_key, 3), *heavy), -most, most).astype(held_as)


def setup_inputs(seed: int = 0, part: int = 0) -> dict:
    seeds = jax.random.split(jax.random.key(seed), 13)
    part_keys = jax.random.split(jax.random.fold_in(seeds[12], part), 13)
    image_rows = gaussian(part_keys[0], (IMAGE, D), 1.0, 6.0, ((0, 16),))
    text_hidden = gaussian_with(part_keys[1], (TEXT, LLAMA), 1.0, 6.0, ((1, 16),), (1, 0, 16, 2.0))
    caption_weight = gaussian(seeds[2], (LLAMA, D), LLAMA ** -0.5, 0.09375, ((0, 16),))
    mod_scale = jnp.clip(1.0 + 0.1 * jax.random.normal(seeds[3], (D,), jnp.float32), 0.5, 1.5)
    mod_shift = gaussian(seeds[4], (D,), 0.5, 3.0, (), jnp.float32)
    router_weight = gaussian(seeds[5], (D, EXPERTS), D ** -0.5, 0.125, (), jnp.float32)
    image_experts_keys = jax.random.split(jax.random.fold_in(part_keys[6], 1), IMAGE // IMG_DEV)
    image_experts_turns = jax.random.permutation(jax.random.fold_in(part_keys[6], 3), IMAGE // IMG_DEV)
    image_experts = jax.vmap(lambda own, number: routed_block(jax.random.fold_in(part_keys[6], 2), own, number, IMG_DEV, EXPERTS, TOP, CAP_IMG, 2))(image_experts_keys, image_experts_turns).reshape((IMAGE, TOP))
    caption_experts_keys = jax.random.split(jax.random.fold_in(part_keys[7], 1), TEXT // TXT_DEV)
    caption_experts_turns = jax.random.permutation(jax.random.fold_in(part_keys[7], 3), TEXT // TXT_DEV)
    caption_experts = jax.vmap(lambda own, number: routed_block(jax.random.fold_in(part_keys[7], 2), own, number, TXT_DEV, EXPERTS, TOP, TXT_CAP, 1))(caption_experts_keys, caption_experts_turns).reshape((TEXT, TOP))
    prompt_lengths = draw_prompt_lengths(jax.random.fold_in(jax.random.fold_in(seeds[12], part), 71), part)
    w_gate = gaussian(seeds[9], (D, EXPERTS * FF), D ** -0.5, 0.125, ((1, 16),))
    w_up = gaussian(seeds[10], (D, EXPERTS * FF), D ** -0.5, 0.125, ((1, 16),))
    w_down = gaussian(seeds[11], (EXPERTS * FF, D), FF ** -0.5, 0.078125, ((0, 16),))
    return dict(image_rows=image_rows, text_hidden=text_hidden, caption_weight=caption_weight, mod_scale=mod_scale, mod_shift=mod_shift, router_weight=router_weight, image_experts=image_experts, caption_experts=caption_experts, prompt_lengths=prompt_lengths, w_gate=w_gate, w_up=w_up, w_down=w_down)


def modulate(inputs, mod_scale, mod_shift):
    values = inputs.astype(jnp.float32)
    center = values - lax.optimization_barrier(jnp.mean(values, axis=1, keepdims=True))
    spread = lax.optimization_barrier(jnp.mean(center * center, axis=1, keepdims=True))
    return (center * lax.rsqrt(spread + 1e-06) * mod_scale + mod_shift).astype(jnp.bfloat16)

def route_weights(normed, router_weight, chosen):
    logits = jnp.dot(normed.astype(jnp.float32), router_weight, precision=lax.Precision.HIGHEST)
    expert_ids = jnp.arange(router_weight.shape[1], dtype=jnp.int32)
    first_logit = lax.optimization_barrier(jnp.sum(jnp.where(chosen[:, 0:1] == expert_ids[None, :], logits, 0.0), axis=1))
    second_logit = lax.optimization_barrier(jnp.sum(jnp.where(chosen[:, 1:2] == expert_ids[None, :], logits, 0.0), axis=1))
    return (jax.nn.sigmoid(first_logit - second_logit), jax.nn.sigmoid(second_logit - first_logit))

def mixture(inputs, chosen, active_rows, mod_scale, mod_shift, router_weight, w_gate, w_up, w_down):
    normed = modulate(inputs, mod_scale, mod_shift)
    weight_first, weight_second = route_weights(normed, router_weight, chosen)
    sharing = N_DEV // EXPERTS
    units_dev = FF // sharing
    count_rows = inputs.shape[0]
    combined = jnp.zeros((count_rows, D), jnp.float32)
    for expert in range(EXPERTS):
        gate_proj = jnp.dot(normed, w_gate[:, expert * FF:(expert + 1) * FF], preferred_element_type=jnp.float32)
        up_proj = jnp.dot(normed, w_up[:, expert * FF:(expert + 1) * FF], preferred_element_type=jnp.float32)
        hidden = (jax.nn.silu(gate_proj) * up_proj).astype(jnp.bfloat16)
        down_rows = w_down[expert * FF:(expert + 1) * FF].reshape(sharing, units_dev, D)
        partial_value = jnp.einsum('rgh,ghd->rgd', hidden.reshape(count_rows, sharing, units_dev).astype(jnp.float32), down_rows.astype(jnp.float32), precision=lax.Precision.HIGHEST).astype(jnp.bfloat16)
        expert_out = lax.optimization_barrier(jnp.sum(partial_value.astype(jnp.float32), axis=1))
        mixing = (weight_first * (chosen[:, 0] == expert) + weight_second * (chosen[:, 1] == expert)) * active_rows
        combined = combined + mixing[:, None] * expert_out
    return combined.astype(jnp.bfloat16)

def reference(image_rows, text_hidden, caption_weight, mod_scale, mod_shift, router_weight, image_experts, caption_experts, prompt_lengths, w_gate, w_up, w_down):
    caption = jnp.dot(text_hidden, caption_weight, preferred_element_type=jnp.float32).astype(jnp.bfloat16)
    position = jnp.arange(TEXT, dtype=jnp.int32)
    active_text = (position % PLEN < prompt_lengths[position // PLEN]).astype(jnp.float32)
    active_image = jnp.ones((image_rows.shape[0],), jnp.float32)
    image_out = mixture(image_rows, image_experts, active_image, mod_scale, mod_shift, router_weight, w_gate, w_up, w_down)
    caption_out = mixture(caption, caption_experts, active_text, mod_scale, mod_shift, router_weight, w_gate, w_up, w_down)
    return (image_out, caption_out)
```

```python
import jax
import jax.numpy as jnp
from jax import lax
from jax.sharding import PartitionSpec as P

PLEN = 128


def modulate(inputs, mod_scale, mod_shift):
    values = inputs.astype(jnp.float32)
    center = values - jnp.mean(values, axis=1, keepdims=True)
    spread = jnp.mean(center * center, axis=1, keepdims=True)
    return (center * lax.rsqrt(spread + 1e-06) * mod_scale + mod_shift).astype(jnp.bfloat16)


def route_weights(normed, router_weight, chosen):
    logits = jnp.dot(normed.astype(jnp.float32), router_weight, precision=lax.Precision.HIGHEST)
    expert_ids = jnp.arange(router_weight.shape[1], dtype=jnp.int32)
    first_logit = jnp.sum(jnp.where(chosen[:, 0:1] == expert_ids[None, :], logits, 0.0), axis=1)
    second_logit = jnp.sum(jnp.where(chosen[:, 1:2] == expert_ids[None, :], logits, 0.0), axis=1)
    return (jax.nn.sigmoid(first_logit - second_logit), jax.nn.sigmoid(second_logit - first_logit))


class Grid:
    def __init__(self, devices, experts):
        self.experts = experts
        self.pairs = devices // experts // 2
        index = lax.axis_index("dev")
        self.index = index
        self.expert = index // (self.pairs * 2)
        self.pair = (index // 2) % self.pairs
        self.core = index % 2

    def send(self, value, axis, step):
        moves = []
        for expert in range(self.experts):
            for pair in range(self.pairs):
                for core in range(2):
                    to = [expert, pair, core]
                    to[axis] = (to[axis] + step) % (self.experts, self.pairs, 2)[axis]
                    moves.append(
                        (
                            (expert * self.pairs + pair) * 2 + core,
                            (to[0] * self.pairs + to[1]) * 2 + to[2],
                        )
                    )
        return lax.ppermute(value, "dev", moves)


def slots(normed, chosen, active_rows, router_weight, capacity, grid):
    weight_first, weight_second = route_weights(normed, router_weight, chosen)
    experts = grid.experts
    expert_ids = (grid.expert + jnp.arange(experts, dtype=jnp.int32)) % experts
    match_first = chosen[:, 0:1] == expert_ids[None, :]
    match_second = chosen[:, 1:2] == expert_ids[None, :]
    routed = (match_first | match_second).astype(jnp.int32) * active_rows[:, None]
    ordinal = jnp.cumsum(routed, axis=0) - routed
    slot_ids = jnp.arange(capacity, dtype=jnp.int32)
    placed = (ordinal[:, :, None] == slot_ids[None, None, :]) & (routed[:, :, None] > 0)
    mixing = weight_first[:, None] * match_first + weight_second[:, None] * match_second
    scatter_table = jnp.transpose(placed, (1, 2, 0)).astype(jnp.bfloat16)
    gather_table = jnp.transpose(placed.astype(jnp.float32) * mixing[:, :, None], (1, 2, 0))
    buckets = [
        jnp.dot(scatter_table[k], normed, preferred_element_type=jnp.float32).astype(jnp.bfloat16)
        for k in range(experts)
    ]
    return (buckets, gather_table)


def dispatch(buckets, grid):
    held = [buckets[0]] + [grid.send(buckets[k], 0, k) for k in range(1, grid.experts)]
    block = jnp.concatenate(held, axis=0)
    block = jnp.concatenate(
        [block] + [grid.send(block, 1, k) for k in range(1, grid.pairs)], axis=0
    )
    return (block, grid.send(block, 2, 1))


def expert_rows(own, other, w_gate, w_up, w_down):
    rows = jnp.concatenate([own, other], axis=0)
    gate_proj = jnp.dot(rows, w_gate, preferred_element_type=jnp.float32)
    up_proj = jnp.dot(rows, w_up, preferred_element_type=jnp.float32)
    hidden = (jax.nn.silu(gate_proj) * up_proj).astype(jnp.bfloat16)
    out = jnp.dot(hidden, w_down, preferred_element_type=jnp.float32).astype(jnp.bfloat16)
    return (out[: own.shape[0]], out[own.shape[0] :])


def give_back(own, other, grid):
    total = own.astype(jnp.float32) + grid.send(other, 2, 1).astype(jnp.float32)
    total = total.astype(jnp.bfloat16)
    rows = total.shape[0] // grid.pairs
    parts = [total[k * rows : (k + 1) * rows] for k in range(grid.pairs)]
    total = parts[0].astype(jnp.float32)
    for k in range(1, grid.pairs):
        total = total + grid.send(parts[k], 1, -k).astype(jnp.float32)
    total = total.astype(jnp.bfloat16)
    rows = rows // grid.experts
    parts = [total[k * rows : (k + 1) * rows] for k in range(grid.experts)]
    return jnp.stack(
        [parts[0]] + [grid.send(parts[k], 0, -k) for k in range(1, grid.experts)], axis=0
    )


def combine(gather_table, expert_out):
    return jnp.einsum(
        "ecr,ecd->rd",
        gather_table,
        expert_out.astype(jnp.float32),
        precision=lax.Precision.HIGHEST,
    ).astype(jnp.bfloat16)


def project(text_hidden, caption_weight, grid):
    rows = text_hidden.shape[0] // (grid.experts * grid.pairs * 2)
    text = text_hidden.reshape(grid.experts, grid.pairs, 2, rows, text_hidden.shape[1])
    text = jnp.roll(text, -grid.expert, axis=0)
    text = jnp.roll(text, -grid.pair, axis=1)
    text = jnp.roll(text, -grid.core, axis=2)
    text = jnp.transpose(text, (2, 1, 0, 3, 4)).reshape(2, -1, text_hidden.shape[1])
    other = jnp.dot(text[1], caption_weight, preferred_element_type=jnp.float32)
    own = jnp.dot(text[0], caption_weight, preferred_element_type=jnp.float32)
    total = own + grid.send(other.astype(jnp.bfloat16), 2, 1).astype(jnp.float32)
    rows_pair = rows * grid.experts
    parts = [total[k * rows_pair : (k + 1) * rows_pair] for k in range(grid.pairs)]
    total = parts[0]
    for k in range(1, grid.pairs):
        total = total + grid.send(parts[k].astype(jnp.bfloat16), 1, k).astype(jnp.float32)
    parts = [total[k * rows : (k + 1) * rows] for k in range(grid.experts)]
    total = parts[0]
    for k in range(1, grid.experts):
        total = total + grid.send(parts[k].astype(jnp.bfloat16), 0, k).astype(jnp.float32)
    return total.astype(jnp.bfloat16)


def local(
    image_rows,
    text_hidden,
    caption_weight,
    mod_scale,
    mod_shift,
    router_weight,
    image_experts,
    caption_experts,
    prompt_lengths,
    w_gate,
    w_up,
    w_down,
):
    devices = lax.axis_size("dev")
    experts = router_weight.shape[1]
    grid = Grid(devices, experts)
    caption_rows = text_hidden.shape[0] // devices
    caption_cap = caption_rows // 2 + 1
    image_cap = image_rows.shape[0] * 3 // 4

    caption = project(text_hidden, caption_weight, grid)

    image_normed = modulate(image_rows, mod_scale, mod_shift)
    image_active = jnp.ones((image_rows.shape[0],), jnp.int32)
    image_buckets, image_table = slots(
        image_normed, image_experts, image_active, router_weight, image_cap, grid
    )
    image_own, image_other = dispatch(image_buckets, grid)
    image_back = give_back(
        *expert_rows(image_own, image_other, w_gate, w_up, w_down), grid
    )
    image_out = combine(image_table, image_back)

    position = grid.index * caption_rows + jnp.arange(caption_rows, dtype=jnp.int32)
    prompt_ids = position // PLEN
    prompt_range = jnp.arange(prompt_lengths.shape[0], dtype=jnp.int32)
    lengths = jnp.sum(
        jnp.where(prompt_ids[:, None] == prompt_range[None, :], prompt_lengths[None, :], 0), axis=1
    )
    caption_active = (position % PLEN < lengths).astype(jnp.int32)
    caption_normed = modulate(caption, mod_scale, mod_shift)
    caption_buckets, caption_table = slots(
        caption_normed, caption_experts, caption_active, router_weight, caption_cap, grid
    )
    caption_own, caption_other = dispatch(caption_buckets, grid)
    caption_back = give_back(
        *expert_rows(caption_own, caption_other, w_gate, w_up, w_down), grid
    )
    caption_out = combine(caption_table, caption_back)
    return (image_out, caption_out)


def solution(mesh):
    in_specs = (
        P(("groups", "dev"), None),
        P("groups", "dev"),
        P("dev", None),
        P(),
        P(),
        P(),
        P(("groups", "dev"), None),
        P(("groups", "dev"), None),
        P("groups"),
        P(None, "dev"),
        P(None, "dev"),
        P("dev", None),
    )
    out_specs = (P(("groups", "dev"), None), P(("groups", "dev"), None))
    return jax.shard_map(local, mesh=mesh, in_specs=in_specs, out_specs=out_specs, check_vma=False)
```

```python
import functools

import jax
import jax.numpy as jnp
from jax import lax
from jax.experimental import pallas as pl
from jax.experimental.pallas import tpu as pltpu
from jax.sharding import PartitionSpec as P

PLEN = 128
VMEM = pl.BlockSpec(memory_space=pltpu.VMEM)
HIDDEN_STEP = 512
FEATURE_STEP = 512


class Grid:
    def __init__(self, devices, experts):
        self.experts = experts
        self.pairs = devices // experts // 2
        index = lax.axis_index("dev")
        self.index = index
        self.expert = index // (self.pairs * 2)
        self.pair = (index // 2) % self.pairs
        self.core = index % 2

    def send(self, value, axis, step):
        moves = []
        for expert in range(self.experts):
            for pair in range(self.pairs):
                for core in range(2):
                    to = [expert, pair, core]
                    to[axis] = (to[axis] + step) % (self.experts, self.pairs, 2)[axis]
                    moves.append(
                        (
                            (expert * self.pairs + pair) * 2 + core,
                            (to[0] * self.pairs + to[1]) * 2 + to[2],
                        )
                    )
        return lax.ppermute(value, "dev", moves)


class Packing:
    def __init__(self, cap, features):
        best = None
        for chunks in range(1, features // 128 + 1):
            if features % (128 * chunks):
                continue
            rows = -(-cap * chunks // 16) * 16
            cost = rows * (features // chunks)
            if best is None or cost < best[0]:
                best = (cost, chunks, rows)
        _, self.chunks, self.rows = best
        self.cap = cap
        self.width = features // self.chunks


def route_weights(normed, router_weight, chosen):
    logits = jnp.dot(normed.astype(jnp.float32), router_weight, precision=lax.Precision.HIGHEST)
    expert_ids = jnp.arange(router_weight.shape[1], dtype=jnp.int32)
    first_logit = jnp.sum(jnp.where(chosen[:, 0:1] == expert_ids[None, :], logits, 0.0), axis=1)
    second_logit = jnp.sum(jnp.where(chosen[:, 1:2] == expert_ids[None, :], logits, 0.0), axis=1)
    return (jax.nn.sigmoid(first_logit - second_logit), jax.nn.sigmoid(second_logit - first_logit))


def tables(chosen, active, packing, grid):
    experts, rows = grid.experts, chosen.shape[0]
    relative = (chosen - grid.expert) % experts
    expert_ids = jnp.arange(experts, dtype=jnp.int32)
    routed = jnp.any(relative[:, :, None] == expert_ids, axis=1) & active[:, None]
    counts = routed.astype(jnp.int32)
    slot = jnp.cumsum(counts, axis=0) - counts
    offset = jnp.arange(packing.chunks, dtype=jnp.int32) * packing.cap
    place = jnp.arange(packing.rows, dtype=jnp.int32)
    into = (place[None, :, None, None] == offset[None, None, :, None] + slot.T[:, None, None, :]) & (
        routed.T[:, None, None, :]
    )
    into = into.reshape(experts * packing.rows, packing.chunks * rows).astype(jnp.bfloat16)
    own_slot = jnp.sum(
        jnp.where(relative[:, :, None] == expert_ids, slot[:, None, :], 0), axis=2
    )
    spot = (relative * packing.rows + own_slot).T
    back = (
        spot[:, None, :, None] + offset[None, :, None, None]
        == jnp.arange(experts * packing.rows, dtype=jnp.int32)
    ) & active[None, None, :, None]
    back = back.reshape(2 * packing.chunks * rows, experts * packing.rows).astype(jnp.bfloat16)
    return (into, back)


def modulate_kernel(packing, experts, count, into_ref, scale_ref, shift_ref, *refs):
    value_refs, out_refs = refs[:count], refs[count:]
    values = value_refs[0][...].astype(jnp.float32)
    for ref in value_refs[1:]:
        values = values + ref[...].astype(jnp.float32)
    values = values.astype(jnp.bfloat16).astype(jnp.float32)
    center = values - jnp.mean(values, axis=1, keepdims=True)
    spread = jnp.mean(center * center, axis=1, keepdims=True)
    normed = center * lax.rsqrt(spread + 1e-06) * scale_ref[...] + shift_ref[...]
    normed = normed.astype(jnp.bfloat16)
    out_refs[0][...] = normed
    width = packing.width
    stacked = jnp.concatenate(
        [normed[:, j * width : (j + 1) * width] for j in range(packing.chunks)], axis=0
    )
    packed = jnp.dot(into_ref[...], stacked, preferred_element_type=jnp.float32)
    for k in range(experts):
        out_refs[1 + k][...] = packed[k * packing.rows : (k + 1) * packing.rows].astype(
            jnp.bfloat16
        )


def modulate(parts, into, mod_scale, mod_shift, packing, experts):
    rows, features = parts[0].shape
    outs = [jax.ShapeDtypeStruct((rows, features), jnp.bfloat16)]
    outs += [jax.ShapeDtypeStruct((packing.rows, packing.width), jnp.bfloat16)] * experts
    results = pl.pallas_call(
        functools.partial(modulate_kernel, packing, experts, len(parts)),
        out_shape=outs,
        in_specs=[VMEM] * (3 + len(parts)),
        out_specs=[VMEM] * len(outs),
        compiler_params=pltpu.CompilerParams(vmem_limit_bytes=8 << 20),
        name="modulate",
    )(into, mod_scale.reshape(1, -1), mod_shift.reshape(1, -1), *parts)
    return (results[0], list(results[1:]))


def cuts(total, step):
    return [(start, min(start + step, total)) for start in range(0, total, step)]


def expert_kernel(
    packing,
    own_ref,
    other_ref,
    gate_hbm,
    up_hbm,
    down_hbm,
    own_out,
    other_out,
    gate_ref,
    up_ref,
    down_ref,
    rows_ref,
    sems,
):
    features, units = gate_hbm.shape
    feature_cuts, unit_cuts = cuts(features, FEATURE_STEP), cuts(units, HIDDEN_STEP)
    copies = []
    for lo, hi in feature_cuts:
        copies.append((gate_hbm.at[lo:hi], gate_ref.at[lo:hi]))
        copies.append((up_hbm.at[lo:hi], up_ref.at[lo:hi]))
    for lo, hi in unit_cuts:
        copies.append((down_hbm.at[lo:hi], down_ref.at[lo:hi]))
    copies = [
        pltpu.make_async_copy(source, target, sems.at[i])
        for i, (source, target) in enumerate(copies)
    ]
    for copy in copies:
        copy.start()

    cap, chunks, width = packing.cap, packing.chunks, packing.width
    blocks = own_ref.shape[0] // packing.rows * 2
    group = 16
    row_at = lax.broadcasted_iota(jnp.int32, (group * cap, group * packing.rows), 0)
    place = lax.broadcasted_iota(jnp.int32, (group * cap, group * packing.rows), 1)
    source_row = (row_at // cap) * packing.rows + row_at % cap
    packed = jnp.concatenate([own_ref[...], other_ref[...]], axis=0)
    for g in range(blocks // group):
        part = packed[g * group * packing.rows : (g + 1) * group * packing.rows]
        for j in range(chunks):
            pick = jnp.where(place == source_row + j * cap, 1.0, 0.0).astype(jnp.bfloat16)
            rows_ref[g * group * cap : (g + 1) * group * cap, j * width : (j + 1) * width] = (
                jnp.dot(pick, part, preferred_element_type=jnp.float32).astype(jnp.bfloat16)
            )

    gate, up = None, None
    for i, (lo, hi) in enumerate(feature_cuts):
        rows = rows_ref[:, lo:hi]
        copies[2 * i].wait()
        term = jnp.dot(rows, gate_ref[lo:hi, :], preferred_element_type=jnp.float32)
        gate = term if gate is None else gate + term
        copies[2 * i + 1].wait()
        term = jnp.dot(rows, up_ref[lo:hi, :], preferred_element_type=jnp.float32)
        up = term if up is None else up + term
    hidden = (gate * jax.nn.sigmoid(gate) * up).astype(jnp.bfloat16)
    total = None
    for i, (lo, hi) in enumerate(unit_cuts):
        copies[2 * len(feature_cuts) + i].wait()
        term = jnp.dot(hidden[:, lo:hi], down_ref[lo:hi, :], preferred_element_type=jnp.float32)
        total = term if total is None else total + term
    total = total.astype(jnp.bfloat16)

    place = lax.broadcasted_iota(jnp.int32, (group * packing.rows, group * cap), 0)
    row_at = lax.broadcasted_iota(jnp.int32, (group * packing.rows, group * cap), 1)
    target = (row_at // cap) * packing.rows + row_at % cap
    results = []
    for g in range(blocks // group):
        packed = None
        for j in range(chunks):
            put = jnp.where(place == target + j * cap, 1.0, 0.0).astype(jnp.bfloat16)
            term = jnp.dot(
                put,
                total[g * group * cap : (g + 1) * group * cap, j * width : (j + 1) * width],
                preferred_element_type=jnp.float32,
            )
            packed = term if packed is None else packed + term
        results.append(packed.astype(jnp.bfloat16))
    packed = results[0] if len(results) == 1 else jnp.concatenate(results, axis=0)
    own_out[...] = packed[: own_out.shape[0]]
    other_out[...] = packed[own_out.shape[0] :]


def expert_rows(own, other, w_gate, w_up, w_down, packing):
    features, units = w_gate.shape
    blocks = own.shape[0] // packing.rows * 2
    rows = blocks * packing.cap
    copies = 2 * len(cuts(features, FEATURE_STEP)) + len(cuts(units, HIDDEN_STEP))
    return pl.pallas_call(
        functools.partial(expert_kernel, packing),
        out_shape=[jax.ShapeDtypeStruct(own.shape, jnp.bfloat16)] * 2,
        in_specs=[VMEM, VMEM] + [pl.BlockSpec(memory_space=pl.ANY)] * 3,
        out_specs=[VMEM, VMEM],
        scratch_shapes=[
            pltpu.VMEM((features, units), jnp.bfloat16),
            pltpu.VMEM((features, units), jnp.bfloat16),
            pltpu.VMEM((units, features), jnp.bfloat16),
            pltpu.VMEM((rows, features), jnp.bfloat16),
            pltpu.SemaphoreType.DMA((copies,)),
        ],
        compiler_params=pltpu.CompilerParams(vmem_limit_bytes=48 << 20),
        cost_estimate=pl.CostEstimate(
            flops=6 * rows * features * units,
            bytes_accessed=6 * features * units,
            transcendentals=rows * units,
        ),
        name="experts",
    )(own, other, w_gate, w_up, w_down)


def combine_kernel(packing, back_ref, first_ref, second_ref, *refs):
    block_refs, out_ref = refs[:-1], refs[-1]
    rows = out_ref.shape[0]
    blocks = jnp.concatenate([ref[...] for ref in block_refs], axis=0)
    picked = jnp.dot(back_ref[...], blocks, preferred_element_type=jnp.float32)
    half = packing.chunks * rows
    for j in range(packing.chunks):
        first = picked[j * rows : (j + 1) * rows]
        second = picked[half + j * rows : half + (j + 1) * rows]
        out_ref[:, j * packing.width : (j + 1) * packing.width] = (
            first_ref[...] * first + second_ref[...] * second
        ).astype(jnp.bfloat16)


def combine(back, weights, blocks, packing, rows, features):
    first, second = weights
    return pl.pallas_call(
        functools.partial(combine_kernel, packing),
        out_shape=jax.ShapeDtypeStruct((rows, features), jnp.bfloat16),
        in_specs=[VMEM] * (3 + len(blocks)),
        out_specs=VMEM,
        compiler_params=pltpu.CompilerParams(vmem_limit_bytes=8 << 20),
        name="combine",
    )(back, first[:, None], second[:, None], *blocks)


def dispatch(blocks, grid):
    held = [blocks[0]] + [grid.send(blocks[k], 0, k) for k in range(1, grid.experts)]
    block = jnp.concatenate(held, axis=0)
    block = jnp.concatenate(
        [block] + [grid.send(block, 1, k) for k in range(1, grid.pairs)], axis=0
    )
    return (block, grid.send(block, 2, 1))


def give_back(own, other, grid):
    total = own.astype(jnp.float32) + grid.send(other, 2, 1).astype(jnp.float32)
    rows = total.shape[0] // grid.pairs
    parts = [total[k * rows : (k + 1) * rows] for k in range(grid.pairs)]
    total = parts[0]
    for k in range(1, grid.pairs):
        total = total + grid.send(parts[k].astype(jnp.bfloat16), 1, -k).astype(jnp.float32)
    total = total.astype(jnp.bfloat16)
    rows = rows // grid.experts
    parts = [total[k * rows : (k + 1) * rows] for k in range(grid.experts)]
    return [parts[0]] + [grid.send(parts[k], 0, -k) for k in range(1, grid.experts)]


def project(text_hidden, caption_weight, grid):
    rows = text_hidden.shape[0] // (grid.experts * grid.pairs * 2)
    text = text_hidden.reshape(grid.experts, grid.pairs, 2, rows, text_hidden.shape[1])
    text = jnp.roll(text, -grid.expert, axis=0)
    text = jnp.roll(text, -grid.pair, axis=1)
    text = jnp.roll(text, -grid.core, axis=2)
    text = jnp.transpose(text, (2, 1, 0, 3, 4)).reshape(2, -1, text_hidden.shape[1])
    other = jnp.dot(text[1], caption_weight, preferred_element_type=jnp.float32)
    own = jnp.dot(text[0], caption_weight, preferred_element_type=jnp.float32)
    total = own + grid.send(other.astype(jnp.bfloat16), 2, 1).astype(jnp.float32)
    rows_pair = rows * grid.experts
    parts = [total[k * rows_pair : (k + 1) * rows_pair] for k in range(grid.pairs)]
    total = parts[0]
    for k in range(1, grid.pairs):
        total = total + grid.send(parts[k].astype(jnp.bfloat16), 1, k).astype(jnp.float32)
    parts = [total[k * rows : (k + 1) * rows] for k in range(grid.experts)]
    return [parts[0]] + [
        grid.send(parts[k].astype(jnp.bfloat16), 0, k) for k in range(1, grid.experts)
    ]


def local(
    image_rows,
    text_hidden,
    caption_weight,
    mod_scale,
    mod_shift,
    router_weight,
    image_experts,
    caption_experts,
    prompt_lengths,
    w_gate,
    w_up,
    w_down,
):
    devices = lax.axis_size("dev")
    features, experts = router_weight.shape
    grid = Grid(devices, experts)
    caption_rows = text_hidden.shape[0] // devices
    caption_packing = Packing(caption_rows // 2 + 1, features)
    image_packing = Packing(image_rows.shape[0] * 3 // 4, features)
    position = grid.index * caption_rows + jnp.arange(caption_rows, dtype=jnp.int32)
    prompt_ids = position // PLEN
    prompt_range = jnp.arange(prompt_lengths.shape[0], dtype=jnp.int32)
    lengths = jnp.sum(
        jnp.where(prompt_ids[:, None] == prompt_range[None, :], prompt_lengths[None, :], 0), axis=1
    )
    caption_active = position % PLEN < lengths
    image_active = jnp.ones((image_rows.shape[0],), jnp.bool_)

    def block(parts, chosen, active, packing):
        into, back = tables(chosen, active, packing, grid)
        normed, blocks = modulate(parts, into, mod_scale, mod_shift, packing, experts)
        own, other = dispatch(blocks, grid)
        own, other = expert_rows(own, other, w_gate, w_up, w_down, packing)
        weights = route_weights(normed, router_weight, chosen)
        blocks = give_back(own, other, grid)
        return combine(back, weights, blocks, packing, chosen.shape[0], features)

    caption = project(text_hidden, caption_weight, grid)
    image_out = block([image_rows], image_experts, image_active, image_packing)
    caption_out = block(caption, caption_experts, caption_active, caption_packing)
    return (image_out, caption_out)


def solution(mesh):
    in_specs = (
        P(("groups", "dev"), None),
        P("groups", "dev"),
        P("dev", None),
        P(),
        P(),
        P(),
        P(("groups", "dev"), None),
        P(("groups", "dev"), None),
        P("groups"),
        P(None, "dev"),
        P(None, "dev"),
        P("dev", None),
    )
    out_specs = (P(("groups", "dev"), None), P(("groups", "dev"), None))
    return jax.shard_map(local, mesh=mesh, in_specs=in_specs, out_specs=out_specs, check_vma=False)
```

```python
import functools

import jax
import jax.numpy as jnp
from jax import lax
from jax.experimental import pallas as pl
from jax.experimental.pallas import tpu as pltpu
from jax.sharding import PartitionSpec as P

PLEN = 128
VMEM = pl.BlockSpec(memory_space=pltpu.VMEM)
SMEM = pl.BlockSpec(memory_space=pltpu.SMEM)
ANY = pl.BlockSpec(memory_space=pl.ANY)
UNIT_STEP = 256


class Grid:
    def __init__(self, devices, experts):
        self.experts = experts
        self.pairs = devices // experts // 2
        index = lax.axis_index("dev")
        self.index = index
        self.expert = index // (self.pairs * 2)
        self.pair = (index // 2) % self.pairs
        self.core = index % 2

    def send(self, value, axis, step):
        moves = []
        for expert in range(self.experts):
            for pair in range(self.pairs):
                for core in range(2):
                    to = [expert, pair, core]
                    to[axis] = (to[axis] + step) % (self.experts, self.pairs, 2)[axis]
                    moves.append(
                        (
                            (expert * self.pairs + pair) * 2 + core,
                            (to[0] * self.pairs + to[1]) * 2 + to[2],
                        )
                    )
        return lax.ppermute(value, "dev", moves)


class Packing:
    def __init__(self, cap, features):
        best = None
        for chunks in range(1, features // 128 + 1):
            if features % (128 * chunks):
                continue
            rows = -(-cap * chunks // 16) * 16
            cost = rows * (features // chunks)
            if best is None or cost < best[0]:
                best = (cost, chunks, rows)
        _, self.chunks, self.rows = best
        self.cap = cap
        self.width = features // self.chunks


def inner_index(experts):
    devices = lax.axis_size("dev")
    index = lax.axis_index("dev")
    return index, index // (devices // experts)


def live(position, lengths_ref):
    prompt = position // PLEN
    length = jnp.zeros_like(position)
    for p in range(lengths_ref.shape[0]):
        length = jnp.where(prompt == p, lengths_ref[p], length)
    return position % PLEN < length


def modulate_kernel(packing, experts, count, prompts, *refs):
    lengths_ref, chosen_ref, scale_ref, shift_ref = refs[:4]
    value_refs, out_refs = refs[4 : 4 + count], refs[len(refs) - 1 - experts :]
    index, own_expert = inner_index(experts)
    rows = value_refs[0].shape[0]
    relative = lax.rem(chosen_ref[...] + (experts - own_expert), experts)
    expert_at = lax.broadcasted_iota(jnp.int32, (experts, rows), 0)
    routed = (relative[0:1] == expert_at) | (relative[1:2] == expert_at)
    if prompts:
        position = index * rows + lax.broadcasted_iota(jnp.int32, (experts, rows), 1)
        routed = routed & live(position, lengths_ref)
    before = lax.broadcasted_iota(jnp.int32, (rows, rows), 0) < lax.broadcasted_iota(
        jnp.int32, (rows, rows), 1
    )
    slot = jnp.dot(
        routed.astype(jnp.float32), before.astype(jnp.float32), preferred_element_type=jnp.float32
    )
    slot = jnp.where(routed, slot, -1024.0)

    values = value_refs[0][...].astype(jnp.float32)
    for ref in value_refs[1:]:
        values = values + ref[...].astype(jnp.float32)
    values = values.astype(jnp.bfloat16).astype(jnp.float32)
    center = values - jnp.mean(values, axis=1, keepdims=True)
    spread = jnp.mean(center * center, axis=1, keepdims=True)
    normed = center * lax.rsqrt(spread + 1e-06) * scale_ref[...] + shift_ref[...]
    normed = normed.astype(jnp.bfloat16)
    out_refs[0][...] = normed

    place = lax.broadcasted_iota(jnp.int32, (packing.rows, rows), 0).astype(jnp.float32)
    packed = None
    for j in range(packing.chunks):
        into = jnp.concatenate(
            [
                jnp.where(place - float(j * packing.cap) == slot[k : k + 1], 1.0, 0.0)
                for k in range(experts)
            ],
            axis=0,
        ).astype(jnp.bfloat16)
        term = jnp.dot(
            into,
            normed[:, j * packing.width : (j + 1) * packing.width],
            preferred_element_type=jnp.float32,
        )
        packed = term if packed is None else packed + term
    for k in range(experts):
        out_refs[1 + k][...] = packed[k * packing.rows : (k + 1) * packing.rows].astype(
            jnp.bfloat16
        )


def modulate(parts, chosen, lengths, mod_scale, mod_shift, packing, experts, prompts, after):
    rows, features = parts[0].shape
    outs = [jax.ShapeDtypeStruct((rows, features), jnp.bfloat16)]
    outs += [jax.ShapeDtypeStruct((packing.rows, packing.width), jnp.bfloat16)] * experts
    results = pl.pallas_call(
        functools.partial(modulate_kernel, packing, experts, len(parts), prompts),
        out_shape=outs,
        in_specs=[SMEM] + [VMEM] * (3 + len(parts)) + [ANY] * len(after),
        out_specs=[VMEM] * len(outs),
        compiler_params=pltpu.CompilerParams(vmem_limit_bytes=8 << 20),
        name="modulate",
    )(lengths, chosen.T, mod_scale.reshape(1, -1), mod_shift.reshape(1, -1), *parts, *after)
    return (results[0], list(results[1:]))


def route_kernel(packing, experts, prompts, lengths_ref, chosen_ref, normed_ref, router_ref, spot_ref, weight_ref):
    index, own_expert = inner_index(experts)
    rows = normed_ref.shape[0]
    chosen = chosen_ref[...]
    relative = lax.rem(chosen + (experts - own_expert), experts)
    expert_at = lax.broadcasted_iota(jnp.int32, (rows, experts), 1)
    routed = (relative[:, 0:1] == expert_at) | (relative[:, 1:2] == expert_at)
    active = None
    if prompts:
        position = index * rows + lax.broadcasted_iota(jnp.int32, (rows, experts), 0)
        active = live(position, lengths_ref)
        routed = routed & active
    before = lax.broadcasted_iota(jnp.int32, (rows, rows), 1) < lax.broadcasted_iota(
        jnp.int32, (rows, rows), 0
    )
    slot = jnp.dot(
        before.astype(jnp.float32), routed.astype(jnp.float32), preferred_element_type=jnp.float32
    )
    normed = normed_ref[...].astype(jnp.float32)
    logits = [
        jnp.sum(normed * router_ref[k : k + 1, :], axis=1, keepdims=True) for k in range(experts)
    ]
    picked = []
    for t in range(2):
        mine = relative[:, t : t + 1] == expert_at
        own_slot = jnp.sum(jnp.where(mine, slot, 0.0), axis=1, keepdims=True)
        spot = relative[:, t : t + 1].astype(jnp.float32) * float(packing.rows) + own_slot
        if active is not None:
            spot = jnp.where(active[:, 0:1], spot, -65536.0)
        spot_ref[:, t : t + 1] = spot
        logit = jnp.zeros((rows, 1), jnp.float32)
        for k in range(experts):
            logit = jnp.where(chosen[:, t : t + 1] == k, logits[k], logit)
        picked.append(logit)
    weight_ref[:, 0:1] = jax.nn.sigmoid(picked[0] - picked[1])
    weight_ref[:, 1:2] = jax.nn.sigmoid(picked[1] - picked[0])


def route(normed, chosen, lengths, router_weight, packing, prompts):
    rows = normed.shape[0]
    return pl.pallas_call(
        functools.partial(route_kernel, packing, router_weight.shape[1], prompts),
        out_shape=[jax.ShapeDtypeStruct((rows, 2), jnp.float32)] * 2,
        in_specs=[SMEM] + [VMEM] * 3,
        out_specs=[VMEM] * 2,
        compiler_params=pltpu.CompilerParams(vmem_limit_bytes=8 << 20),
        name="route",
    )(lengths, chosen, normed, router_weight.T)


def cuts(total, step):
    return [(start, min(start + step, total)) for start in range(0, total, step)]


def expert_kernel(packing, count, after, *refs):
    row_refs = refs[:count]
    gate_hbm, up_hbm, down_hbm = refs[count : count + 3]
    out_refs = refs[count + 3 + after : 2 * count + 3 + after]
    gate_ref, up_ref, down_ref, rows_ref, total_ref, sems = refs[2 * count + 3 + after :]
    units = gate_hbm.shape[0]
    unit_cuts = cuts(units, UNIT_STEP)
    copies = []
    for i, (lo, hi) in enumerate(unit_cuts):
        for t, (source, target) in enumerate(
            ((gate_hbm, gate_ref), (up_hbm, up_ref), (down_hbm, down_ref))
        ):
            copies.append(
                pltpu.make_async_copy(source.at[lo:hi], target.at[lo:hi], sems.at[3 * i + t])
            )
    for copy in copies:
        copy.start()

    cap, chunks, width, high = packing.cap, packing.chunks, packing.width, packing.rows
    per_ref = row_refs[0].shape[0] // high
    blocks = count * per_ref
    group = 16
    row_at = lax.broadcasted_iota(jnp.int32, (group * cap, group * high), 0)
    place = lax.broadcasted_iota(jnp.int32, (group * cap, group * high), 1)
    source_row = (row_at // cap) * high + row_at % cap
    packed = jnp.concatenate([ref[...] for ref in row_refs], axis=0)
    for g in range(blocks // group):
        part = packed[g * group * high : (g + 1) * group * high]
        for j in range(chunks):
            pick = jnp.where(place == source_row + j * cap, 1.0, 0.0).astype(jnp.bfloat16)
            rows_ref[g * group * cap : (g + 1) * group * cap, j * width : (j + 1) * width] = (
                jnp.dot(pick, part, preferred_element_type=jnp.float32).astype(jnp.bfloat16)
            )

    def down(i, hidden):
        lo, hi = unit_cuts[i]
        copies[3 * i + 2].wait()
        term = jnp.dot(hidden, down_ref[lo:hi, :], preferred_element_type=jnp.float32)
        if i == 0:
            total_ref[...] = term
        else:
            total_ref[...] += term

    hidden = None
    for i, (lo, hi) in enumerate(unit_cuts):
        contract = (((1,), (1,)), ((), ()))
        rows = rows_ref[...]
        copies[3 * i].wait()
        gate = lax.dot_general(
            rows, gate_ref[lo:hi, :], contract, preferred_element_type=jnp.float32
        )
        copies[3 * i + 1].wait()
        up = lax.dot_general(rows, up_ref[lo:hi, :], contract, preferred_element_type=jnp.float32)
        if i > 0:
            down(i - 1, hidden)
        hidden = (gate * jax.nn.sigmoid(gate) * up).astype(jnp.bfloat16)
    down(len(unit_cuts) - 1, hidden)
    total = total_ref[...].astype(jnp.bfloat16)

    place = lax.broadcasted_iota(jnp.int32, (group * high, group * cap), 0)
    row_at = lax.broadcasted_iota(jnp.int32, (group * high, group * cap), 1)
    target = (row_at // cap) * high + row_at % cap
    per_group = group // per_ref
    for g in range(blocks // group):
        packed = None
        for j in range(chunks):
            put = jnp.where(place == target + j * cap, 1.0, 0.0).astype(jnp.bfloat16)
            term = jnp.dot(
                put,
                total[g * group * cap : (g + 1) * group * cap, j * width : (j + 1) * width],
                preferred_element_type=jnp.float32,
            )
            packed = term if packed is None else packed + term
        packed = packed.astype(jnp.bfloat16)
        for i in range(per_group):
            out_refs[g * per_group + i][...] = packed[i * per_ref * high : (i + 1) * per_ref * high]


def expert_rows(arrays, w_gate, w_up, w_down, packing, after):
    features, units = w_gate.shape
    rows = len(arrays) * (arrays[0].shape[0] // packing.rows) * packing.cap
    return pl.pallas_call(
        functools.partial(expert_kernel, packing, len(arrays), len(after)),
        out_shape=[jax.ShapeDtypeStruct(arrays[0].shape, jnp.bfloat16)] * len(arrays),
        in_specs=[VMEM] * len(arrays) + [ANY] * (3 + len(after)),
        out_specs=[VMEM] * len(arrays),
        scratch_shapes=[
            pltpu.VMEM((units, features), jnp.bfloat16),
            pltpu.VMEM((units, features), jnp.bfloat16),
            pltpu.VMEM((units, features), jnp.bfloat16),
            pltpu.VMEM((rows, features), jnp.bfloat16),
            pltpu.VMEM((rows, features), jnp.float32),
            pltpu.SemaphoreType.DMA((3 * len(cuts(units, UNIT_STEP)),)),
        ],
        compiler_params=pltpu.CompilerParams(vmem_limit_bytes=48 << 20),
        cost_estimate=pl.CostEstimate(
            flops=6 * rows * features * units,
            bytes_accessed=6 * features * units,
            transcendentals=rows * units,
        ),
        name="experts",
    )(*arrays, w_gate.T, w_up.T, w_down, *after)


def combine_kernel(packing, spot_ref, weight_ref, *refs):
    block_refs, out_ref = refs[:-1], refs[-1]
    rows = out_ref.shape[0]
    blocks = jnp.concatenate([ref[...] for ref in block_refs], axis=0)
    place = lax.broadcasted_iota(jnp.int32, (rows, blocks.shape[0]), 1).astype(jnp.float32)
    picks = [
        jnp.where(place - float(j * packing.cap) == spot_ref[:, t : t + 1], 1.0, 0.0)
        for t in range(2)
        for j in range(packing.chunks)
    ]
    if rows % 16 == 0:
        table = jnp.concatenate(picks, axis=0).astype(jnp.bfloat16)
        picked = jnp.dot(table, blocks, preferred_element_type=jnp.float32)
        picked = [picked[i * rows : (i + 1) * rows] for i in range(len(picks))]
    else:
        picked = [
            jnp.dot(pick.astype(jnp.bfloat16), blocks, preferred_element_type=jnp.float32)
            for pick in picks
        ]
    for j in range(packing.chunks):
        out_ref[:, j * packing.width : (j + 1) * packing.width] = (
            weight_ref[:, 0:1] * picked[j] + weight_ref[:, 1:2] * picked[packing.chunks + j]
        ).astype(jnp.bfloat16)


def combine(spot, weights, blocks, packing, rows, features):
    return pl.pallas_call(
        functools.partial(combine_kernel, packing),
        out_shape=jax.ShapeDtypeStruct((rows, features), jnp.bfloat16),
        in_specs=[VMEM] * (2 + len(blocks)),
        out_specs=VMEM,
        compiler_params=pltpu.CompilerParams(vmem_limit_bytes=8 << 20),
        name="combine",
    )(spot, weights, *blocks)


def dispatch(blocks, grid):
    first = jnp.concatenate(
        [blocks[0]] + [grid.send(blocks[k], 0, k) for k in range(1, grid.experts)], axis=0
    )
    own = [first] + [grid.send(first, 1, k) for k in range(1, grid.pairs)]
    return own + [grid.send(value, 2, 1) for value in own]


def give_back(results, grid):
    own, other = results[: grid.pairs], results[grid.pairs :]
    sums = []
    for k in list(range(1, grid.pairs)) + [0]:
        sums.append(own[k].astype(jnp.float32) + grid.send(other[k], 2, 1).astype(jnp.float32))
    total = sums[-1]
    for k in range(1, grid.pairs):
        total = total + grid.send(sums[k - 1].astype(jnp.bfloat16), 1, -k).astype(jnp.float32)
    total = total.astype(jnp.bfloat16)
    rows = total.shape[0] // grid.experts
    parts = [total[k * rows : (k + 1) * rows] for k in range(grid.experts)]
    return [parts[0]] + [grid.send(parts[k], 0, -k) for k in range(1, grid.experts)]


def project(text_hidden, caption_weight, grid):
    rows = text_hidden.shape[0] // (grid.experts * grid.pairs * 2)
    text = text_hidden.reshape(grid.experts, grid.pairs, 2, rows, text_hidden.shape[1])
    text = jnp.roll(text, -grid.expert, axis=0)
    text = jnp.roll(text, -grid.pair, axis=1)
    text = jnp.roll(text, -grid.core, axis=2)
    text = jnp.transpose(text, (2, 1, 0, 3, 4)).reshape(2, -1, text_hidden.shape[1])
    other = jnp.dot(text[1], caption_weight, preferred_element_type=jnp.float32)
    own = jnp.dot(text[0], caption_weight, preferred_element_type=jnp.float32)
    total = own + grid.send(other.astype(jnp.bfloat16), 2, 1).astype(jnp.float32)
    rows_pair = rows * grid.experts
    parts = [total[k * rows_pair : (k + 1) * rows_pair] for k in range(grid.pairs)]
    total = parts[0]
    crossing = [part.astype(jnp.bfloat16) for part in parts[1:]]
    for k in range(1, grid.pairs):
        total = total + grid.send(crossing[k - 1], 1, k).astype(jnp.float32)
    parts = [total[k * rows : (k + 1) * rows] for k in range(grid.experts)]
    terms = [parts[0]] + [
        grid.send(parts[k].astype(jnp.bfloat16), 0, k) for k in range(1, grid.experts)
    ]
    return (terms, crossing)


def local(
    image_rows,
    text_hidden,
    caption_weight,
    mod_scale,
    mod_shift,
    router_weight,
    image_experts,
    caption_experts,
    prompt_lengths,
    w_gate,
    w_up,
    w_down,
):
    devices = lax.axis_size("dev")
    features, experts = router_weight.shape
    grid = Grid(devices, experts)
    image_packing = Packing(image_rows.shape[0] * 3 // 4, features)
    caption_packing = Packing(text_hidden.shape[0] // devices // 2 + 1, features)

    terms, crossing = project(text_hidden, caption_weight, grid)
    caption_normed, caption_blocks = modulate(
        terms, caption_experts, prompt_lengths, mod_scale, mod_shift,
        caption_packing, experts, True, [],
    )
    image_normed, image_blocks = modulate(
        [image_rows], image_experts, prompt_lengths, mod_scale, mod_shift,
        image_packing, experts, False, crossing[:1],
    )

    def finish(normed, blocks, chosen, packing, prompts, after):
        arrays = dispatch(blocks, grid)
        spot, weights = route(normed, chosen, prompt_lengths, router_weight, packing, prompts)
        results = expert_rows(arrays, w_gate, w_up, w_down, packing, after + [spot])
        blocks = give_back(results, grid)
        return combine(spot, weights, blocks, packing, chosen.shape[0], features)

    image_out = finish(
        image_normed, image_blocks, image_experts, image_packing, False, caption_blocks[:1]
    )
    caption_out = finish(
        caption_normed, caption_blocks, caption_experts, caption_packing, True, []
    )
    return (image_out, caption_out)


def solution(mesh):
    in_specs = (
        P(("groups", "dev"), None),
        P("groups", "dev"),
        P("dev", None),
        P(),
        P(),
        P(),
        P(("groups", "dev"), None),
        P(("groups", "dev"), None),
        P("groups"),
        P(None, "dev"),
        P(None, "dev"),
        P("dev", None),
    )
    out_specs = (P(("groups", "dev"), None), P(("groups", "dev"), None))
    return jax.shard_map(local, mesh=mesh, in_specs=in_specs, out_specs=out_specs, check_vma=False)
```

```python
import functools

import jax
import jax.numpy as jnp
from jax import lax
from jax.experimental import pallas as pl
from jax.experimental.pallas import tpu as pltpu
from jax.sharding import PartitionSpec as P

PLEN = 128
VMEM = pl.BlockSpec(memory_space=pltpu.VMEM)
SMEM = pl.BlockSpec(memory_space=pltpu.SMEM)
ANY = pl.BlockSpec(memory_space=pl.ANY)
UNIT_STEP = 256


class Grid:
    def __init__(self, devices, experts):
        self.experts = experts
        self.pairs = devices // experts // 2
        index = lax.axis_index("dev")
        self.pair = (index // 2) % self.pairs
        self.core = index % 2

    def send(self, value, axis, step):
        moves = []
        for expert in range(self.experts):
            for pair in range(self.pairs):
                for core in range(2):
                    to = [expert, pair, core]
                    to[axis] = (to[axis] + step) % (self.experts, self.pairs, 2)[axis]
                    moves.append(
                        (
                            (expert * self.pairs + pair) * 2 + core,
                            (to[0] * self.pairs + to[1]) * 2 + to[2],
                        )
                    )
        return lax.ppermute(value, "dev", moves)

    def exchange(self, value):
        sharing = self.pairs * 2
        groups = [[e * sharing + i for e in range(self.experts)] for i in range(sharing)]
        return lax.all_to_all(
            value, "dev", split_axis=0, concat_axis=0, axis_index_groups=groups, tiled=True
        )


class Packing:
    def __init__(self, cap, features):
        best = None
        for chunks in range(1, features // 128 + 1):
            if features % (128 * chunks):
                continue
            rows = -(-cap * chunks // 16) * 16
            cost = rows * (features // chunks)
            if best is None or cost < best[0]:
                best = (cost, chunks, rows)
        _, self.chunks, self.rows = best
        self.cap = cap
        self.width = features // self.chunks


def live(position, lengths_ref):
    prompt = position // PLEN
    length = jnp.zeros_like(position)
    for p in range(lengths_ref.shape[0]):
        length = jnp.where(prompt == p, lengths_ref[p], length)
    return position % PLEN < length


def place_kernel(packing, prompts, lengths_ref, across_ref, down_ref, slot_ref, spot_ref):
    experts, rows = slot_ref.shape
    dead = -65536.0
    first_row = lax.axis_index("dev") * rows

    def order(dim):
        ids = [lax.broadcasted_iota(jnp.int32, (rows, rows), d) for d in (dim, 1 - dim)]
        return (ids[0] < ids[1]).astype(jnp.float32)

    expert_at = lax.broadcasted_iota(jnp.int32, (experts, rows), 0)
    routed = (across_ref[0:1, :] == expert_at) | (across_ref[1:2, :] == expert_at)
    if prompts:
        row = lax.broadcasted_iota(jnp.int32, (experts, rows), 1)
        routed = routed & live(first_row + row, lengths_ref)
    slot = jnp.dot(routed.astype(jnp.float32), order(0), preferred_element_type=jnp.float32)
    slot_ref[...] = jnp.where(routed, slot, dead)

    expert_at = lax.broadcasted_iota(jnp.int32, (rows, experts), 1)
    routed = (down_ref[:, 0:1] == expert_at) | (down_ref[:, 1:2] == expert_at)
    if prompts:
        row = lax.broadcasted_iota(jnp.int32, (rows, experts), 0)
        routed = routed & live(first_row + row, lengths_ref)
    slot = jnp.dot(order(1), routed.astype(jnp.float32), preferred_element_type=jnp.float32)
    spot = expert_at.astype(jnp.float32) * float(packing.rows) + slot
    spot = jnp.where(routed, spot, dead)
    for t in range(2):
        mine = down_ref[:, t : t + 1] == expert_at
        spot_ref[:, t : t + 1] = jnp.sum(jnp.where(mine, spot, 0.0), axis=1, keepdims=True)


def place(chosen, lengths, experts, packing, prompts):
    rows = chosen.shape[0]
    return pl.pallas_call(
        functools.partial(place_kernel, packing, prompts),
        out_shape=[
            jax.ShapeDtypeStruct((experts, rows), jnp.float32),
            jax.ShapeDtypeStruct((rows, 2), jnp.float32),
        ],
        in_specs=[SMEM] + [VMEM] * 2,
        out_specs=[VMEM] * 2,
        compiler_params=pltpu.CompilerParams(vmem_limit_bytes=8 << 20),
        name="place",
    )(lengths, chosen.T, chosen)


def modulate_kernel(packing, experts, slot_ref, scale_ref, shift_ref, value_ref, *refs):
    normed_ref, packed_ref = refs[-2:]
    rows = normed_ref.shape[0]
    values = value_ref[0].astype(jnp.float32)
    for k in range(1, value_ref.shape[0]):
        values = values + value_ref[k].astype(jnp.float32)
    values = values.astype(jnp.bfloat16).astype(jnp.float32)
    center = values - jnp.mean(values, axis=1, keepdims=True)
    spread = jnp.mean(center * center, axis=1, keepdims=True)
    normed = center * lax.rsqrt(spread + 1e-06) * scale_ref[...] + shift_ref[...]
    normed = normed.astype(jnp.bfloat16)
    normed_ref[...] = normed

    place = lax.broadcasted_iota(jnp.int32, (packing.rows, rows), 0).astype(jnp.float32)
    packed = None
    for j in range(packing.chunks):
        into = jnp.concatenate(
            [
                jnp.where(place - float(j * packing.cap) == slot_ref[k : k + 1, :], 1.0, 0.0)
                for k in range(experts)
            ],
            axis=0,
        ).astype(jnp.bfloat16)
        term = jnp.dot(
            into,
            normed[:, j * packing.width : (j + 1) * packing.width],
            preferred_element_type=jnp.float32,
        )
        packed = term if packed is None else packed + term
    packed_ref[...] = packed.astype(jnp.bfloat16)
def modulate(terms, slot, mod_scale, mod_shift, packing, experts, after):
    _, rows, features = terms.shape
    return pl.pallas_call(
        functools.partial(modulate_kernel, packing, experts),
        out_shape=[
            jax.ShapeDtypeStruct((rows, features), jnp.bfloat16),
            jax.ShapeDtypeStruct((experts * packing.rows, packing.width), jnp.bfloat16),
        ],
        in_specs=[VMEM] * 4 + [ANY] * len(after),
        out_specs=[VMEM] * 2,
        compiler_params=pltpu.CompilerParams(vmem_limit_bytes=8 << 20),
        name="modulate",
    )(slot, mod_scale.reshape(1, -1), mod_shift.reshape(1, -1), terms, *after)


def route_kernel(chosen_ref, normed_ref, router_ref, weight_ref):
    normed = normed_ref[...].astype(jnp.float32)
    logits = [
        jnp.sum(normed * router_ref[k : k + 1, :], axis=1, keepdims=True)
        for k in range(router_ref.shape[0])
    ]
    picked = []
    for t in range(2):
        logit = jnp.zeros_like(logits[0])
        for k, value in enumerate(logits):
            logit = jnp.where(chosen_ref[:, t : t + 1] == k, value, logit)
        picked.append(logit)
    weight_ref[:, 0:1] = jax.nn.sigmoid(picked[0] - picked[1])
    weight_ref[:, 1:2] = jax.nn.sigmoid(picked[1] - picked[0])


def route(normed, chosen, router_weight):
    return pl.pallas_call(
        route_kernel,
        out_shape=jax.ShapeDtypeStruct(chosen.shape, jnp.float32),
        in_specs=[VMEM] * 3,
        out_specs=VMEM,
        compiler_params=pltpu.CompilerParams(vmem_limit_bytes=8 << 20),
        name="route",
    )(chosen, normed, router_weight.T)


def cuts(total, step):
    return [(start, min(start + step, total)) for start in range(0, total, step)]


def expert_kernel(packing, count, after, *refs):
    row_refs = refs[:count]
    gate_hbm, up_hbm, down_hbm = refs[count : count + 3]
    out_refs = refs[count + 3 + after : 2 * count + 3 + after]
    gate_ref, up_ref, down_ref, rows_ref, total_ref, sems = refs[2 * count + 3 + after :]
    rows = total_ref.shape[0]
    units = gate_hbm.shape[0]
    unit_cuts = cuts(units, UNIT_STEP)
    copies = []
    for i, (lo, hi) in enumerate(unit_cuts):
        for t, (source, target) in enumerate(
            ((gate_hbm, gate_ref), (up_hbm, up_ref), (down_hbm, down_ref))
        ):
            copies.append(
                pltpu.make_async_copy(source.at[lo:hi], target.at[lo:hi], sems.at[3 * i + t])
            )
    for copy in copies:
        copy.start()

    cap, chunks, width, high = packing.cap, packing.chunks, packing.width, packing.rows
    per_ref = row_refs[0].shape[0] // high
    blocks = count * per_ref
    group = 16
    row_at = lax.broadcasted_iota(jnp.int32, (group * cap, group * high), 0)
    place = lax.broadcasted_iota(jnp.int32, (group * cap, group * high), 1)
    source_row = (row_at // cap) * high + row_at % cap
    packed = jnp.concatenate([ref[...] for ref in row_refs], axis=0)
    spare = rows_ref.shape[1] - rows
    for j in range(chunks):
        pick = jnp.where(place == source_row + j * cap, 1.0, 0.0).astype(jnp.bfloat16)
        parts = [
            jnp.dot(
                pick,
                packed[g * group * high : (g + 1) * group * high],
                preferred_element_type=jnp.float32,
            )
            for g in range(blocks // group)
        ]
        if spare:
            parts.append(jnp.zeros((spare, width), jnp.float32))
        part = jnp.concatenate(parts, axis=0)
        rows_ref[j * width : (j + 1) * width, :] = part.T.astype(jnp.bfloat16)

    def down(i, hidden):
        lo, hi = unit_cuts[i]
        copies[3 * i + 2].wait()
        term = jnp.dot(hidden, down_ref[lo:hi, :], preferred_element_type=jnp.float32)
        if i == 0:
            total_ref[...] = term
        else:
            total_ref[...] += term

    hidden = None
    for i, (lo, hi) in enumerate(unit_cuts):
        copies[3 * i].wait()
        gate = jnp.dot(gate_ref[lo:hi, :], rows_ref[...], preferred_element_type=jnp.float32)
        copies[3 * i + 1].wait()
        up = jnp.dot(up_ref[lo:hi, :], rows_ref[...], preferred_element_type=jnp.float32)
        if i > 0:
            down(i - 1, hidden)
        hidden = (gate * jax.nn.sigmoid(gate) * up).T[0:rows].astype(jnp.bfloat16)
    down(len(unit_cuts) - 1, hidden)
    total = total_ref[...].astype(jnp.bfloat16)

    place = lax.broadcasted_iota(jnp.int32, (group * high, group * cap), 0)
    row_at = lax.broadcasted_iota(jnp.int32, (group * high, group * cap), 1)
    target = (row_at // cap) * high + row_at % cap
    per_group = group // per_ref
    for g in range(blocks // group):
        packed = None
        for j in range(chunks):
            put = jnp.where(place == target + j * cap, 1.0, 0.0).astype(jnp.bfloat16)
            term = jnp.dot(
                put,
                total[g * group * cap : (g + 1) * group * cap, j * width : (j + 1) * width],
                preferred_element_type=jnp.float32,
            )
            packed = term if packed is None else packed + term
        packed = packed.astype(jnp.bfloat16)
        for i in range(per_group):
            out_refs[g * per_group + i][...] = packed[i * per_ref * high : (i + 1) * per_ref * high]


def expert_rows(arrays, w_gate, w_up, w_down, packing, after):
    features, units = w_gate.shape
    rows = len(arrays) * (arrays[0].shape[0] // packing.rows) * packing.cap
    return pl.pallas_call(
        functools.partial(expert_kernel, packing, len(arrays), len(after)),
        out_shape=[jax.ShapeDtypeStruct(arrays[0].shape, jnp.bfloat16)] * len(arrays),
        in_specs=[VMEM] * len(arrays) + [ANY] * (3 + len(after)),
        out_specs=[VMEM] * len(arrays),
        scratch_shapes=[
            pltpu.VMEM((units, features), jnp.bfloat16),
            pltpu.VMEM((units, features), jnp.bfloat16),
            pltpu.VMEM((units, features), jnp.bfloat16),
            pltpu.VMEM((features, -(-rows // 128) * 128), jnp.bfloat16),
            pltpu.VMEM((rows, features), jnp.float32),
            pltpu.SemaphoreType.DMA((3 * len(cuts(units, UNIT_STEP)),)),
        ],
        compiler_params=pltpu.CompilerParams(vmem_limit_bytes=48 << 20),
        cost_estimate=pl.CostEstimate(
            flops=6 * rows * features * units,
            bytes_accessed=6 * features * units,
            transcendentals=rows * units,
        ),
        name="experts",
    )(*arrays, w_gate.T, w_up.T, w_down, *after)


def combine_kernel(packing, spot_ref, weight_ref, block_ref, out_ref):
    rows = out_ref.shape[0]
    blocks = block_ref[...]
    place = lax.broadcasted_iota(jnp.int32, (rows, blocks.shape[0]), 1).astype(jnp.float32)
    picks = [
        jnp.where(place - float(j * packing.cap) == spot_ref[:, t : t + 1], 1.0, 0.0)
        for t in range(2)
        for j in range(packing.chunks)
    ]
    if rows % 16 == 0:
        table = jnp.concatenate(picks, axis=0).astype(jnp.bfloat16)
        picked = jnp.dot(table, blocks, preferred_element_type=jnp.float32)
        picked = [picked[i * rows : (i + 1) * rows] for i in range(len(picks))]
    else:
        picked = [
            jnp.dot(pick.astype(jnp.bfloat16), blocks, preferred_element_type=jnp.float32)
            for pick in picks
        ]
    for j in range(packing.chunks):
        out_ref[:, j * packing.width : (j + 1) * packing.width] = (
            weight_ref[:, 0:1] * picked[j] + weight_ref[:, 1:2] * picked[packing.chunks + j]
        ).astype(jnp.bfloat16)


def combine(spot, weights, blocks, packing, rows, features):
    return pl.pallas_call(
        functools.partial(combine_kernel, packing),
        out_shape=jax.ShapeDtypeStruct((rows, features), jnp.bfloat16),
        in_specs=[VMEM] * 3,
        out_specs=VMEM,
        compiler_params=pltpu.CompilerParams(vmem_limit_bytes=8 << 20),
        name="combine",
    )(spot, weights, blocks)


def dispatch(blocks, grid):
    first = grid.exchange(blocks)
    own = [first] + [grid.send(first, 1, k) for k in range(1, grid.pairs)]
    return own + [grid.send(value, 2, 1) for value in own]


def give_back(results, grid):
    own, other = results[: grid.pairs], results[grid.pairs :]
    sums = []
    for k in list(range(1, grid.pairs)) + [0]:
        sums.append(own[k].astype(jnp.float32) + grid.send(other[k], 2, 1).astype(jnp.float32))
    total = sums[-1]
    for k in range(1, grid.pairs):
        total = total + grid.send(sums[k - 1].astype(jnp.bfloat16), 1, -k).astype(jnp.float32)
    return grid.exchange(total.astype(jnp.bfloat16))


def project(text_hidden, caption_weight, grid):
    rows = text_hidden.shape[0] // (grid.experts * grid.pairs * 2)
    text = text_hidden.reshape(grid.experts, grid.pairs, 2, rows, text_hidden.shape[1])
    text = jnp.roll(text, -grid.pair, axis=1)
    text = jnp.roll(text, -grid.core, axis=2)
    text = jnp.transpose(text, (2, 1, 0, 3, 4)).reshape(2, -1, text_hidden.shape[1])
    other = jnp.dot(text[1], caption_weight, preferred_element_type=jnp.float32)
    own = jnp.dot(text[0], caption_weight, preferred_element_type=jnp.float32)
    total = own + grid.send(other.astype(jnp.bfloat16), 2, 1).astype(jnp.float32)
    rows_pair = rows * grid.experts
    parts = [total[k * rows_pair : (k + 1) * rows_pair] for k in range(grid.pairs)]
    total = parts[0]
    crossing = [part.astype(jnp.bfloat16) for part in parts[1:]]
    for k in range(1, grid.pairs):
        total = total + grid.send(crossing[k - 1], 1, k).astype(jnp.float32)
    terms = grid.exchange(total.astype(jnp.bfloat16))
    return (terms.reshape(grid.experts, rows, -1), crossing)


def local(
    image_rows,
    text_hidden,
    caption_weight,
    mod_scale,
    mod_shift,
    router_weight,
    image_experts,
    caption_experts,
    prompt_lengths,
    w_gate,
    w_up,
    w_down,
):
    devices = lax.axis_size("dev")
    features, experts = router_weight.shape
    grid = Grid(devices, experts)
    image_packing = Packing(image_rows.shape[0] * 3 // 4, features)
    caption_packing = Packing(text_hidden.shape[0] // devices // 2 + 1, features)

    terms, crossing = project(text_hidden, caption_weight, grid)
    image_slot, image_spot = place(image_experts, prompt_lengths, experts, image_packing, False)
    caption_slot, caption_spot = place(
        caption_experts, prompt_lengths, experts, caption_packing, True
    )
    caption_normed, caption_blocks = modulate(
        terms, caption_slot, mod_scale, mod_shift, caption_packing, experts, []
    )
    image_normed, image_blocks = modulate(
        image_rows[None], image_slot, mod_scale, mod_shift, image_packing, experts, crossing[:1]
    )

    def finish(normed, blocks, chosen, spot, packing, after):
        arrays = dispatch(blocks, grid)
        weights = route(normed, chosen, router_weight)
        results = expert_rows(arrays, w_gate, w_up, w_down, packing, after + [weights])
        blocks = give_back(results, grid)
        return combine(spot, weights, blocks, packing, chosen.shape[0], features)

    image_out = finish(
        image_normed, image_blocks, image_experts, image_spot, image_packing, [caption_blocks]
    )
    caption_out = finish(
        caption_normed, caption_blocks, caption_experts, caption_spot, caption_packing, []
    )
    return (image_out, caption_out)


def solution(mesh):
    in_specs = (
        P(("groups", "dev"), None),
        P("groups", "dev"),
        P("dev", None),
        P(),
        P(),
        P(),
        P(("groups", "dev"), None),
        P(("groups", "dev"), None),
        P("groups"),
        P(None, "dev"),
        P(None, "dev"),
        P("dev", None),
    )
    out_specs = (P(("groups", "dev"), None), P(("groups", "dev"), None))
    return jax.shard_map(local, mesh=mesh, in_specs=in_specs, out_specs=out_specs, check_vma=False)
```

```python
import functools

import jax
import jax.numpy as jnp
from jax import lax
from jax.experimental import pallas as pl
from jax.experimental.pallas import tpu as pltpu
from jax.sharding import PartitionSpec as P

PLEN = 128
VMEM = pl.BlockSpec(memory_space=pltpu.VMEM)
SMEM = pl.BlockSpec(memory_space=pltpu.SMEM)
ANY = pl.BlockSpec(memory_space=pl.ANY)
UNIT_STEP = 640


class Grid:
    def __init__(self, devices, experts):
        self.experts = experts
        self.pairs = devices // experts // 2
        index = lax.axis_index("dev")
        self.expert = index // (self.pairs * 2)
        self.pair = (index // 2) % self.pairs
        self.core = index % 2

    def send(self, value, axis, step):
        moves = []
        for expert in range(self.experts):
            for pair in range(self.pairs):
                for core in range(2):
                    to = [expert, pair, core]
                    to[axis] = (to[axis] + step) % (self.experts, self.pairs, 2)[axis]
                    moves.append(
                        (
                            (expert * self.pairs + pair) * 2 + core,
                            (to[0] * self.pairs + to[1]) * 2 + to[2],
                        )
                    )
        return lax.ppermute(value, "dev", moves)


class Packing:
    def __init__(self, cap, features):
        best = None
        for chunks in range(1, features // 128 + 1):
            if features % (128 * chunks):
                continue
            rows = -(-cap * chunks // 16) * 16
            cost = rows * (features // chunks)
            if best is None or cost < best[0]:
                best = (cost, chunks, rows)
        _, self.chunks, self.rows = best
        self.cap = cap
        self.width = features // self.chunks


def live(position, lengths_ref):
    prompt = position // PLEN
    length = jnp.zeros_like(position)
    for p in range(lengths_ref.shape[0]):
        length = jnp.where(prompt == p, lengths_ref[p], length)
    return position % PLEN < length


def place_kernel(packing, prompts, lengths_ref, across_ref, down_ref, slot_ref, spot_ref):
    experts, rows = slot_ref.shape
    dead = -65536.0
    index = lax.axis_index("dev")
    first_row = index * rows
    shift = experts - index // (lax.axis_size("dev") // experts)
    across, down = lax.rem(across_ref[...] + shift, experts), lax.rem(down_ref[...] + shift, experts)

    def order(dim):
        ids = [lax.broadcasted_iota(jnp.int32, (rows, rows), d) for d in (dim, 1 - dim)]
        return (ids[0] < ids[1]).astype(jnp.float32)

    expert_at = lax.broadcasted_iota(jnp.int32, (experts, rows), 0)
    routed = (across[0:1, :] == expert_at) | (across[1:2, :] == expert_at)
    if prompts:
        row = lax.broadcasted_iota(jnp.int32, (experts, rows), 1)
        routed = routed & live(first_row + row, lengths_ref)
    slot = jnp.dot(routed.astype(jnp.float32), order(0), preferred_element_type=jnp.float32)
    slot_ref[...] = jnp.where(routed, slot, dead)

    expert_at = lax.broadcasted_iota(jnp.int32, (rows, experts), 1)
    routed = (down[:, 0:1] == expert_at) | (down[:, 1:2] == expert_at)
    if prompts:
        row = lax.broadcasted_iota(jnp.int32, (rows, experts), 0)
        routed = routed & live(first_row + row, lengths_ref)
    slot = jnp.dot(order(1), routed.astype(jnp.float32), preferred_element_type=jnp.float32)
    spot = expert_at.astype(jnp.float32) * float(packing.rows) + slot
    spot = jnp.where(routed, spot, dead)
    for t in range(2):
        mine = down[:, t : t + 1] == expert_at
        spot_ref[:, t : t + 1] = jnp.sum(jnp.where(mine, spot, 0.0), axis=1, keepdims=True)


def place(chosen, lengths, experts, packing, prompts):
    rows = chosen.shape[0]
    return pl.pallas_call(
        functools.partial(place_kernel, packing, prompts),
        out_shape=[
            jax.ShapeDtypeStruct((experts, rows), jnp.float32),
            jax.ShapeDtypeStruct((rows, 2), jnp.float32),
        ],
        in_specs=[SMEM] + [VMEM] * 2,
        out_specs=[VMEM] * 2,
        compiler_params=pltpu.CompilerParams(vmem_limit_bytes=8 << 20),
        name="place",
    )(lengths, chosen.T, chosen)


def modulate_kernel(packing, experts, count, slot_ref, scale_ref, shift_ref, *refs):
    normed_ref, packed_refs = refs[-1 - experts], refs[-experts:]
    rows = normed_ref.shape[0]
    values = refs[0][...].astype(jnp.float32)
    for ref in refs[1:count]:
        values = values + ref[...].astype(jnp.float32)
    values = values.astype(jnp.bfloat16).astype(jnp.float32)
    center = values - jnp.mean(values, axis=1, keepdims=True)
    spread = jnp.mean(center * center, axis=1, keepdims=True)
    normed = center * lax.rsqrt(spread + 1e-06) * scale_ref[...] + shift_ref[...]
    normed = normed.astype(jnp.bfloat16)
    normed_ref[...] = normed

    place = lax.broadcasted_iota(jnp.int32, (packing.rows, rows), 0).astype(jnp.float32)
    packed = None
    for j in range(packing.chunks):
        into = jnp.concatenate(
            [
                jnp.where(place - float(j * packing.cap) == slot_ref[k : k + 1, :], 1.0, 0.0)
                for k in range(experts)
            ],
            axis=0,
        ).astype(jnp.bfloat16)
        term = jnp.dot(
            into,
            normed[:, j * packing.width : (j + 1) * packing.width],
            preferred_element_type=jnp.float32,
        )
        packed = term if packed is None else packed + term
    for k in range(experts):
        packed_refs[k][...] = packed[k * packing.rows : (k + 1) * packing.rows].astype(
            jnp.bfloat16
        )
def modulate(terms, slot, mod_scale, mod_shift, packing, experts, after):
    rows, features = terms[0].shape
    packed = jax.ShapeDtypeStruct((packing.rows, packing.width), jnp.bfloat16)
    results = pl.pallas_call(
        functools.partial(modulate_kernel, packing, experts, len(terms)),
        out_shape=[jax.ShapeDtypeStruct((rows, features), jnp.bfloat16)] + [packed] * experts,
        in_specs=[VMEM] * (3 + len(terms)) + [ANY] * len(after),
        out_specs=[VMEM] * (1 + experts),
        compiler_params=pltpu.CompilerParams(vmem_limit_bytes=8 << 20),
        name="modulate",
    )(slot, mod_scale.reshape(1, -1), mod_shift.reshape(1, -1), *terms, *after)
    return (results[0], list(results[1:]))


def route_kernel(chosen_ref, normed_ref, router_ref, weight_ref):
    normed = normed_ref[...].astype(jnp.float32)
    logits = [
        jnp.sum(normed * router_ref[k : k + 1, :], axis=1, keepdims=True)
        for k in range(router_ref.shape[0])
    ]
    picked = []
    for t in range(2):
        logit = jnp.zeros_like(logits[0])
        for k, value in enumerate(logits):
            logit = jnp.where(chosen_ref[:, t : t + 1] == k, value, logit)
        picked.append(logit)
    weight_ref[:, 0:1] = jax.nn.sigmoid(picked[0] - picked[1])
    weight_ref[:, 1:2] = jax.nn.sigmoid(picked[1] - picked[0])


def route(normed, chosen, router_weight):
    return pl.pallas_call(
        route_kernel,
        out_shape=jax.ShapeDtypeStruct(chosen.shape, jnp.float32),
        in_specs=[VMEM] * 3,
        out_specs=VMEM,
        compiler_params=pltpu.CompilerParams(vmem_limit_bytes=8 << 20),
        name="route",
    )(chosen, normed, router_weight.T)


def cuts(total, step):
    return [(start, min(start + step, total)) for start in range(0, total, step)]


def expert_kernel(packing, count, after, *refs):
    row_refs = refs[:count]
    gate_hbm, up_hbm, down_hbm = refs[count : count + 3]
    out_refs = refs[count + 3 + after : 2 * count + 3 + after]
    gate_ref, up_ref, down_ref, rows_ref, total_ref, sems = refs[2 * count + 3 + after :]
    rows = total_ref.shape[0]
    units = gate_hbm.shape[0]
    unit_cuts = cuts(units, UNIT_STEP)
    copies = []
    for i, (lo, hi) in enumerate(unit_cuts):
        for t, (source, target) in enumerate(
            ((gate_hbm, gate_ref), (up_hbm, up_ref), (down_hbm, down_ref))
        ):
            copies.append(
                pltpu.make_async_copy(source.at[lo:hi], target.at[lo:hi], sems.at[3 * i + t])
            )
    for copy in copies:
        copy.start()

    cap, chunks, width, high = packing.cap, packing.chunks, packing.width, packing.rows
    per_ref = row_refs[0].shape[0] // high
    blocks = count * per_ref
    group = 16
    row_at = lax.broadcasted_iota(jnp.int32, (group * cap, group * high), 0)
    place = lax.broadcasted_iota(jnp.int32, (group * cap, group * high), 1)
    source_row = (row_at // cap) * high + row_at % cap
    packed = jnp.concatenate([ref[...] for ref in row_refs], axis=0)
    spare = rows_ref.shape[1] - rows
    for j in range(chunks):
        pick = jnp.where(place == source_row + j * cap, 1.0, 0.0).astype(jnp.bfloat16)
        parts = [
            jnp.dot(
                pick,
                packed[g * group * high : (g + 1) * group * high],
                preferred_element_type=jnp.float32,
            )
            for g in range(blocks // group)
        ]
        if spare:
            parts.append(jnp.zeros((spare, width), jnp.float32))
        part = jnp.concatenate(parts, axis=0)
        rows_ref[j * width : (j + 1) * width, :] = part.T.astype(jnp.bfloat16)

    def down(i, hidden):
        lo, hi = unit_cuts[i]
        term = jnp.dot(hidden, down_ref[lo:hi, :], preferred_element_type=jnp.float32)
        if i == 0:
            total_ref[...] = term
        else:
            total_ref[...] += term

    features = gate_hbm.shape[1]
    middle = features // 256 * 128

    def product(weight_ref, lo, hi):
        return jnp.dot(
            weight_ref[lo:hi, :middle], rows_ref[:middle, :], preferred_element_type=jnp.float32
        ) + jnp.dot(
            weight_ref[lo:hi, middle:], rows_ref[middle:, :], preferred_element_type=jnp.float32
        )

    hidden = None
    for i, (lo, hi) in enumerate(unit_cuts):
        if i > 0:
            copies[3 * i - 1].wait()
        copies[3 * i].wait()
        copies[3 * i + 1].wait()
        gate = product(gate_ref, lo, hi)
        up = product(up_ref, lo, hi)
        if i > 0:
            down(i - 1, hidden)
        hidden = (gate * jax.nn.sigmoid(gate) * up).T[0:rows].astype(jnp.bfloat16)
    copies[-1].wait()
    down(len(unit_cuts) - 1, hidden)
    total = total_ref[...].astype(jnp.bfloat16)

    place = lax.broadcasted_iota(jnp.int32, (group * high, group * cap), 0)
    row_at = lax.broadcasted_iota(jnp.int32, (group * high, group * cap), 1)
    target = (row_at // cap) * high + row_at % cap
    per_group = group // per_ref
    for g in range(blocks // group):
        packed = None
        for j in range(chunks):
            put = jnp.where(place == target + j * cap, 1.0, 0.0).astype(jnp.bfloat16)
            term = jnp.dot(
                put,
                total[g * group * cap : (g + 1) * group * cap, j * width : (j + 1) * width],
                preferred_element_type=jnp.float32,
            )
            packed = term if packed is None else packed + term
        packed = packed.astype(jnp.bfloat16)
        for i in range(per_group):
            out_refs[g * per_group + i][...] = packed[i * per_ref * high : (i + 1) * per_ref * high]


def expert_rows(arrays, w_gate, w_up, w_down, packing, after):
    features, units = w_gate.shape
    rows = len(arrays) * (arrays[0].shape[0] // packing.rows) * packing.cap
    return pl.pallas_call(
        functools.partial(expert_kernel, packing, len(arrays), len(after)),
        out_shape=[jax.ShapeDtypeStruct(arrays[0].shape, jnp.bfloat16)] * len(arrays),
        in_specs=[VMEM] * len(arrays) + [ANY] * (3 + len(after)),
        out_specs=[VMEM] * len(arrays),
        scratch_shapes=[
            pltpu.VMEM((units, features), jnp.bfloat16),
            pltpu.VMEM((units, features), jnp.bfloat16),
            pltpu.VMEM((units, features), jnp.bfloat16),
            pltpu.VMEM((features, -(-rows // 128) * 128), jnp.bfloat16),
            pltpu.VMEM((rows, features), jnp.float32),
            pltpu.SemaphoreType.DMA((3 * len(cuts(units, UNIT_STEP)),)),
        ],
        compiler_params=pltpu.CompilerParams(vmem_limit_bytes=48 << 20),
        cost_estimate=pl.CostEstimate(
            flops=6 * rows * features * units,
            bytes_accessed=6 * features * units,
            transcendentals=rows * units,
        ),
        name="experts",
    )(*arrays, w_gate.T, w_up.T, w_down, *after)


def combine_kernel(packing, spot_ref, weight_ref, *refs):
    block_refs, out_ref = refs[:-1], refs[-1]
    rows = out_ref.shape[0]
    blocks = jnp.concatenate([ref[...] for ref in block_refs], axis=0)
    place = lax.broadcasted_iota(jnp.int32, (rows, blocks.shape[0]), 1).astype(jnp.float32)
    picks = [
        jnp.where(place - float(j * packing.cap) == spot_ref[:, t : t + 1], 1.0, 0.0)
        for t in range(2)
        for j in range(packing.chunks)
    ]
    if rows % 16 == 0:
        table = jnp.concatenate(picks, axis=0).astype(jnp.bfloat16)
        picked = jnp.dot(table, blocks, preferred_element_type=jnp.float32)
        picked = [picked[i * rows : (i + 1) * rows] for i in range(len(picks))]
    else:
        picked = [
            jnp.dot(pick.astype(jnp.bfloat16), blocks, preferred_element_type=jnp.float32)
            for pick in picks
        ]
    for j in range(packing.chunks):
        out_ref[:, j * packing.width : (j + 1) * packing.width] = (
            weight_ref[:, 0:1] * picked[j] + weight_ref[:, 1:2] * picked[packing.chunks + j]
        ).astype(jnp.bfloat16)


def combine(spot, weights, blocks, packing, rows, features):
    return pl.pallas_call(
        functools.partial(combine_kernel, packing),
        out_shape=jax.ShapeDtypeStruct((rows, features), jnp.bfloat16),
        in_specs=[VMEM] * (2 + len(blocks)),
        out_specs=VMEM,
        compiler_params=pltpu.CompilerParams(vmem_limit_bytes=8 << 20),
        name="combine",
    )(spot, weights, *blocks)


def dispatch(blocks, grid):
    first = jnp.concatenate(
        [blocks[0]] + [grid.send(blocks[k], 0, k) for k in range(1, grid.experts)], axis=0
    )
    own = [first] + [grid.send(first, 1, k) for k in range(1, grid.pairs)]
    return own + [grid.send(value, 2, 1) for value in own]


def give_back(results, grid):
    own, other = results[: grid.pairs], results[grid.pairs :]
    sums = []
    for k in list(range(1, grid.pairs)) + [0]:
        sums.append(own[k].astype(jnp.float32) + grid.send(other[k], 2, 1).astype(jnp.float32))
    total = sums[-1]
    for k in range(1, grid.pairs):
        total = total + grid.send(sums[k - 1].astype(jnp.bfloat16), 1, -k).astype(jnp.float32)
    total = total.astype(jnp.bfloat16)
    rows = total.shape[0] // grid.experts
    parts = [total[k * rows : (k + 1) * rows] for k in range(grid.experts)]
    return [parts[0]] + [grid.send(parts[k], 0, -k) for k in range(1, grid.experts)]


def project_kernel(experts, pairs, text_ref, weight_ref, *out_refs):
    devices = experts * pairs * 2
    rows = text_ref.shape[0] // devices
    index = lax.axis_index("dev")
    expert, pair, core = index // (pairs * 2), lax.rem(index // 2, pairs), lax.rem(index, 2)
    place = 0
    for c in (1, 0):
        for p in list(range(1, pairs)) + [0]:
            picked = []
            for e in range(experts):
                owner = lax.rem(expert + e, experts) * pairs + lax.rem(pair + p, pairs)
                start = (owner * 2 + lax.rem(core + c, 2)) * rows
                picked.append(text_ref[pl.ds(pl.multiple_of(start, rows), rows), :])
            out = jnp.dot(
                jnp.concatenate(picked, axis=0),
                weight_ref[...],
                preferred_element_type=jnp.float32,
            )
            out_refs[place][...] = out.astype(out_refs[place].dtype)
            place += 1


def partial_captions(text_hidden, caption_weight, grid):
    groups = grid.pairs * 2
    rows = text_hidden.shape[0] // (grid.experts * groups)
    depth, features = caption_weight.shape
    kinds = [jnp.bfloat16] * grid.pairs + [jnp.float32] * grid.pairs
    if rows % 16 == 0:
        return pl.pallas_call(
            functools.partial(project_kernel, grid.experts, grid.pairs),
            out_shape=[
                jax.ShapeDtypeStruct((rows * grid.experts, features), kind) for kind in kinds
            ],
            in_specs=[VMEM] * 2,
            out_specs=[VMEM] * len(kinds),
            compiler_params=pltpu.CompilerParams(vmem_limit_bytes=16 << 20),
            name="project",
        )(text_hidden, caption_weight)
    text = text_hidden.reshape(grid.experts, grid.pairs, 2, rows, depth)
    text = jnp.roll(text, -grid.expert, axis=0)
    text = jnp.roll(text, -1 - grid.pair, axis=1)
    text = jnp.roll(text, -1 - grid.core, axis=2)
    text = jnp.transpose(text, (2, 1, 0, 3, 4)).reshape(groups, -1, depth)
    return [
        jnp.dot(text[i], caption_weight, preferred_element_type=jnp.float32).astype(kind)
        for i, kind in enumerate(kinds)
    ]


def project(text_hidden, caption_weight, grid):
    rows = text_hidden.shape[0] // (grid.experts * grid.pairs * 2)
    partial = partial_captions(text_hidden, caption_weight, grid)
    sums = [
        partial[grid.pairs + i] + grid.send(partial[i], 2, 1).astype(jnp.float32)
        for i in range(grid.pairs)
    ]
    half = grid.experts // 2
    pieces = [list(range(grid.experts - half, grid.experts)), list(range(grid.experts - half))]
    crossing, terms = [], [None] * grid.experts
    for piece in pieces:
        lo, hi = piece[0] * rows, (piece[-1] + 1) * rows
        crossing.append([sums[k - 1][lo:hi].astype(jnp.bfloat16) for k in range(1, grid.pairs)])
    for piece, sent in zip(pieces, crossing):
        lo, hi = piece[0] * rows, (piece[-1] + 1) * rows
        total = sums[-1][lo:hi]
        for k in range(1, grid.pairs):
            total = total + grid.send(sent[k - 1], 1, k).astype(jnp.float32)
        for i, e in enumerate(piece):
            part = total[i * rows : (i + 1) * rows]
            terms[e] = part if e == 0 else grid.send(part.astype(jnp.bfloat16), 0, e)
    return (terms, crossing[-1])


def local(
    image_rows,
    text_hidden,
    caption_weight,
    mod_scale,
    mod_shift,
    router_weight,
    image_experts,
    caption_experts,
    prompt_lengths,
    w_gate,
    w_up,
    w_down,
):
    devices = lax.axis_size("dev")
    features, experts = router_weight.shape
    grid = Grid(devices, experts)
    image_packing = Packing(image_rows.shape[0] * 3 // 4, features)
    caption_packing = Packing(text_hidden.shape[0] // devices // 2 + 1, features)

    terms, crossing = project(text_hidden, caption_weight, grid)
    image_slot, image_spot = place(image_experts, prompt_lengths, experts, image_packing, False)
    caption_slot, caption_spot = place(
        caption_experts, prompt_lengths, experts, caption_packing, True
    )
    caption_normed, caption_blocks = modulate(
        terms, caption_slot, mod_scale, mod_shift, caption_packing, experts, []
    )
    image_normed, image_blocks = modulate(
        [image_rows], image_slot, mod_scale, mod_shift, image_packing, experts, crossing[:1]
    )

    image_arrays = dispatch(image_blocks, grid)
    caption_arrays = dispatch(caption_blocks, grid)

    def finish(normed, arrays, chosen, spot, packing, after):
        weights = route(normed, chosen, router_weight)
        results = expert_rows(arrays, w_gate, w_up, w_down, packing, after + [weights])
        blocks = give_back(results, grid)
        return combine(spot, weights, blocks, packing, chosen.shape[0], features)

    image_out = finish(
        image_normed, image_arrays, image_experts, image_spot, image_packing, caption_arrays[:1]
    )
    caption_out = finish(
        caption_normed, caption_arrays, caption_experts, caption_spot, caption_packing, []
    )
    return (image_out, caption_out)


def solution(mesh):
    in_specs = (
        P(("groups", "dev"), None),
        P("groups", "dev"),
        P("dev", None),
        P(),
        P(),
        P(),
        P(("groups", "dev"), None),
        P(("groups", "dev"), None),
        P("groups"),
        P(None, "dev"),
        P(None, "dev"),
        P("dev", None),
    )
    out_specs = (P(("groups", "dev"), None), P(("groups", "dev"), None))
    return jax.shard_map(local, mesh=mesh, in_specs=in_specs, out_specs=out_specs, check_vma=False)
```

```python
import functools

import jax
import jax.numpy as jnp
from jax import lax
from jax.experimental import pallas as pl
from jax.experimental.pallas import tpu as pltpu
from jax.sharding import PartitionSpec as P

PLEN = 128
VMEM = pl.BlockSpec(memory_space=pltpu.VMEM)
SMEM = pl.BlockSpec(memory_space=pltpu.SMEM)
ANY = pl.BlockSpec(memory_space=pl.ANY)


class Grid:
    def __init__(self, devices, experts):
        self.experts = experts
        self.pairs = devices // experts // 2
        index = lax.axis_index("dev")
        self.expert = index // (self.pairs * 2)
        self.pair = (index // 2) % self.pairs
        self.core = index % 2

    def send(self, value, axis, step):
        moves = []
        for expert in range(self.experts):
            for pair in range(self.pairs):
                for core in range(2):
                    to = [expert, pair, core]
                    to[axis] = (to[axis] + step) % (self.experts, self.pairs, 2)[axis]
                    moves.append(
                        (
                            (expert * self.pairs + pair) * 2 + core,
                            (to[0] * self.pairs + to[1]) * 2 + to[2],
                        )
                    )
        return lax.ppermute(value, "dev", moves)


class Packing:
    def __init__(self, cap, features):
        best = None
        for chunks in range(1, features // 128 + 1):
            if features % (128 * chunks):
                continue
            rows = -(-cap * chunks // 16) * 16
            cost = rows * (features // chunks)
            if best is None or cost < best[0]:
                best = (cost, chunks, rows)
        _, self.chunks, self.rows = best
        self.cap = cap
        self.width = features // self.chunks


def live(position, lengths_ref):
    prompt = position // PLEN
    length = jnp.zeros_like(position)
    for p in range(lengths_ref.shape[0]):
        length = jnp.where(prompt == p, lengths_ref[p], length)
    return position % PLEN < length


def place_kernel(packings, experts, after, lengths_ref, *refs):
    index = lax.axis_index("dev")
    shift = experts - index // (lax.axis_size("dev") // experts)
    for i, packing in enumerate(packings):
        chosen, out_ref = refs[i][...], refs[len(refs) - len(packings) + i]
        rows = chosen.shape[1]
        relative = lax.rem(chosen + shift, experts)
        expert_at = lax.broadcasted_iota(jnp.int32, (experts, rows), 0)
        routed = (relative[0:1, :] == expert_at) | (relative[1:2, :] == expert_at)
        if i == 1:
            position = index * rows + lax.broadcasted_iota(jnp.int32, (experts, rows), 1)
            routed = routed & live(position, lengths_ref)
        at = [lax.broadcasted_iota(jnp.int32, (rows, rows), d) for d in range(2)]
        before = (at[0] < at[1]).astype(jnp.float32)
        spot = jnp.dot(routed.astype(jnp.float32), before, preferred_element_type=jnp.float32)
        spot = spot + expert_at.astype(jnp.float32) * float(packing.rows)
        spot = jnp.where(routed, spot, -65536.0)
        for t in range(2):
            own = jnp.where(relative[t : t + 1, :] == expert_at, spot, 0.0)
            own = jnp.sum(own, axis=0, keepdims=True)
            for column, value in ((t, own), (2 + t, chosen[t : t + 1, :].astype(jnp.float32))):
                out_ref[:, column : column + 1] = jnp.sum(
                    jnp.where(at[0] == at[1], value, 0.0), axis=1, keepdims=True
                )


def place(chosen, lengths, experts, packings, after):
    return pl.pallas_call(
        functools.partial(place_kernel, packings, experts, len(after)),
        out_shape=[jax.ShapeDtypeStruct((ids.shape[0], 4), jnp.float32) for ids in chosen],
        in_specs=[SMEM] + [VMEM] * len(chosen) + [ANY] * len(after),
        out_specs=[VMEM] * len(chosen),
        compiler_params=pltpu.CompilerParams(vmem_limit_bytes=8 << 20),
        name="place",
    )(lengths, *[ids.T for ids in chosen], *after)


def tie(value, after):
    return pl.pallas_call(
        lambda *refs: None,
        out_shape=jax.ShapeDtypeStruct(value.shape, value.dtype),
        in_specs=[ANY] * (1 + len(after)),
        out_specs=ANY,
        input_output_aliases={0: 0},
        cost_estimate=pl.CostEstimate(flops=0, bytes_accessed=0, transcendentals=0),
        name="tie",
    )(value, *after)


def modulate_kernel(packing, experts, count, spot_ref, scale_ref, shift_ref, *refs):
    normed_ref, packed_refs = refs[-1 - experts], refs[-experts:]
    rows = normed_ref.shape[0]
    values = refs[0][...].astype(jnp.float32)
    for ref in refs[1:count]:
        values = values + ref[...].astype(jnp.float32)
    values = values.astype(jnp.bfloat16).astype(jnp.float32)
    center = values - jnp.mean(values, axis=1, keepdims=True)
    spread = jnp.mean(center * center, axis=1, keepdims=True)
    normed = center * lax.rsqrt(spread + 1e-06) * scale_ref[...][None, :] + shift_ref[...][None, :]
    normed = normed.astype(jnp.bfloat16)
    normed_ref[...] = normed

    place = lax.broadcasted_iota(jnp.int32, (rows, experts * packing.rows), 1).astype(jnp.float32)
    packed = None
    for j in range(packing.chunks):
        at = place - float(j * packing.cap)
        into = jnp.where((at == spot_ref[:, 0:1]) | (at == spot_ref[:, 1:2]), 1.0, 0.0)
        into = into.T.astype(jnp.bfloat16)
        term = jnp.dot(
            into,
            normed[:, j * packing.width : (j + 1) * packing.width],
            preferred_element_type=jnp.float32,
        )
        packed = term if packed is None else packed + term
    for k in range(experts):
        packed_refs[k][...] = packed[k * packing.rows : (k + 1) * packing.rows].astype(
            jnp.bfloat16
        )
def modulate(terms, spot, mod_scale, mod_shift, packing, experts, after):
    rows, features = terms[0].shape
    packed = jax.ShapeDtypeStruct((packing.rows, packing.width), jnp.bfloat16)
    results = pl.pallas_call(
        functools.partial(modulate_kernel, packing, experts, len(terms)),
        out_shape=[jax.ShapeDtypeStruct((rows, features), jnp.bfloat16)] + [packed] * experts,
        in_specs=[VMEM] * (3 + len(terms)) + [ANY] * len(after),
        out_specs=[VMEM] * (1 + experts),
        compiler_params=pltpu.CompilerParams(vmem_limit_bytes=8 << 20),
        name="modulate",
    )(spot, mod_scale, mod_shift, *terms, *after)
    return (results[0], list(results[1:]))


def route_kernel(spot_ref, normed_ref, router_ref, weight_ref):
    normed = normed_ref[...].astype(jnp.float32)
    logits = [
        jnp.sum(normed * router_ref[k : k + 1, :], axis=1, keepdims=True)
        for k in range(router_ref.shape[0])
    ]
    picked = []
    for t in range(2):
        logit = jnp.zeros_like(logits[0])
        for k, value in enumerate(logits):
            logit = jnp.where(spot_ref[:, 2 + t : 3 + t] == float(k), value, logit)
        picked.append(logit)
    weight_ref[:, 0:1] = jax.nn.sigmoid(picked[0] - picked[1])
    weight_ref[:, 1:2] = jax.nn.sigmoid(picked[1] - picked[0])


def route(normed, spot, router_weight):
    return pl.pallas_call(
        route_kernel,
        out_shape=jax.ShapeDtypeStruct((spot.shape[0], 2), jnp.float32),
        in_specs=[VMEM] * 3,
        out_specs=VMEM,
        compiler_params=pltpu.CompilerParams(vmem_limit_bytes=8 << 20),
        name="route",
    )(spot, normed, router_weight.T)


def cuts(units):
    edges = [0, units] if units <= 1024 else [0, 384, 1024, units]
    return list(zip(edges[:-1], edges[1:]))


def expert_kernel(packing, count, after, *refs):
    row_refs = refs[:count]
    gate_hbm, up_hbm, down_hbm = refs[count : count + 3]
    out_refs = refs[count + 3 + after : 2 * count + 3 + after]
    gate_ref, up_ref, down_ref, rows_ref, total_ref, packed_ref, sems = refs[2 * count + 3 + after :]
    rows = total_ref.shape[1]
    units = gate_hbm.shape[0]
    unit_cuts = cuts(units)
    copies = []
    for i, (lo, hi) in enumerate(unit_cuts):
        for t, (source, target) in enumerate(
            ((gate_hbm, gate_ref), (up_hbm, up_ref), (down_hbm, down_ref))
        ):
            copies.append(
                pltpu.make_async_copy(source.at[lo:hi], target.at[lo:hi], sems.at[3 * i + t])
            )
    for copy in copies:
        copy.start()

    cap, chunks, width, high = packing.cap, packing.chunks, packing.width, packing.rows
    per_ref = row_refs[0].shape[0] // high
    blocks = count * per_ref
    lanes = width // 128
    for i, ref in enumerate(row_refs):
        for c in range(lanes):
            packed_ref[c, i * per_ref * high : (i + 1) * per_ref * high, :] = ref[
                :, c * 128 : (c + 1) * 128
            ].astype(jnp.float32)
    spare = rows_ref.shape[1] - rows
    for j in range(chunks):
        for c in range(lanes):
            for slot in range(cap):
                total_ref[j * lanes + c, pl.ds(slot, blocks, stride=cap), :] = packed_ref[
                    c, pl.ds(j * cap + slot, blocks, stride=high), :
                ]
    for c in range(chunks * lanes):
        part = total_ref[c]
        if spare:
            part = jnp.concatenate([part, jnp.zeros((spare, 128), jnp.float32)], axis=0)
        rows_ref[c * 128 : (c + 1) * 128, :] = part.T.astype(jnp.bfloat16)

    def down(i, hidden):
        lo, hi = unit_cuts[i]
        term = jnp.dot(hidden, down_ref[lo:hi, :], preferred_element_type=jnp.float32)
        for c in range(chunks * lanes):
            if i == 0:
                total_ref[c] = term[:, c * 128 : (c + 1) * 128]
            else:
                total_ref[c] += term[:, c * 128 : (c + 1) * 128]

    features = gate_hbm.shape[1]
    middle = features // 256 * 128

    def product(weight_ref, lo, hi):
        return jnp.dot(
            weight_ref[lo:hi, :middle], rows_ref[:middle, :], preferred_element_type=jnp.float32
        ) + jnp.dot(
            weight_ref[lo:hi, middle:], rows_ref[middle:, :], preferred_element_type=jnp.float32
        )

    hidden = None
    for i, (lo, hi) in enumerate(unit_cuts):
        if i > 0:
            copies[3 * i - 1].wait()
        copies[3 * i].wait()
        copies[3 * i + 1].wait()
        gate = product(gate_ref, lo, hi)
        up = product(up_ref, lo, hi)
        if i > 0:
            down(i - 1, hidden)
        hidden = (gate * jax.nn.sigmoid(gate) * up).T[0:rows].astype(jnp.bfloat16)
    copies[-1].wait()
    down(len(unit_cuts) - 1, hidden)

    for c in range(lanes):
        for row in range(chunks * cap, high):
            packed_ref[c, pl.ds(row, blocks, stride=high), :] = jnp.zeros(
                (blocks, 128), jnp.float32
            )
        for j in range(chunks):
            for slot in range(cap):
                packed_ref[c, pl.ds(j * cap + slot, blocks, stride=high), :] = total_ref[
                    j * lanes + c, pl.ds(slot, blocks, stride=cap), :
                ]
    for i, ref in enumerate(out_refs):
        for c in range(lanes):
            ref[:, c * 128 : (c + 1) * 128] = packed_ref[
                c, i * per_ref * high : (i + 1) * per_ref * high, :
            ].astype(jnp.bfloat16)


def expert_rows(arrays, w_gate, w_up, w_down, packing, after):
    features, units = w_gate.shape
    rows = len(arrays) * (arrays[0].shape[0] // packing.rows) * packing.cap
    return pl.pallas_call(
        functools.partial(expert_kernel, packing, len(arrays), len(after)),
        out_shape=[jax.ShapeDtypeStruct(arrays[0].shape, jnp.bfloat16)] * len(arrays),
        in_specs=[VMEM] * len(arrays) + [ANY] * (3 + len(after)),
        out_specs=[VMEM] * len(arrays),
        scratch_shapes=[
            pltpu.VMEM((units, features), jnp.bfloat16),
            pltpu.VMEM((units, features), jnp.bfloat16),
            pltpu.VMEM((units, features), jnp.bfloat16),
            pltpu.VMEM((features, -(-rows // 128) * 128), jnp.bfloat16),
            pltpu.VMEM((features // 128, rows, 128), jnp.float32),
            pltpu.VMEM((packing.width // 128, len(arrays) * arrays[0].shape[0], 128), jnp.float32),
            pltpu.SemaphoreType.DMA((3 * len(cuts(units)),)),
        ],
        compiler_params=pltpu.CompilerParams(vmem_limit_bytes=48 << 20),
        cost_estimate=pl.CostEstimate(
            flops=6 * rows * features * units,
            bytes_accessed=6 * features * units,
            transcendentals=rows * units,
        ),
        name="experts",
    )(*arrays, w_gate.T, w_up.T, w_down, *after)


def combine_kernel(packing, spot_ref, weight_ref, *refs):
    block_refs, out_ref = refs[:-1], refs[-1]
    rows = out_ref.shape[0]
    blocks = jnp.concatenate([ref[...] for ref in block_refs], axis=0)
    place = lax.broadcasted_iota(jnp.int32, (rows, blocks.shape[0]), 1).astype(jnp.float32)
    picks = [
        jnp.where(place - float(j * packing.cap) == spot_ref[:, t : t + 1], 1.0, 0.0)
        for t in range(2)
        for j in range(packing.chunks)
    ]
    if rows % 16 == 0:
        table = jnp.concatenate(picks, axis=0).astype(jnp.bfloat16)
        picked = jnp.dot(table, blocks, preferred_element_type=jnp.float32)
        picked = [picked[i * rows : (i + 1) * rows] for i in range(len(picks))]
    else:
        picked = [
            jnp.dot(pick.astype(jnp.bfloat16), blocks, preferred_element_type=jnp.float32)
            for pick in picks
        ]
    for j in range(packing.chunks):
        out_ref[:, j * packing.width : (j + 1) * packing.width] = (
            weight_ref[:, 0:1] * picked[j] + weight_ref[:, 1:2] * picked[packing.chunks + j]
        ).astype(jnp.bfloat16)


def combine(spot, weights, blocks, packing, rows, features):
    return pl.pallas_call(
        functools.partial(combine_kernel, packing),
        out_shape=jax.ShapeDtypeStruct((rows, features), jnp.bfloat16),
        in_specs=[VMEM] * (2 + len(blocks)),
        out_specs=VMEM,
        compiler_params=pltpu.CompilerParams(vmem_limit_bytes=8 << 20),
        name="combine",
    )(spot, weights, *blocks)


def project_kernel(experts, pairs, text_hbm, weight_hbm, *refs):
    out_refs, (text_ref, weight_ref, sems) = refs[:-3], refs[-3:]
    copies = [
        pltpu.make_async_copy(text_hbm, text_ref, sems.at[0]),
        pltpu.make_async_copy(weight_hbm, weight_ref, sems.at[1]),
    ]
    for copy in copies:
        copy.start()
    rows = text_ref.shape[0] // (experts * pairs * 2)
    index = lax.axis_index("dev")
    expert, pair, core = index // (pairs * 2), lax.rem(index // 2, pairs), lax.rem(index, 2)
    copies[0].wait()
    picked = []
    for c in (1, 0):
        for p in list(range(1, pairs)) + [0]:
            for e in range(experts):
                owner = lax.rem(expert + e, experts) * pairs + lax.rem(pair + p, pairs)
                start = (owner * 2 + lax.rem(core + c, 2)) * rows
                picked.append(text_ref[pl.ds(pl.multiple_of(start, rows), rows), :])
    picked = jnp.concatenate(picked, axis=0)
    copies[1].wait()
    out = jnp.dot(picked, weight_ref[...], preferred_element_type=jnp.float32)
    high = rows * experts
    for i, ref in enumerate(out_refs):
        ref[...] = out[i * high : (i + 1) * high].astype(ref.dtype)


def partial_captions(text_hidden, caption_weight, grid):
    groups = grid.pairs * 2
    rows = text_hidden.shape[0] // (grid.experts * groups)
    depth, features = caption_weight.shape
    kinds = [jnp.bfloat16] * grid.pairs + [jnp.float32] * grid.pairs
    if rows % 16 == 0:
        return pl.pallas_call(
            functools.partial(project_kernel, grid.experts, grid.pairs),
            out_shape=[
                jax.ShapeDtypeStruct((rows * grid.experts, features), kind) for kind in kinds
            ],
            in_specs=[ANY] * 2,
            out_specs=[VMEM] * len(kinds),
            scratch_shapes=[
                pltpu.VMEM(text_hidden.shape, text_hidden.dtype),
                pltpu.VMEM(caption_weight.shape, caption_weight.dtype),
                pltpu.SemaphoreType.DMA((2,)),
            ],
            compiler_params=pltpu.CompilerParams(vmem_limit_bytes=16 << 20),
            name="project",
        )(text_hidden, caption_weight)
    text = text_hidden.reshape(grid.experts, grid.pairs, 2, rows, depth)
    text = jnp.roll(text, -grid.expert, axis=0)
    text = jnp.roll(text, -1 - grid.pair, axis=1)
    text = jnp.roll(text, -1 - grid.core, axis=2)
    text = jnp.transpose(text, (2, 1, 0, 3, 4)).reshape(groups, -1, depth)
    return [
        jnp.dot(text[i], caption_weight, preferred_element_type=jnp.float32).astype(kind)
        for i, kind in enumerate(kinds)
    ]


def local(
    image_rows,
    text_hidden,
    caption_weight,
    mod_scale,
    mod_shift,
    router_weight,
    image_experts,
    caption_experts,
    prompt_lengths,
    w_gate,
    w_up,
    w_down,
):
    devices = lax.axis_size("dev")
    features, experts = router_weight.shape
    grid = Grid(devices, experts)
    pairs = grid.pairs
    wide, narrow = jnp.float32, jnp.bfloat16
    image_packing = Packing(image_rows.shape[0] * 3 // 4, features)
    caption_packing = Packing(text_hidden.shape[0] // devices // 2 + 1, features)

    def split(value, count):
        rows = value.shape[0] // count
        return [value[k * rows : (k + 1) * rows] for k in range(count)]

    def to_experts(blocks):
        return [grid.send(blocks[k], 0, k) for k in range(1, experts)]

    def to_pairs(first):
        return [first] + [grid.send(first, 1, k) for k in range(1, pairs)]

    def over_cores(values):
        return [grid.send(value, 2, 1) for value in values]

    def join_cores(results):
        own, other = results[:pairs], results[pairs:]
        sums = [None] * pairs
        for k in list(range(1, pairs)) + [0]:
            sums[k] = own[k].astype(wide) + grid.send(other[k], 2, 1).astype(wide)
        return sums[0], [value.astype(narrow) for value in sums[1:]]

    def from_pairs(crossing):
        return [grid.send(value, 1, -k) for k, value in enumerate(crossing, 1)]

    def from_experts(kept, received):
        total = kept
        for value in received:
            total = total + value.astype(wide)
        parts = split(total.astype(narrow), experts)
        return [parts[0]] + [grid.send(parts[k], 0, -k) for k in range(1, experts)]

    partial = partial_captions(text_hidden, caption_weight, grid)
    sums = [
        partial[pairs + i] + grid.send(partial[i], 2, 1).astype(wide) for i in range(pairs)
    ]
    crossing = [value.astype(narrow) for value in sums[:-1]]
    total = sums[-1]
    for k in range(1, pairs):
        total = total + grid.send(crossing[k - 1], 1, k).astype(wide)

    image_spot, caption_spot = place(
        [image_experts, caption_experts],
        prompt_lengths,
        experts,
        [image_packing, caption_packing],
        crossing[:1],
    )
    image_normed, blocks = modulate(
        [image_rows], image_spot, mod_scale, mod_shift, image_packing, experts, crossing[:1]
    )
    image_first = [blocks[0]] + to_experts(blocks)

    parts = split(total, experts)
    sent = [part.astype(narrow) for part in parts]
    terms = [parts[0]] + to_experts(sent)

    image_first = jnp.concatenate([tie(image_first[0], sent[1:])] + image_first[1:], axis=0)
    image_own = to_pairs(image_first)
    image_arrays = image_own + over_cores(image_own)

    caption_normed, blocks = modulate(
        terms, caption_spot, mod_scale, mod_shift, caption_packing, experts, []
    )
    caption_first = jnp.concatenate([blocks[0]] + to_experts(blocks), axis=0)
    caption_own = to_pairs(caption_first)

    image_weights = route(image_normed, image_spot, router_weight)
    caption_weights = route(caption_normed, caption_spot, router_weight)
    image_results = expert_rows(
        image_arrays, w_gate, w_up, w_down, image_packing, [caption_first, image_weights]
    )
    caption_own = caption_own[:1] + [tie(value, image_results[:1]) for value in caption_own[1:]]
    image_results = list(image_results[:pairs]) + [
        tie(value, caption_own[1:2]) for value in image_results[pairs:]
    ]
    image_kept, image_crossing = join_cores(image_results)
    caption_results = expert_rows(
        caption_own + over_cores(caption_own),
        w_gate,
        w_up,
        w_down,
        caption_packing,
        image_crossing[:1] + [caption_weights],
    )
    image_received = [
        tie(value, caption_results[:1]) for value in from_pairs(image_crossing)
    ]
    caption_results = list(caption_results[:pairs]) + [
        tie(value, image_received[:1]) for value in caption_results[pairs:]
    ]
    caption_kept, caption_crossing = join_cores(caption_results)
    image_received = [tie(value, caption_crossing[:1]) for value in image_received]
    caption_received = from_pairs(caption_crossing)
    image_blocks = from_experts(image_kept, image_received)
    caption_blocks = from_experts(caption_kept, caption_received)

    rows = image_rows.shape[0]
    image_out = combine(image_spot, image_weights, image_blocks, image_packing, rows, features)
    rows = text_hidden.shape[0] // devices
    caption_out = combine(
        caption_spot, caption_weights, caption_blocks, caption_packing, rows, features
    )
    return (image_out, caption_out)


def solution(mesh):
    in_specs = (
        P(("groups", "dev"), None),
        P("groups", "dev"),
        P("dev", None),
        P(),
        P(),
        P(),
        P(("groups", "dev"), None),
        P(("groups", "dev"), None),
        P("groups"),
        P(None, "dev"),
        P(None, "dev"),
        P("dev", None),
    )
    out_specs = (P(("groups", "dev"), None), P(("groups", "dev"), None))
    return jax.shard_map(local, mesh=mesh, in_specs=in_specs, out_specs=out_specs, check_vma=False)
```

```python
import functools

import jax
import jax.numpy as jnp
from jax import lax
from jax.experimental import pallas as pl
from jax.experimental.pallas import tpu as pltpu
from jax.sharding import PartitionSpec as P

PLEN = 128
VMEM = pl.BlockSpec(memory_space=pltpu.VMEM)
SMEM = pl.BlockSpec(memory_space=pltpu.SMEM)
ANY = pl.BlockSpec(memory_space=pl.ANY)
HBM = pl.BlockSpec(memory_space=pltpu.HBM)


class Grid:
    def __init__(self, devices, experts):
        self.experts = experts
        self.pairs = devices // experts // 2
        index = lax.axis_index("dev")
        self.index = index
        self.expert = index // (self.pairs * 2)
        self.pair = (index // 2) % self.pairs
        self.core = index % 2

    def send(self, value, axis, step):
        moves = []
        for expert in range(self.experts):
            for pair in range(self.pairs):
                for core in range(2):
                    to = [expert, pair, core]
                    to[axis] = (to[axis] + step) % (self.experts, self.pairs, 2)[axis]
                    moves.append(
                        (
                            (expert * self.pairs + pair) * 2 + core,
                            (to[0] * self.pairs + to[1]) * 2 + to[2],
                        )
                    )
        return lax.ppermute(value, "dev", moves)


class Packing:
    def __init__(self, cap, features):
        best = None
        for chunks in range(1, features // 128 + 1):
            if features % (128 * chunks):
                continue
            rows = -(-cap * chunks // 16) * 16
            cost = rows * (features // chunks)
            if best is None or cost < best[0]:
                best = (cost, chunks, rows)
        _, self.chunks, self.rows = best
        self.cap = cap
        self.width = features // self.chunks


def place(chosen, packing, experts, out_ref):
    index = lax.axis_index("dev")
    rows = chosen.shape[1]
    relative = lax.rem(chosen + (experts - index // (lax.axis_size("dev") // experts)), experts)
    expert_at = lax.broadcasted_iota(jnp.int32, (experts, rows), 0)
    routed = (relative[0:1, :] == expert_at) | (relative[1:2, :] == expert_at)
    routed = routed & (chosen[0:1, :] >= 0)
    at = [lax.broadcasted_iota(jnp.int32, (rows, rows), d) for d in range(2)]
    before = (at[0] < at[1]).astype(jnp.float32)
    spot = jnp.dot(routed.astype(jnp.float32), before, preferred_element_type=jnp.float32)
    spot = spot + expert_at.astype(jnp.float32) * float(packing.rows)
    spot = jnp.where(routed, spot, -65536.0)
    for t in range(2):
        own = jnp.where(relative[t : t + 1, :] == expert_at, spot, 0.0)
        own = jnp.sum(own, axis=0, keepdims=True)
        for column, value in ((t, own), (2 + t, chosen[t : t + 1, :].astype(jnp.float32))):
            out_ref[:, column : column + 1] = jnp.sum(
                jnp.where(at[0] == at[1], value, 0.0), axis=1, keepdims=True
            )


def norm_and_pack(values, small_ref, spot_ref, packing, experts, normed_ref, packed_refs):
    rows = values.shape[0]
    center = values - jnp.mean(values, axis=1, keepdims=True)
    spread = jnp.mean(center * center, axis=1, keepdims=True)
    normed = center * lax.rsqrt(spread + 1e-06) * small_ref[0:1, :] + small_ref[1:2, :]
    normed = normed.astype(jnp.bfloat16)
    normed_ref[...] = normed
    place = lax.broadcasted_iota(jnp.int32, (rows, experts * packing.rows), 1).astype(jnp.float32)
    packed = None
    for j in range(packing.chunks):
        at = place - float(j * packing.cap)
        into = jnp.where((at == spot_ref[:, 0:1]) | (at == spot_ref[:, 1:2]), 1.0, 0.0)
        term = jnp.dot(
            into.T.astype(jnp.bfloat16),
            normed[:, j * packing.width : (j + 1) * packing.width],
            preferred_element_type=jnp.float32,
        )
        packed = term if packed is None else packed + term
    for k in range(experts):
        packed_refs[k][...] = packed[k * packing.rows : (k + 1) * packing.rows].astype(
            jnp.bfloat16
        )


def prepare_kernel(packings, experts, after, ids_ref, small_ref, image_ref, *refs):
    image_spot, caption_spot, normed_ref = refs[after : after + 3]
    image_rows, caption_rows = image_spot.shape[0], caption_spot.shape[0]
    place(ids_ref[0:2, 0:image_rows], packings[0], experts, image_spot)
    place(ids_ref[2:4, 0:caption_rows], packings[1], experts, caption_spot)
    norm_and_pack(
        image_ref[...].astype(jnp.float32),
        small_ref,
        image_spot,
        packings[0],
        experts,
        normed_ref,
        refs[after + 3 :],
    )


def prepare(ids, small, image_rows, caption_rows, packings, experts, after):
    rows, features = image_rows.shape
    packed = jax.ShapeDtypeStruct((packings[0].rows, packings[0].width), jnp.bfloat16)
    results = pl.pallas_call(
        functools.partial(prepare_kernel, packings, experts, len(after)),
        out_shape=[
            jax.ShapeDtypeStruct((rows, 4), jnp.float32),
            jax.ShapeDtypeStruct((caption_rows, 4), jnp.float32),
            jax.ShapeDtypeStruct((rows, features), jnp.bfloat16),
        ]
        + [packed] * experts,
        in_specs=[VMEM] * 3 + [ANY] * len(after),
        out_specs=[VMEM] * (3 + experts),
        compiler_params=pltpu.CompilerParams(vmem_limit_bytes=8 << 20),
        name="prepare",
    )(ids, small, image_rows, *after)
    return results[:3], list(results[3:])


def tie_kernel(value_ref, *refs):
    refs[-1][...] = value_ref[...]


def tie(value, after):
    return pl.pallas_call(
        tie_kernel,
        out_shape=jax.ShapeDtypeStruct(value.shape, value.dtype),
        in_specs=[VMEM] + [ANY] * len(after),
        out_specs=VMEM,
        compiler_params=pltpu.CompilerParams(vmem_limit_bytes=8 << 20),
        name="tie",
    )(value, *after)


def modulate_kernel(packing, experts, count, spot_ref, small_ref, *refs):
    values = refs[0][...].astype(jnp.float32)
    for ref in refs[1:count]:
        values = values + ref[...].astype(jnp.float32)
    values = values.astype(jnp.bfloat16).astype(jnp.float32)
    norm_and_pack(
        values, small_ref, spot_ref, packing, experts, refs[count], refs[count + 1 :]
    )


def modulate(terms, spot, small, packing, experts):
    rows, features = terms[0].shape
    packed = jax.ShapeDtypeStruct((packing.rows, packing.width), jnp.bfloat16)
    results = pl.pallas_call(
        functools.partial(modulate_kernel, packing, experts, len(terms)),
        out_shape=[jax.ShapeDtypeStruct((rows, features), jnp.bfloat16)] + [packed] * experts,
        in_specs=[VMEM] * (2 + len(terms)),
        out_specs=[VMEM] * (1 + experts),
        compiler_params=pltpu.CompilerParams(vmem_limit_bytes=8 << 20),
        name="modulate",
    )(spot, small, *terms)
    return (results[0], list(results[1:]))


def route_kernel(spot_ref, normed_ref, small_ref, weight_ref):
    normed = normed_ref[...].astype(jnp.float32)
    logits = [
        jnp.sum(normed * small_ref[2 + k : 3 + k, :], axis=1, keepdims=True)
        for k in range(small_ref.shape[0] - 2)
    ]
    picked = []
    for t in range(2):
        logit = jnp.zeros_like(logits[0])
        for k, value in enumerate(logits):
            logit = jnp.where(spot_ref[:, 2 + t : 3 + t] == float(k), value, logit)
        picked.append(logit)
    weight_ref[:, 0:1] = jax.nn.sigmoid(picked[0] - picked[1])
    weight_ref[:, 1:2] = jax.nn.sigmoid(picked[1] - picked[0])


def route(normed, spot, small):
    return pl.pallas_call(
        route_kernel,
        out_shape=jax.ShapeDtypeStruct((spot.shape[0], 2), jnp.float32),
        in_specs=[VMEM] * 3,
        out_specs=VMEM,
        compiler_params=pltpu.CompilerParams(vmem_limit_bytes=8 << 20),
        name="route",
    )(spot, normed, small)


def cuts(units):
    edges = [0, units] if units <= 1024 else [0, 256, 768, 1280, units]
    return list(zip(edges[:-1], edges[1:]))


def expert_kernel(packing, count, after, *refs):
    row_refs = refs[:count]
    gate_hbm, up_hbm, down_hbm = refs[count : count + 3]
    out_refs = refs[count + 3 + after : 2 * count + 3 + after]
    gate_ref, up_ref, down_ref, rows_ref, total_ref, packed_ref, sems = refs[2 * count + 3 + after :]
    rows = total_ref.shape[1]
    units = gate_hbm.shape[0]
    unit_cuts = cuts(units)
    copies = []
    for i, (lo, hi) in enumerate(unit_cuts):
        for t, (source, target) in enumerate(
            ((gate_hbm, gate_ref), (up_hbm, up_ref), (down_hbm, down_ref))
        ):
            copies.append(
                pltpu.make_async_copy(source.at[lo:hi], target.at[lo:hi], sems.at[3 * i + t])
            )
    for copy in copies[:6]:
        copy.start()

    cap, chunks, width, high = packing.cap, packing.chunks, packing.width, packing.rows
    per_ref = row_refs[0].shape[0] // high
    blocks = count * per_ref
    lanes = width // 128
    for i, ref in enumerate(row_refs):
        for c in range(lanes):
            packed_ref[c, i * per_ref * high : (i + 1) * per_ref * high, :] = ref[
                :, c * 128 : (c + 1) * 128
            ].astype(jnp.float32)
    spare = rows_ref.shape[1] - rows
    for j in range(chunks):
        for c in range(lanes):
            for slot in range(cap):
                total_ref[j * lanes + c, pl.ds(slot, blocks, stride=cap), :] = packed_ref[
                    c, pl.ds(j * cap + slot, blocks, stride=high), :
                ]
    for c in range(chunks * lanes):
        part = total_ref[c]
        if spare:
            part = jnp.concatenate([part, jnp.zeros((spare, 128), jnp.float32)], axis=0)
        rows_ref[c * 128 : (c + 1) * 128, :] = part.T.astype(jnp.bfloat16)

    def down(i, hidden):
        lo, hi = unit_cuts[i]
        term = jnp.dot(hidden, down_ref[lo:hi, :], preferred_element_type=jnp.float32)
        for c in range(chunks * lanes):
            if i == 0:
                total_ref[c] = term[:, c * 128 : (c + 1) * 128]
            else:
                total_ref[c] += term[:, c * 128 : (c + 1) * 128]

    features = gate_hbm.shape[1]
    middle = features // 256 * 128

    def product(weight_ref, lo, hi):
        return jnp.dot(
            weight_ref[lo:hi, :middle], rows_ref[:middle, :], preferred_element_type=jnp.float32
        ) + jnp.dot(
            weight_ref[lo:hi, middle:], rows_ref[middle:, :], preferred_element_type=jnp.float32
        )

    hidden = None
    for i, (lo, hi) in enumerate(unit_cuts):
        if i > 0:
            copies[3 * i - 1].wait()
        copies[3 * i].wait()
        copies[3 * i + 1].wait()
        for copy in copies[3 * (i + 2) : 3 * (i + 3)]:
            copy.start()
        gate = product(gate_ref, lo, hi)
        up = product(up_ref, lo, hi)
        if i > 0:
            down(i - 1, hidden)
        hidden = (gate * jax.nn.sigmoid(gate) * up).T[0:rows].astype(jnp.bfloat16)
    copies[-1].wait()
    down(len(unit_cuts) - 1, hidden)

    for c in range(lanes):
        for row in range(chunks * cap, high):
            packed_ref[c, pl.ds(row, blocks, stride=high), :] = jnp.zeros(
                (blocks, 128), jnp.float32
            )
        for j in range(chunks):
            for slot in range(cap):
                packed_ref[c, pl.ds(j * cap + slot, blocks, stride=high), :] = total_ref[
                    j * lanes + c, pl.ds(slot, blocks, stride=cap), :
                ]
    for i, ref in enumerate(out_refs):
        for c in range(lanes):
            ref[:, c * 128 : (c + 1) * 128] = packed_ref[
                c, i * per_ref * high : (i + 1) * per_ref * high, :
            ].astype(jnp.bfloat16)


def expert_rows(arrays, w_gate, w_up, w_down, packing, after):
    features, units = w_gate.shape
    rows = len(arrays) * (arrays[0].shape[0] // packing.rows) * packing.cap
    return pl.pallas_call(
        functools.partial(expert_kernel, packing, len(arrays), len(after)),
        out_shape=[jax.ShapeDtypeStruct(arrays[0].shape, jnp.bfloat16)] * len(arrays),
        in_specs=[VMEM] * len(arrays) + [HBM] * 3 + [ANY] * len(after),
        out_specs=[VMEM] * len(arrays),
        scratch_shapes=[
            pltpu.VMEM((units, features), jnp.bfloat16),
            pltpu.VMEM((units, features), jnp.bfloat16),
            pltpu.VMEM((units, features), jnp.bfloat16),
            pltpu.VMEM((features, -(-rows // 128) * 128), jnp.bfloat16),
            pltpu.VMEM((features // 128, rows, 128), jnp.float32),
            pltpu.VMEM((packing.width // 128, len(arrays) * arrays[0].shape[0], 128), jnp.float32),
            pltpu.SemaphoreType.DMA((3 * len(cuts(units)),)),
        ],
        compiler_params=pltpu.CompilerParams(vmem_limit_bytes=48 << 20),
        cost_estimate=pl.CostEstimate(
            flops=6 * rows * features * units,
            bytes_accessed=6 * features * units,
            transcendentals=rows * units,
        ),
        name="experts",
    )(*arrays, w_gate.T, w_up.T, w_down, *after)


def combine_kernel(packing, spot_ref, weight_ref, *refs):
    block_refs, out_ref = refs[:-1], refs[-1]
    rows = out_ref.shape[0]
    blocks = jnp.concatenate([ref[...] for ref in block_refs], axis=0)
    place = lax.broadcasted_iota(jnp.int32, (rows, blocks.shape[0]), 1).astype(jnp.float32)
    picks = [
        jnp.where(place - float(j * packing.cap) == spot_ref[:, t : t + 1], 1.0, 0.0)
        for t in range(2)
        for j in range(packing.chunks)
    ]
    if rows % 16 == 0:
        table = jnp.concatenate(picks, axis=0).astype(jnp.bfloat16)
        picked = jnp.dot(table, blocks, preferred_element_type=jnp.float32)
        picked = [picked[i * rows : (i + 1) * rows] for i in range(len(picks))]
    else:
        picked = [
            jnp.dot(pick.astype(jnp.bfloat16), blocks, preferred_element_type=jnp.float32)
            for pick in picks
        ]
    for j in range(packing.chunks):
        out_ref[:, j * packing.width : (j + 1) * packing.width] = (
            weight_ref[:, 0:1] * picked[j] + weight_ref[:, 1:2] * picked[packing.chunks + j]
        ).astype(jnp.bfloat16)


def combine(spot, weights, blocks, packing, rows, features):
    return pl.pallas_call(
        functools.partial(combine_kernel, packing),
        out_shape=jax.ShapeDtypeStruct((rows, features), jnp.bfloat16),
        in_specs=[VMEM] * (2 + len(blocks)),
        out_specs=VMEM,
        compiler_params=pltpu.CompilerParams(vmem_limit_bytes=8 << 20),
        name="combine",
    )(spot, weights, *blocks)


def partial_captions(text_hidden, caption_weight, grid):
    groups = grid.pairs * 2
    rows = text_hidden.shape[0] // (grid.experts * groups)
    depth = caption_weight.shape[0]
    text = text_hidden.reshape(grid.experts, grid.pairs, 2, rows, depth)
    text = jnp.roll(text, -grid.expert, axis=0)
    text = jnp.roll(text, -1 - grid.pair, axis=1)
    text = jnp.roll(text, -1 - grid.core, axis=2)
    text = jnp.transpose(text, (2, 1, 0, 3, 4)).reshape(2, -1, depth)
    other, own = [
        jnp.dot(text[c], caption_weight, preferred_element_type=jnp.float32).astype(kind)
        for c, kind in enumerate((jnp.bfloat16, jnp.float32))
    ]
    high = rows * grid.experts
    return [
        value[k * high : (k + 1) * high] for value in (other, own) for k in range(grid.pairs)
    ]


def local(
    image_rows,
    text_hidden,
    caption_weight,
    mod_scale,
    mod_shift,
    router_weight,
    image_experts,
    caption_experts,
    prompt_lengths,
    w_gate,
    w_up,
    w_down,
):
    devices = lax.axis_size("dev")
    features, experts = router_weight.shape
    grid = Grid(devices, experts)
    pairs = grid.pairs
    wide, narrow = jnp.float32, jnp.bfloat16
    image_packing = Packing(image_rows.shape[0] * 3 // 4, features)
    caption_packing = Packing(text_hidden.shape[0] // devices // 2 + 1, features)

    def split(value, count):
        rows = value.shape[0] // count
        return [value[k * rows : (k + 1) * rows] for k in range(count)]

    def to_experts(blocks):
        return [grid.send(blocks[k], 0, k) for k in range(1, experts)]

    def to_pairs(first):
        return [first] + [grid.send(first, 1, k) for k in range(1, pairs)]

    def over_cores(values):
        return [grid.send(value, 2, 1) for value in values]

    def join_cores(results):
        own, other = results[:pairs], results[pairs:]
        sums = [None] * pairs
        for k in list(range(1, pairs)) + [0]:
            sums[k] = own[k].astype(wide) + grid.send(other[k], 2, 1).astype(wide)
        return sums[0], [value.astype(narrow) for value in sums[1:]]

    def from_pairs(crossing):
        return [grid.send(value, 1, -k) for k, value in enumerate(crossing, 1)]

    def from_experts(kept, received):
        total = kept
        for value in received:
            total = total + value.astype(wide)
        parts = split(total.astype(narrow), experts)
        return [parts[0]] + [grid.send(parts[k], 0, -k) for k in range(1, experts)]

    partial = partial_captions(text_hidden, caption_weight, grid)
    sums = [
        partial[pairs + i] + grid.send(partial[i], 2, 1).astype(wide) for i in range(pairs)
    ]
    crossing = [value.astype(narrow) for value in sums[:-1]]
    received = [grid.send(value, 1, k) for k, value in enumerate(crossing, 1)]

    rows = text_hidden.shape[0] // devices
    position = grid.index * rows + jnp.arange(rows, dtype=jnp.int32)
    prompts = jnp.arange(prompt_lengths.shape[0], dtype=jnp.int32)
    lengths = jnp.where(position[:, None] // PLEN == prompts, prompt_lengths, 0).sum(axis=1)
    ids = jnp.where((position % PLEN < lengths)[None, :], caption_experts.T, -1)
    ids = jnp.pad(ids, ((0, 0), (0, image_rows.shape[0] - rows)))
    ids = jnp.concatenate([image_experts.T, ids], axis=0)
    small = jnp.concatenate([mod_scale[None], mod_shift[None], router_weight.T], axis=0)
    (image_spot, caption_spot, image_normed), blocks = prepare(
        ids, small, image_rows, rows, [image_packing, caption_packing], experts, crossing[:1]
    )
    image_first = [blocks[0]] + to_experts(blocks)

    received[0] = tie(received[0], blocks[1:2])
    total = sums[-1]
    for value in received:
        total = total + value.astype(wide)
    parts = split(total, experts)
    terms = [parts[0]] + to_experts([part.astype(narrow) for part in parts])
    caption_normed, blocks = modulate(terms, caption_spot, small, caption_packing, experts)
    caption_first = jnp.concatenate([blocks[0]] + to_experts(blocks), axis=0)
    caption_own = to_pairs(caption_first)

    image_first = jnp.concatenate([tie(image_first[0], blocks[1:2])] + image_first[1:], axis=0)
    image_own = to_pairs(image_first)
    image_own = image_own[:1] + [tie(value, [caption_first]) for value in image_own[1:]]
    image_arrays = image_own + over_cores(image_own)

    image_weights = route(image_normed, image_spot, small)
    caption_weights = route(caption_normed, caption_spot, small)
    image_results = expert_rows(
        image_arrays, w_gate, w_up, w_down, image_packing, [caption_first, image_weights]
    )
    caption_own = caption_own[:1] + [tie(value, image_results[:1]) for value in caption_own[1:]]
    image_results = list(image_results[:pairs]) + [
        tie(value, caption_own[1:2]) for value in image_results[pairs:]
    ]
    image_kept, image_crossing = join_cores(image_results)
    caption_results = expert_rows(
        caption_own + over_cores(caption_own),
        w_gate,
        w_up,
        w_down,
        caption_packing,
        image_crossing[:1] + [caption_weights],
    )
    image_received = [
        tie(value, caption_results[:1]) for value in from_pairs(image_crossing)
    ]
    caption_results = list(caption_results[:pairs]) + [
        tie(value, image_received[:1]) for value in caption_results[pairs:]
    ]
    caption_kept, caption_crossing = join_cores(caption_results)
    image_received = [tie(value, caption_crossing[:1]) for value in image_received]
    caption_received = from_pairs(caption_crossing)
    image_blocks = from_experts(image_kept, image_received)
    caption_blocks = from_experts(caption_kept, caption_received)

    rows = image_rows.shape[0]
    image_out = combine(image_spot, image_weights, image_blocks, image_packing, rows, features)
    rows = text_hidden.shape[0] // devices
    caption_out = combine(
        caption_spot, caption_weights, caption_blocks, caption_packing, rows, features
    )
    return (image_out, caption_out)


def solution(mesh):
    in_specs = (
        P(("groups", "dev"), None),
        P("groups", "dev"),
        P("dev", None),
        P(),
        P(),
        P(),
        P(("groups", "dev"), None),
        P(("groups", "dev"), None),
        P("groups"),
        P(None, "dev"),
        P(None, "dev"),
        P("dev", None),
    )
    out_specs = (P(("groups", "dev"), None), P(("groups", "dev"), None))
    return jax.shard_map(local, mesh=mesh, in_specs=in_specs, out_specs=out_specs, check_vma=False)
```

```python
import functools

import jax
import jax.numpy as jnp
from jax import lax
from jax.experimental import pallas as pl
from jax.experimental.pallas import tpu as pltpu
from jax.sharding import PartitionSpec as P

PLEN = 128
VMEM = pl.BlockSpec(memory_space=pltpu.VMEM)
SMEM = pl.BlockSpec(memory_space=pltpu.SMEM)
ANY = pl.BlockSpec(memory_space=pl.ANY)
HBM = pl.BlockSpec(memory_space=pltpu.HBM)


class Grid:
    def __init__(self, devices, experts):
        self.experts = experts
        self.pairs = devices // experts // 2
        index = lax.axis_index("dev")
        self.index = index
        self.expert = index // (self.pairs * 2)
        self.pair = (index // 2) % self.pairs
        self.core = index % 2

    def swap(self, value, axis, step):
        moves = []
        for expert in range(self.experts):
            for pair in range(self.pairs):
                for core in range(2):
                    to = [expert, pair, core]
                    to[axis] ^= step
                    moves.append(
                        (
                            (expert * self.pairs + pair) * 2 + core,
                            (to[0] * self.pairs + to[1]) * 2 + to[2],
                        )
                    )
        return lax.ppermute(value, "dev", moves)


class Packing:
    def __init__(self, cap, features):
        best = None
        for chunks in range(1, features // 128 + 1):
            if features % (128 * chunks):
                continue
            rows = -(-cap * chunks // 16) * 16
            cost = rows * (features // chunks)
            if best is None or cost < best[0]:
                best = (cost, chunks, rows)
        _, self.chunks, self.rows = best
        self.cap = cap
        self.width = features // self.chunks


def place(chosen, packing, experts, out_ref):
    index = lax.axis_index("dev")
    rows = chosen.shape[1]
    relative = chosen ^ (index // (lax.axis_size("dev") // experts))
    expert_at = lax.broadcasted_iota(jnp.int32, (experts, rows), 0)
    routed = (relative[0:1, :] == expert_at) | (relative[1:2, :] == expert_at)
    routed = routed & (chosen[0:1, :] >= 0)
    at = [lax.broadcasted_iota(jnp.int32, (rows, rows), d) for d in range(2)]
    before = (at[0] < at[1]).astype(jnp.float32)
    spot = jnp.dot(routed.astype(jnp.float32), before, preferred_element_type=jnp.float32)
    spot = spot + expert_at.astype(jnp.float32) * float(packing.rows)
    for t in range(2):
        own = jnp.where(relative[t : t + 1, :] == expert_at, spot, 0.0)
        own = jnp.sum(own, axis=0, keepdims=True)
        own = jnp.where(chosen[t : t + 1, :] >= 0, own, -65536.0)
        for column, value in ((t, own), (2 + t, chosen[t : t + 1, :].astype(jnp.float32))):
            out_ref[:, column : column + 1] = jnp.sum(
                jnp.where(at[0] == at[1], value, 0.0), axis=1, keepdims=True
            )


def norm_and_pack(values, small_ref, spot_ref, packing, experts, normed_ref, packed_refs):
    rows = values.shape[0]
    center = values - jnp.mean(values, axis=1, keepdims=True)
    spread = jnp.mean(center * center, axis=1, keepdims=True)
    normed = center * lax.rsqrt(spread + 1e-06) * small_ref[0:1, :] + small_ref[1:2, :]
    normed = normed.astype(jnp.bfloat16)
    normed_ref[...] = normed
    place = lax.broadcasted_iota(jnp.int32, (rows, experts * packing.rows), 1).astype(jnp.float32)
    packed = None
    for j in range(packing.chunks):
        at = place - float(j * packing.cap)
        into = jnp.where((at == spot_ref[:, 0:1]) | (at == spot_ref[:, 1:2]), 1.0, 0.0)
        term = jnp.dot(
            into.T.astype(jnp.bfloat16),
            normed[:, j * packing.width : (j + 1) * packing.width],
            preferred_element_type=jnp.float32,
        )
        packed = term if packed is None else packed + term
    for k in range(experts):
        packed_refs[k][...] = packed[k * packing.rows : (k + 1) * packing.rows].astype(
            jnp.bfloat16
        )


def prepare_kernel(packings, experts, after, ids_ref, small_ref, image_ref, *refs):
    image_spot, caption_spot, normed_ref = refs[after : after + 3]
    image_rows, caption_rows = image_spot.shape[0], caption_spot.shape[0]
    place(ids_ref[0:2, 0:image_rows], packings[0], experts, image_spot)
    place(ids_ref[2:4, 0:caption_rows], packings[1], experts, caption_spot)
    norm_and_pack(
        image_ref[...].astype(jnp.float32),
        small_ref,
        image_spot,
        packings[0],
        experts,
        normed_ref,
        refs[after + 3 :],
    )


def prepare(ids, small, image_rows, caption_rows, packings, experts, after):
    rows, features = image_rows.shape
    packed = jax.ShapeDtypeStruct((packings[0].rows, packings[0].width), jnp.bfloat16)
    results = pl.pallas_call(
        functools.partial(prepare_kernel, packings, experts, len(after)),
        out_shape=[
            jax.ShapeDtypeStruct((rows, 4), jnp.float32),
            jax.ShapeDtypeStruct((caption_rows, 4), jnp.float32),
            jax.ShapeDtypeStruct((rows, features), jnp.bfloat16),
        ]
        + [packed] * experts,
        in_specs=[VMEM] * 3 + [ANY] * len(after),
        out_specs=[VMEM] * (3 + experts),
        compiler_params=pltpu.CompilerParams(vmem_limit_bytes=8 << 20),
        name="prepare",
    )(ids, small, image_rows, *after)
    return results[:3], list(results[3:])


def tie_kernel(value_ref, *refs):
    refs[-1][...] = value_ref[...]


def tie(value, after):
    return pl.pallas_call(
        tie_kernel,
        out_shape=jax.ShapeDtypeStruct(value.shape, value.dtype),
        in_specs=[VMEM] + [ANY] * len(after),
        out_specs=VMEM,
        compiler_params=pltpu.CompilerParams(vmem_limit_bytes=8 << 20),
        name="tie",
    )(value, *after)


def modulate_kernel(packing, experts, count, spot_ref, small_ref, *refs):
    values = refs[0][...].astype(jnp.float32)
    for ref in refs[1:count]:
        values = values + ref[...].astype(jnp.float32)
    values = values.astype(jnp.bfloat16).astype(jnp.float32)
    norm_and_pack(
        values, small_ref, spot_ref, packing, experts, refs[count], refs[count + 1 :]
    )


def modulate(terms, spot, small, packing, experts):
    rows, features = terms[0].shape
    packed = jax.ShapeDtypeStruct((packing.rows, packing.width), jnp.bfloat16)
    results = pl.pallas_call(
        functools.partial(modulate_kernel, packing, experts, len(terms)),
        out_shape=[jax.ShapeDtypeStruct((rows, features), jnp.bfloat16)] + [packed] * experts,
        in_specs=[VMEM] * (2 + len(terms)),
        out_specs=[VMEM] * (1 + experts),
        compiler_params=pltpu.CompilerParams(vmem_limit_bytes=8 << 20),
        name="modulate",
    )(spot, small, *terms)
    return (results[0], list(results[1:]))


def route_kernel(spot_ref, normed_ref, small_ref, weight_ref):
    normed = normed_ref[...].astype(jnp.float32)
    logits = [
        jnp.sum(normed * small_ref[2 + k : 3 + k, :], axis=1, keepdims=True)
        for k in range(small_ref.shape[0] - 2)
    ]
    picked = []
    for t in range(2):
        logit = jnp.zeros_like(logits[0])
        for k, value in enumerate(logits):
            logit = jnp.where(spot_ref[:, 2 + t : 3 + t] == float(k), value, logit)
        picked.append(logit)
    weight_ref[:, 0:1] = jax.nn.sigmoid(picked[0] - picked[1])
    weight_ref[:, 1:2] = jax.nn.sigmoid(picked[1] - picked[0])


def route(normed, spot, small):
    return pl.pallas_call(
        route_kernel,
        out_shape=jax.ShapeDtypeStruct((spot.shape[0], 2), jnp.float32),
        in_specs=[VMEM] * 3,
        out_specs=VMEM,
        compiler_params=pltpu.CompilerParams(vmem_limit_bytes=8 << 20),
        name="route",
    )(spot, normed, small)


def cuts(units):
    edges = [0, units] if units <= 1024 else [0, 384, 1152, units]
    return list(zip(edges[:-1], edges[1:]))


def expert_kernel(packing, count, after, *refs):
    row_refs = refs[:count]
    gate_hbm, up_hbm, down_hbm = refs[count : count + 3]
    out_refs = refs[count + 3 + after : 2 * count + 3 + after]
    inner_ref, down_ref, rows_ref, total_ref, packed_ref, sems = refs[2 * count + 3 + after :]
    rows = total_ref.shape[1]
    units = gate_hbm.shape[0]
    unit_cuts = cuts(units)
    copies = []
    for i, (lo, hi) in enumerate(unit_cuts):
        for t, (source, target) in enumerate(
            (
                (gate_hbm, inner_ref.at[2 * lo : lo + hi]),
                (up_hbm, inner_ref.at[lo + hi : 2 * hi]),
                (down_hbm, down_ref.at[lo:hi]),
            )
        ):
            copies.append(pltpu.make_async_copy(source.at[lo:hi], target, sems.at[3 * i + t]))
    for copy in copies[:6]:
        copy.start()

    cap, chunks, width, high = packing.cap, packing.chunks, packing.width, packing.rows
    per_ref = row_refs[0].shape[0] // high
    blocks = count * per_ref
    lanes = width // 128
    for i, ref in enumerate(row_refs):
        for c in range(lanes):
            packed_ref[c, i * per_ref * high : (i + 1) * per_ref * high, :] = ref[
                :, c * 128 : (c + 1) * 128
            ].astype(jnp.float32)
    spare = rows_ref.shape[1] - rows
    for j in range(chunks):
        for c in range(lanes):
            for slot in range(cap):
                total_ref[j * lanes + c, pl.ds(slot, blocks, stride=cap), :] = packed_ref[
                    c, pl.ds(j * cap + slot, blocks, stride=high), :
                ]
    for c in range(chunks * lanes):
        part = total_ref[c]
        if spare:
            part = jnp.concatenate([part, jnp.zeros((spare, 128), jnp.float32)], axis=0)
        rows_ref[c * 128 : (c + 1) * 128, :] = part.T.astype(jnp.bfloat16)

    def down(i, hidden):
        lo, hi = unit_cuts[i]
        term = jnp.dot(hidden, down_ref[lo:hi, :], preferred_element_type=jnp.float32)
        for c in range(chunks * lanes):
            if i == 0:
                total_ref[c] = term[:, c * 128 : (c + 1) * 128]
            else:
                total_ref[c] += term[:, c * 128 : (c + 1) * 128]

    features = gate_hbm.shape[1]
    middle = features // 256 * 128

    def product(lo, hi):
        return jnp.dot(
            inner_ref[lo:hi, :middle], rows_ref[:middle, :], preferred_element_type=jnp.float32
        ) + jnp.dot(
            inner_ref[lo:hi, middle:], rows_ref[middle:, :], preferred_element_type=jnp.float32
        )

    hidden = None
    for i, (lo, hi) in enumerate(unit_cuts):
        if i > 0:
            copies[3 * i - 1].wait()
        copies[3 * i].wait()
        copies[3 * i + 1].wait()
        for copy in copies[3 * (i + 2) : 3 * (i + 3)]:
            copy.start()
        inner = product(2 * lo, 2 * hi)
        gate, up = inner[: hi - lo], inner[hi - lo :]
        if i > 0:
            down(i - 1, hidden)
        hidden = (gate * jax.nn.sigmoid(gate) * up).T[0:rows].astype(jnp.bfloat16)
    copies[-1].wait()
    down(len(unit_cuts) - 1, hidden)

    for c in range(lanes):
        for row in range(chunks * cap, high):
            packed_ref[c, pl.ds(row, blocks, stride=high), :] = jnp.zeros(
                (blocks, 128), jnp.float32
            )
        for j in range(chunks):
            for slot in range(cap):
                packed_ref[c, pl.ds(j * cap + slot, blocks, stride=high), :] = total_ref[
                    j * lanes + c, pl.ds(slot, blocks, stride=cap), :
                ]
    for i, ref in enumerate(out_refs):
        for c in range(lanes):
            ref[:, c * 128 : (c + 1) * 128] = packed_ref[
                c, i * per_ref * high : (i + 1) * per_ref * high, :
            ].astype(jnp.bfloat16)


def expert_rows(arrays, w_gate, w_up, w_down, packing, after):
    features, units = w_gate.shape
    rows = len(arrays) * (arrays[0].shape[0] // packing.rows) * packing.cap
    return pl.pallas_call(
        functools.partial(expert_kernel, packing, len(arrays), len(after)),
        out_shape=[jax.ShapeDtypeStruct(arrays[0].shape, jnp.bfloat16)] * len(arrays),
        in_specs=[VMEM] * len(arrays) + [HBM] * 3 + [ANY] * len(after),
        out_specs=[VMEM] * len(arrays),
        scratch_shapes=[
            pltpu.VMEM((2 * units, features), jnp.bfloat16),
            pltpu.VMEM((units, features), jnp.bfloat16),
            pltpu.VMEM((features, -(-rows // 128) * 128), jnp.bfloat16),
            pltpu.VMEM((features // 128, rows, 128), jnp.float32),
            pltpu.VMEM((packing.width // 128, len(arrays) * arrays[0].shape[0], 128), jnp.float32),
            pltpu.SemaphoreType.DMA((3 * len(cuts(units)),)),
        ],
        compiler_params=pltpu.CompilerParams(vmem_limit_bytes=48 << 20),
        cost_estimate=pl.CostEstimate(
            flops=6 * rows * features * units,
            bytes_accessed=6 * features * units,
            transcendentals=rows * units,
        ),
        name="experts",
    )(*arrays, w_gate.T, w_up.T, w_down, *after)


def combine_kernel(packing, spot_ref, weight_ref, *refs):
    block_refs, out_ref = refs[:-1], refs[-1]
    rows = out_ref.shape[0]
    blocks = jnp.concatenate([ref[...] for ref in block_refs], axis=0)
    place = lax.broadcasted_iota(jnp.int32, (rows, blocks.shape[0]), 1).astype(jnp.float32)
    picks = [
        jnp.where(place - float(j * packing.cap) == spot_ref[:, t : t + 1], 1.0, 0.0)
        for t in range(2)
        for j in range(packing.chunks)
    ]
    if rows % 16 == 0:
        table = jnp.concatenate(picks, axis=0).astype(jnp.bfloat16)
        picked = jnp.dot(table, blocks, preferred_element_type=jnp.float32)
        picked = [picked[i * rows : (i + 1) * rows] for i in range(len(picks))]
    else:
        picked = [
            jnp.dot(pick.astype(jnp.bfloat16), blocks, preferred_element_type=jnp.float32)
            for pick in picks
        ]
    for j in range(packing.chunks):
        out_ref[:, j * packing.width : (j + 1) * packing.width] = (
            weight_ref[:, 0:1] * picked[j] + weight_ref[:, 1:2] * picked[packing.chunks + j]
        ).astype(jnp.bfloat16)


def combine(spot, weights, blocks, packing, rows, features):
    return pl.pallas_call(
        functools.partial(combine_kernel, packing),
        out_shape=jax.ShapeDtypeStruct((rows, features), jnp.bfloat16),
        in_specs=[VMEM] * (2 + len(blocks)),
        out_specs=VMEM,
        compiler_params=pltpu.CompilerParams(vmem_limit_bytes=8 << 20),
        name="combine",
    )(spot, weights, *blocks)


def partial_captions(text_hidden, caption_weight, grid):
    groups = grid.pairs * 2
    rows = text_hidden.shape[0] // (grid.experts * groups)
    text = [
        [
            lax.dynamic_slice_in_dim(
                text_hidden,
                (((grid.expert ^ e) * grid.pairs + (grid.pair ^ p)) * 2 + (grid.core ^ c)) * rows,
                rows,
            )
            for p in list(range(1, grid.pairs)) + [0]
            for e in range(grid.experts)
        ]
        for c in (1, 0)
    ]
    text = [jnp.concatenate(part, axis=0) for part in text]
    other, own = [
        jnp.dot(text[c], caption_weight, preferred_element_type=jnp.float32).astype(kind)
        for c, kind in enumerate((jnp.bfloat16, jnp.float32))
    ]
    high = rows * grid.experts
    return [
        value[k * high : (k + 1) * high] for value in (other, own) for k in range(grid.pairs)
    ]


def local(
    image_rows,
    text_hidden,
    caption_weight,
    mod_scale,
    mod_shift,
    router_weight,
    image_experts,
    caption_experts,
    prompt_lengths,
    w_gate,
    w_up,
    w_down,
):
    devices = lax.axis_size("dev")
    features, experts = router_weight.shape
    grid = Grid(devices, experts)
    pairs = grid.pairs
    wide, narrow = jnp.float32, jnp.bfloat16
    image_packing = Packing(image_rows.shape[0] * 3 // 4, features)
    caption_packing = Packing(text_hidden.shape[0] // devices // 2 + 1, features)

    def split(value, count):
        rows = value.shape[0] // count
        return [value[k * rows : (k + 1) * rows] for k in range(count)]

    def to_experts(blocks):
        return [grid.swap(blocks[k], 0, k) for k in range(1, experts)]

    def to_pairs(first):
        return [first] + [grid.swap(first, 1, k) for k in range(1, pairs)]

    def over_cores(values):
        return [grid.swap(value, 2, 1) for value in values]

    def join_cores(results):
        own, other = results[:pairs], results[pairs:]
        sums = [None] * pairs
        for k in list(range(1, pairs)) + [0]:
            sums[k] = own[k].astype(wide) + grid.swap(other[k], 2, 1).astype(wide)
        return sums[0], [value.astype(narrow) for value in sums[1:]]

    def from_pairs(crossing):
        return [grid.swap(value, 1, k) for k, value in enumerate(crossing, 1)]

    def from_experts(kept, received, high, first=0):
        total = kept
        for value in received:
            total = total + value.astype(wide)
        parts = split(total.astype(narrow), kept.shape[0] // high)
        return [grid.swap(part, 0, k) if k else part for k, part in enumerate(parts, first)]

    partial = partial_captions(text_hidden, caption_weight, grid)
    sums = [
        partial[pairs + i] + grid.swap(partial[i], 2, 1).astype(wide) for i in range(pairs)
    ]
    crossing = [value.astype(narrow) for value in sums[:-1]]
    received = [grid.swap(value, 1, k) for k, value in enumerate(crossing, 1)]

    rows = text_hidden.shape[0] // devices
    position = grid.index * rows + jnp.arange(rows, dtype=jnp.int32)
    prompts = jnp.arange(prompt_lengths.shape[0], dtype=jnp.int32)
    lengths = jnp.where(position[:, None] // PLEN == prompts, prompt_lengths, 0).sum(axis=1)
    ids = jnp.where((position % PLEN < lengths)[None, :], caption_experts.T, -1)
    ids = jnp.pad(ids, ((0, 0), (0, image_rows.shape[0] - rows)))
    ids = jnp.concatenate([image_experts.T, ids], axis=0)
    small = jnp.concatenate([mod_scale[None], mod_shift[None], router_weight.T], axis=0)
    (image_spot, caption_spot, image_normed), blocks = prepare(
        ids, small, image_rows, rows, [image_packing, caption_packing], experts, crossing[:1]
    )
    image_first = [blocks[0]] + to_experts(blocks)

    received[0] = tie(received[0], image_first[1:])
    total = sums[-1]
    for value in received:
        total = total + value.astype(wide)
    parts = split(total, experts)
    sent = [part.astype(narrow) for part in parts]
    terms = [parts[0]] + to_experts(sent)
    image_first = jnp.concatenate([tie(image_first[0], sent[1:])] + image_first[1:], axis=0)
    image_own = to_pairs(image_first)
    caption_normed, blocks = modulate(terms, caption_spot, small, caption_packing, experts)
    caption_first = jnp.concatenate([blocks[0]] + to_experts(blocks), axis=0)
    caption_own = to_pairs(caption_first)
    image_own = image_own[:1] + [tie(value, blocks[1:2]) for value in image_own[1:]]
    image_arrays = image_own + over_cores(image_own)

    image_weights = route(image_normed, image_spot, small)
    caption_weights = route(caption_normed, caption_spot, small)
    image_results = expert_rows(
        image_arrays, w_gate, w_up, w_down, image_packing, [caption_first, image_weights]
    )
    caption_own = caption_own[:1] + [tie(value, image_results[:1]) for value in caption_own[1:]]
    image_results = list(image_results[:pairs]) + [
        tie(value, caption_own[1:2]) for value in image_results[pairs:]
    ]
    image_kept, image_crossing = join_cores(image_results)
    caption_results = expert_rows(
        caption_own + over_cores(caption_own),
        w_gate,
        w_up,
        w_down,
        caption_packing,
        image_crossing[:1] + [caption_weights],
    )
    image_received = [
        tie(value, caption_results[:1]) for value in from_pairs(image_crossing)
    ]
    caption_results = list(caption_results[:pairs]) + [
        tie(value, image_received[:1]) for value in caption_results[pairs:]
    ]
    caption_kept, caption_crossing = join_cores(caption_results)
    image_received = [tie(value, caption_crossing[:1]) for value in image_received]
    image_blocks = from_experts(image_kept, image_received, image_packing.rows)
    caption_blocks = [None] * experts
    high = caption_packing.rows
    for lo, hi in ((experts // 2, experts), (0, experts // 2)):
        strip = slice(lo * high, hi * high)
        caption_blocks[lo:hi] = from_experts(
            caption_kept[strip], from_pairs([value[strip] for value in caption_crossing]), high, lo
        )

    rows = image_rows.shape[0]
    image_out = combine(image_spot, image_weights, image_blocks, image_packing, rows, features)
    rows = text_hidden.shape[0] // devices
    caption_out = combine(
        caption_spot, caption_weights, caption_blocks, caption_packing, rows, features
    )
    return (image_out, caption_out)


def solution(mesh):
    in_specs = (
        P(("groups", "dev"), None),
        P("groups", "dev"),
        P("dev", None),
        P(),
        P(),
        P(),
        P(("groups", "dev"), None),
        P(("groups", "dev"), None),
        P("groups"),
        P(None, "dev"),
        P(None, "dev"),
        P("dev", None),
    )
    out_specs = (P(("groups", "dev"), None), P(("groups", "dev"), None))
    return jax.shard_map(local, mesh=mesh, in_specs=in_specs, out_specs=out_specs, check_vma=False)
```

```python
import functools

import jax
import jax.numpy as jnp
from jax import lax
from jax.experimental import pallas as pl
from jax.experimental.pallas import tpu as pltpu
from jax.sharding import PartitionSpec as P

PLEN = 128
VMEM = pl.BlockSpec(memory_space=pltpu.VMEM)
SMEM = pl.BlockSpec(memory_space=pltpu.SMEM)
ANY = pl.BlockSpec(memory_space=pl.ANY)
HBM = pl.BlockSpec(memory_space=pltpu.HBM)


class Grid:
    def __init__(self, devices, experts):
        self.experts = experts
        self.pairs = devices // experts // 2
        index = lax.axis_index("dev")
        self.index = index
        self.expert = index // (self.pairs * 2)
        self.pair = (index // 2) % self.pairs
        self.core = index % 2

    def swap(self, value, axis, step):
        moves = []
        for expert in range(self.experts):
            for pair in range(self.pairs):
                for core in range(2):
                    to = [expert, pair, core]
                    to[axis] ^= step
                    moves.append(
                        (
                            (expert * self.pairs + pair) * 2 + core,
                            (to[0] * self.pairs + to[1]) * 2 + to[2],
                        )
                    )
        return lax.ppermute(value, "dev", moves)


class Packing:
    def __init__(self, cap, features):
        best = None
        for chunks in range(1, features // 128 + 1):
            if features % (128 * chunks):
                continue
            rows = -(-cap * chunks // 16) * 16
            cost = rows * (features // chunks)
            if best is None or cost < best[0]:
                best = (cost, chunks, rows)
        _, self.chunks, self.rows = best
        self.cap = cap
        self.width = features // self.chunks


def place(chosen, packing, experts, out_ref):
    index = lax.axis_index("dev")
    rows = chosen.shape[1]
    relative = chosen ^ (index // (lax.axis_size("dev") // experts))
    expert_at = lax.broadcasted_iota(jnp.int32, (experts, rows), 0)
    routed = (relative[0:1, :] == expert_at) | (relative[1:2, :] == expert_at)
    routed = routed & (chosen[0:1, :] >= 0)
    at = [lax.broadcasted_iota(jnp.int32, (rows, rows), d) for d in range(2)]
    before = (at[0] < at[1]).astype(jnp.float32)
    spot = jnp.dot(routed.astype(jnp.float32), before, preferred_element_type=jnp.float32)
    spot = spot + expert_at.astype(jnp.float32) * float(packing.rows)
    for t in range(2):
        own = jnp.where(relative[t : t + 1, :] == expert_at, spot, 0.0)
        own = jnp.sum(own, axis=0, keepdims=True)
        own = jnp.where(chosen[t : t + 1, :] >= 0, own, -65536.0)
        for column, value in ((t, own), (2 + t, chosen[t : t + 1, :].astype(jnp.float32))):
            out_ref[:, column : column + 1] = jnp.sum(
                jnp.where(at[0] == at[1], value, 0.0), axis=1, keepdims=True
            )


def norm_and_pack(values, small_ref, spot_ref, packing, experts, normed_ref, packed_refs):
    rows = values.shape[0]
    center = values - jnp.mean(values, axis=1, keepdims=True)
    spread = jnp.mean(center * center, axis=1, keepdims=True)
    normed = center * lax.rsqrt(spread + 1e-06) * small_ref[0:1, :] + small_ref[1:2, :]
    normed = normed.astype(jnp.bfloat16)
    normed_ref[...] = normed
    place = lax.broadcasted_iota(jnp.int32, (rows, experts * packing.rows), 1).astype(jnp.float32)
    packed = None
    for j in range(packing.chunks):
        at = place - float(j * packing.cap)
        into = jnp.where((at == spot_ref[:, 0:1]) | (at == spot_ref[:, 1:2]), 1.0, 0.0)
        term = jnp.dot(
            into.T.astype(jnp.bfloat16),
            normed[:, j * packing.width : (j + 1) * packing.width],
            preferred_element_type=jnp.float32,
        )
        packed = term if packed is None else packed + term
    for k in range(experts):
        packed_refs[k][...] = packed[k * packing.rows : (k + 1) * packing.rows].astype(
            jnp.bfloat16
        )


def prepare_kernel(packings, experts, after, ids_ref, small_ref, image_ref, *refs):
    image_spot, caption_spot, normed_ref = refs[after : after + 3]
    image_rows, caption_rows = image_spot.shape[0], caption_spot.shape[0]
    place(ids_ref[0:2, 0:image_rows], packings[0], experts, image_spot)
    place(ids_ref[2:4, 0:caption_rows], packings[1], experts, caption_spot)
    norm_and_pack(
        image_ref[...].astype(jnp.float32),
        small_ref,
        image_spot,
        packings[0],
        experts,
        normed_ref,
        refs[after + 3 :],
    )


def prepare(ids, small, image_rows, caption_rows, packings, experts, after):
    rows, features = image_rows.shape
    packed = jax.ShapeDtypeStruct((packings[0].rows, packings[0].width), jnp.bfloat16)
    results = pl.pallas_call(
        functools.partial(prepare_kernel, packings, experts, len(after)),
        out_shape=[
            jax.ShapeDtypeStruct((rows, 4), jnp.float32),
            jax.ShapeDtypeStruct((caption_rows, 4), jnp.float32),
            jax.ShapeDtypeStruct((rows, features), jnp.bfloat16),
        ]
        + [packed] * experts,
        in_specs=[VMEM] * 3 + [ANY] * len(after),
        out_specs=[VMEM] * (3 + experts),
        compiler_params=pltpu.CompilerParams(vmem_limit_bytes=8 << 20),
        name="prepare",
    )(ids, small, image_rows, *after)
    return results[:3], list(results[3:])


def tie_kernel(value_ref, *refs):
    refs[-1][...] = value_ref[...]


def tie(value, after):
    return pl.pallas_call(
        tie_kernel,
        out_shape=jax.ShapeDtypeStruct(value.shape, value.dtype),
        in_specs=[VMEM] + [ANY] * len(after),
        out_specs=VMEM,
        compiler_params=pltpu.CompilerParams(vmem_limit_bytes=8 << 20),
        name="tie",
    )(value, *after)


def modulate_kernel(packing, experts, count, spot_ref, small_ref, *refs):
    values = refs[0][...].astype(jnp.float32)
    for ref in refs[1:count]:
        values = values + ref[...].astype(jnp.float32)
    values = values.astype(jnp.bfloat16).astype(jnp.float32)
    norm_and_pack(
        values, small_ref, spot_ref, packing, experts, refs[count], refs[count + 1 :]
    )


def modulate(terms, spot, small, packing, experts):
    rows, features = terms[0].shape
    packed = jax.ShapeDtypeStruct((packing.rows, packing.width), jnp.bfloat16)
    results = pl.pallas_call(
        functools.partial(modulate_kernel, packing, experts, len(terms)),
        out_shape=[jax.ShapeDtypeStruct((rows, features), jnp.bfloat16)] + [packed] * experts,
        in_specs=[VMEM] * (2 + len(terms)),
        out_specs=[VMEM] * (1 + experts),
        compiler_params=pltpu.CompilerParams(vmem_limit_bytes=8 << 20),
        name="modulate",
    )(spot, small, *terms)
    return (results[0], list(results[1:]))


def route_kernel(spot_ref, normed_ref, small_ref, weight_ref):
    normed = normed_ref[...].astype(jnp.float32)
    logits = [
        jnp.sum(normed * small_ref[2 + k : 3 + k, :], axis=1, keepdims=True)
        for k in range(small_ref.shape[0] - 2)
    ]
    picked = []
    for t in range(2):
        logit = jnp.zeros_like(logits[0])
        for k, value in enumerate(logits):
            logit = jnp.where(spot_ref[:, 2 + t : 3 + t] == float(k), value, logit)
        picked.append(logit)
    weight_ref[:, 0:1] = jax.nn.sigmoid(picked[0] - picked[1])
    weight_ref[:, 1:2] = jax.nn.sigmoid(picked[1] - picked[0])


def route(normed, spot, small):
    return pl.pallas_call(
        route_kernel,
        out_shape=jax.ShapeDtypeStruct((spot.shape[0], 2), jnp.float32),
        in_specs=[VMEM] * 3,
        out_specs=VMEM,
        compiler_params=pltpu.CompilerParams(vmem_limit_bytes=8 << 20),
        name="route",
    )(spot, normed, small)


def cuts(units, part, parts):
    first, last = [units * p // parts // 16 * 16 for p in (part, part + 1)]
    edges = [first] + list(range(first + 256, last - 255, 512 if parts == 1 else 320)) + [last]
    return list(zip(edges[:-1], edges[1:]))


def expert_kernel(packing, unit_cuts, count, before, after, *refs):
    row_refs, before_refs = refs[:count], refs[count : count + before]
    gate_hbm, up_hbm, down_hbm = refs[count + before : count + before + 3]
    place = count + before + 3 + after
    out_refs = refs[place : place + count]
    gate_ref, up_ref, down_ref, rows_ref, total_ref, packed_ref, sems = refs[place + count :]
    rows = total_ref.shape[1]
    origin = unit_cuts[0][0]
    copies = []
    for i, (lo, hi) in enumerate(unit_cuts):
        for t, (source, target) in enumerate(
            ((gate_hbm, gate_ref), (up_hbm, up_ref), (down_hbm, down_ref))
        ):
            copies.append(
                pltpu.make_async_copy(
                    source.at[lo:hi], target.at[lo - origin : hi - origin], sems.at[3 * i + t]
                )
            )
    unit_cuts = [(lo - origin, hi - origin) for lo, hi in unit_cuts]
    for copy in copies[:6]:
        copy.start()

    cap, chunks, width, high = packing.cap, packing.chunks, packing.width, packing.rows
    per_ref = row_refs[0].shape[0] // high
    blocks = count * per_ref
    lanes = width // 128
    for i, ref in enumerate(row_refs):
        for c in range(lanes):
            packed_ref[c, i * per_ref * high : (i + 1) * per_ref * high, :] = ref[
                :, c * 128 : (c + 1) * 128
            ].astype(jnp.float32)
    spare = rows_ref.shape[1] - rows
    for j in range(chunks):
        for c in range(lanes):
            for slot in range(cap):
                total_ref[j * lanes + c, pl.ds(slot, blocks, stride=cap), :] = packed_ref[
                    c, pl.ds(j * cap + slot, blocks, stride=high), :
                ]
    for c in range(chunks * lanes):
        part = total_ref[c]
        if spare:
            part = jnp.concatenate([part, jnp.zeros((spare, 128), jnp.float32)], axis=0)
        rows_ref[c * 128 : (c + 1) * 128, :] = part.T.astype(jnp.bfloat16)

    def down(i, hidden):
        lo, hi = unit_cuts[i]
        term = jnp.dot(hidden, down_ref[lo:hi, :], preferred_element_type=jnp.float32)
        for c in range(chunks * lanes):
            if i == 0:
                total_ref[c] = term[:, c * 128 : (c + 1) * 128]
            else:
                total_ref[c] += term[:, c * 128 : (c + 1) * 128]

    features = gate_hbm.shape[1]
    middle = features // 256 * 128

    def product(weight_ref, lo, hi):
        return jnp.dot(
            weight_ref[lo:hi, :middle], rows_ref[:middle, :], preferred_element_type=jnp.float32
        ) + jnp.dot(
            weight_ref[lo:hi, middle:], rows_ref[middle:, :], preferred_element_type=jnp.float32
        )

    hidden = None
    for i, (lo, hi) in enumerate(unit_cuts):
        if i > 0:
            copies[3 * i - 1].wait()
        copies[3 * i].wait()
        copies[3 * i + 1].wait()
        for copy in copies[3 * (i + 2) : 3 * (i + 3)]:
            copy.start()
        gate = product(gate_ref, lo, hi)
        up = product(up_ref, lo, hi)
        if i > 0:
            down(i - 1, hidden)
        hidden = (gate * jax.nn.sigmoid(gate) * up).T[0:rows].astype(jnp.bfloat16)
    copies[-1].wait()
    down(len(unit_cuts) - 1, hidden)

    for c in range(lanes):
        for row in range(chunks * cap, high):
            packed_ref[c, pl.ds(row, blocks, stride=high), :] = jnp.zeros(
                (blocks, 128), jnp.float32
            )
        for j in range(chunks):
            for slot in range(cap):
                packed_ref[c, pl.ds(j * cap + slot, blocks, stride=high), :] = total_ref[
                    j * lanes + c, pl.ds(slot, blocks, stride=cap), :
                ]
    for i, ref in enumerate(out_refs):
        for c in range(lanes):
            columns = slice(c * 128, (c + 1) * 128)
            part = packed_ref[c, i * per_ref * high : (i + 1) * per_ref * high, :]
            if before:
                part = part + before_refs[i][:, columns].astype(jnp.float32)
            ref[:, columns] = part.astype(jnp.bfloat16)


def expert_rows(arrays, w_gate, w_up, w_down, packing, after, part=0, parts=1, before=()):
    features, units = w_gate.shape
    rows = len(arrays) * (arrays[0].shape[0] // packing.rows) * packing.cap
    unit_cuts = cuts(units, part, parts)
    own = unit_cuts[-1][1] - unit_cuts[0][0]
    return pl.pallas_call(
        functools.partial(
            expert_kernel, packing, unit_cuts, len(arrays), len(before), len(after)
        ),
        out_shape=[jax.ShapeDtypeStruct(arrays[0].shape, jnp.bfloat16)] * len(arrays),
        in_specs=[VMEM] * (len(arrays) + len(before)) + [HBM] * 3 + [ANY] * len(after),
        out_specs=[VMEM] * len(arrays),
        scratch_shapes=[
            pltpu.VMEM((own, features), jnp.bfloat16),
            pltpu.VMEM((own, features), jnp.bfloat16),
            pltpu.VMEM((own, features), jnp.bfloat16),
            pltpu.VMEM((features, -(-rows // 128) * 128), jnp.bfloat16),
            pltpu.VMEM((features // 128, rows, 128), jnp.float32),
            pltpu.VMEM((packing.width // 128, len(arrays) * arrays[0].shape[0], 128), jnp.float32),
            pltpu.SemaphoreType.DMA((3 * len(unit_cuts),)),
        ],
        compiler_params=pltpu.CompilerParams(vmem_limit_bytes=48 << 20),
        cost_estimate=pl.CostEstimate(
            flops=6 * rows * features * own,
            bytes_accessed=6 * features * own,
            transcendentals=rows * own,
        ),
        name="experts",
    )(*arrays, *before, w_gate.T, w_up.T, w_down, *after)


def combine_kernel(packing, spot_ref, weight_ref, *refs):
    block_refs, out_ref = refs[:-1], refs[-1]
    rows = out_ref.shape[0]
    blocks = jnp.concatenate([ref[...] for ref in block_refs], axis=0)
    place = lax.broadcasted_iota(jnp.int32, (rows, blocks.shape[0]), 1).astype(jnp.float32)
    picks = [
        jnp.where(place - float(j * packing.cap) == spot_ref[:, t : t + 1], 1.0, 0.0)
        for t in range(2)
        for j in range(packing.chunks)
    ]
    if rows % 16 == 0:
        table = jnp.concatenate(picks, axis=0).astype(jnp.bfloat16)
        picked = jnp.dot(table, blocks, preferred_element_type=jnp.float32)
        picked = [picked[i * rows : (i + 1) * rows] for i in range(len(picks))]
    else:
        picked = [
            jnp.dot(pick.astype(jnp.bfloat16), blocks, preferred_element_type=jnp.float32)
            for pick in picks
        ]
    for j in range(packing.chunks):
        out_ref[:, j * packing.width : (j + 1) * packing.width] = (
            weight_ref[:, 0:1] * picked[j] + weight_ref[:, 1:2] * picked[packing.chunks + j]
        ).astype(jnp.bfloat16)


def combine(spot, weights, blocks, packing, rows, features):
    return pl.pallas_call(
        functools.partial(combine_kernel, packing),
        out_shape=jax.ShapeDtypeStruct((rows, features), jnp.bfloat16),
        in_specs=[VMEM] * (2 + len(blocks)),
        out_specs=VMEM,
        compiler_params=pltpu.CompilerParams(vmem_limit_bytes=8 << 20),
        name="combine",
    )(spot, weights, *blocks)


def partial_captions(text_hidden, caption_weight, grid):
    groups = grid.pairs * 2
    rows = text_hidden.shape[0] // (grid.experts * groups)
    bits = (grid.experts * groups).bit_length() - 1
    text = text_hidden.reshape((2,) * bits + (rows, -1))
    for bit in range(bits):
        text = jnp.roll(text, (grid.index >> (bits - 1 - bit)) & 1, axis=bit)
    text = text.reshape(grid.experts, grid.pairs, 2, rows, -1)
    text = jnp.concatenate([text[:, 1:], text[:, :1]], axis=1)
    text = [
        jnp.transpose(text[:, :, c], (1, 0, 2, 3)).reshape(-1, text_hidden.shape[1])
        for c in (1, 0)
    ]
    other, own = [
        jnp.dot(text[c], caption_weight, preferred_element_type=jnp.float32).astype(kind)
        for c, kind in enumerate((jnp.bfloat16, jnp.float32))
    ]
    high = rows * grid.experts
    return [
        value[k * high : (k + 1) * high] for value in (other, own) for k in range(grid.pairs)
    ]


def local(
    image_rows,
    text_hidden,
    caption_weight,
    mod_scale,
    mod_shift,
    router_weight,
    image_experts,
    caption_experts,
    prompt_lengths,
    w_gate,
    w_up,
    w_down,
):
    devices = lax.axis_size("dev")
    features, experts = router_weight.shape
    grid = Grid(devices, experts)
    pairs = grid.pairs
    wide, narrow = jnp.float32, jnp.bfloat16
    image_packing = Packing(image_rows.shape[0] * 3 // 4, features)
    caption_packing = Packing(text_hidden.shape[0] // devices // 2 + 1, features)

    def split(value, count):
        rows = value.shape[0] // count
        return [value[k * rows : (k + 1) * rows] for k in range(count)]

    def to_experts(blocks):
        return [grid.swap(blocks[k], 0, k) for k in range(1, experts)]

    def to_pairs(first):
        return [first] + [grid.swap(first, 1, k) for k in range(1, pairs)]

    def over_cores(values):
        return [grid.swap(value, 2, 1) for value in values]

    def join_cores(results):
        own, other = results[:pairs], results[pairs:]
        sums = [None] * pairs
        for k in list(range(1, pairs)) + [0]:
            sums[k] = own[k].astype(wide) + grid.swap(other[k], 2, 1).astype(wide)
        return sums[0], [value.astype(narrow) for value in sums[1:]]

    def from_pairs(crossing):
        return [grid.swap(value, 1, k) for k, value in enumerate(crossing, 1)]

    def from_experts(kept, received):
        total = kept
        for value in received:
            total = total + value.astype(wide)
        parts = split(total.astype(narrow), experts)
        return [parts[0]] + [grid.swap(parts[k], 0, k) for k in range(1, experts)]

    partial = partial_captions(text_hidden, caption_weight, grid)
    sums = [
        partial[pairs + i] + grid.swap(partial[i], 2, 1).astype(wide) for i in range(pairs)
    ]
    crossing = [value.astype(narrow) for value in sums[:-1]]
    received = [grid.swap(value, 1, k) for k, value in enumerate(crossing, 1)]

    rows = text_hidden.shape[0] // devices
    position = grid.index * rows + jnp.arange(rows, dtype=jnp.int32)
    prompts = jnp.arange(prompt_lengths.shape[0], dtype=jnp.int32)
    lengths = jnp.where(position[:, None] // PLEN == prompts, prompt_lengths, 0).sum(axis=1)
    ids = jnp.where((position % PLEN < lengths)[None, :], caption_experts.T, -1)
    ids = jnp.pad(ids, ((0, 0), (0, image_rows.shape[0] - rows)))
    ids = jnp.concatenate([image_experts.T, ids], axis=0)
    small = jnp.concatenate([mod_scale[None], mod_shift[None], router_weight.T], axis=0)
    (image_spot, caption_spot, image_normed), blocks = prepare(
        ids, small, image_rows, rows, [image_packing, caption_packing], experts, crossing[:1]
    )
    image_first = [blocks[0]] + to_experts(blocks)

    received[0] = tie(received[0], image_first[1:])
    total = sums[-1]
    for value in received:
        total = total + value.astype(wide)
    parts = split(total, experts)
    sent = [part.astype(narrow) for part in parts]
    terms = [parts[0]] + to_experts(sent)
    image_first = jnp.concatenate([tie(image_first[0], sent[1:])] + image_first[1:], axis=0)
    image_own = to_pairs(image_first)
    image_own = image_own[:1] + [tie(value, terms[1:]) for value in image_own[1:]]
    image_arrays = image_own + over_cores(image_own)
    weights = (w_gate, w_up, w_down)

    caption_normed, blocks = modulate(terms, caption_spot, small, caption_packing, experts)
    image_half = expert_rows(image_arrays, *weights, image_packing, blocks[1:2], 0, 2)
    received = to_experts(blocks)
    caption_first = jnp.concatenate([tie(blocks[0], image_half[:1])] + received, axis=0)
    caption_own = to_pairs(caption_first)

    image_weights = route(image_normed, image_spot, small)
    caption_weights = route(caption_normed, caption_spot, small)
    image_results = expert_rows(
        image_arrays, *weights, image_packing, [caption_first, image_weights], 1, 2, image_half
    )
    caption_own = caption_own[:1] + [tie(value, image_results[:1]) for value in caption_own[1:]]
    image_results = list(image_results[:pairs]) + [
        tie(value, caption_own[1:2]) for value in image_results[pairs:]
    ]
    image_kept, image_crossing = join_cores(image_results)
    caption_results = expert_rows(
        caption_own + over_cores(caption_own),
        *weights,
        caption_packing,
        image_crossing[:1] + [caption_weights],
    )
    image_received = [
        tie(value, caption_results[:1]) for value in from_pairs(image_crossing)
    ]
    caption_results = list(caption_results[:pairs]) + [
        tie(value, image_received[:1]) for value in caption_results[pairs:]
    ]
    caption_kept, caption_crossing = join_cores(caption_results)
    image_received = [tie(value, caption_crossing[:1]) for value in image_received]
    image_blocks = from_experts(image_kept, image_received)
    caption_received = from_pairs(caption_crossing)
    caption_blocks = from_experts(caption_kept, caption_received)

    rows = image_rows.shape[0]
    image_out = combine(image_spot, image_weights, image_blocks, image_packing, rows, features)
    rows = text_hidden.shape[0] // devices
    caption_out = combine(
        caption_spot, caption_weights, caption_blocks, caption_packing, rows, features
    )
    return (image_out, caption_out)


def solution(mesh):
    in_specs = (
        P(("groups", "dev"), None),
        P("groups", "dev"),
        P("dev", None),
        P(),
        P(),
        P(),
        P(("groups", "dev"), None),
        P(("groups", "dev"), None),
        P("groups"),
        P(None, "dev"),
        P(None, "dev"),
        P("dev", None),
    )
    out_specs = (P(("groups", "dev"), None), P(("groups", "dev"), None))
    return jax.shard_map(local, mesh=mesh, in_specs=in_specs, out_specs=out_specs, check_vma=False)
```

```python
import functools

import jax
import jax.numpy as jnp
from jax import lax
from jax.experimental import pallas as pl
from jax.experimental.pallas import tpu as pltpu
from jax.sharding import PartitionSpec as P

PLEN = 128
HINT = 1 << 33
VMEM = pl.BlockSpec(memory_space=pltpu.VMEM)
SMEM = pl.BlockSpec(memory_space=pltpu.SMEM)
ANY = pl.BlockSpec(memory_space=pl.ANY)
HBM = pl.BlockSpec(memory_space=pltpu.HBM)


class Grid:
    def __init__(self, devices, experts):
        self.experts = experts
        self.pairs = devices // experts // 2
        index = lax.axis_index("dev")
        self.index = index
        self.expert = index // (self.pairs * 2)
        self.pair = (index // 2) % self.pairs
        self.core = index % 2

    def swap(self, value, axis, step):
        moves = []
        for expert in range(self.experts):
            for pair in range(self.pairs):
                for core in range(2):
                    to = [expert, pair, core]
                    to[axis] ^= step
                    moves.append(
                        (
                            (expert * self.pairs + pair) * 2 + core,
                            (to[0] * self.pairs + to[1]) * 2 + to[2],
                        )
                    )
        return lax.ppermute(value, "dev", moves)


class Packing:
    def __init__(self, cap, features):
        best = None
        for chunks in range(1, features // 128 + 1):
            if features % (128 * chunks):
                continue
            rows = -(-cap * chunks // 16) * 16
            cost = rows * (features // chunks)
            if best is None or cost < best[0]:
                best = (cost, chunks, rows)
        _, self.chunks, self.rows = best
        self.cap = cap
        self.width = features // self.chunks


def place(chosen, packing, experts, out_ref):
    index = lax.axis_index("dev")
    rows = chosen.shape[1]
    relative = chosen ^ (index // (lax.axis_size("dev") // experts))
    expert_at = lax.broadcasted_iota(jnp.int32, (experts, rows), 0)
    routed = (relative[0:1, :] == expert_at) | (relative[1:2, :] == expert_at)
    routed = routed & (chosen[0:1, :] >= 0)
    at = [lax.broadcasted_iota(jnp.int32, (rows, rows), d) for d in range(2)]
    before = (at[0] < at[1]).astype(jnp.float32)
    spot = jnp.dot(routed.astype(jnp.float32), before, preferred_element_type=jnp.float32)
    spot = spot + expert_at.astype(jnp.float32) * float(packing.rows)
    for t in range(2):
        own = jnp.where(relative[t : t + 1, :] == expert_at, spot, 0.0)
        own = jnp.sum(own, axis=0, keepdims=True)
        own = jnp.where(chosen[t : t + 1, :] >= 0, own, -65536.0)
        for column, value in ((t, own), (2 + t, chosen[t : t + 1, :].astype(jnp.float32))):
            out_ref[:, column : column + 1] = jnp.sum(
                jnp.where(at[0] == at[1], value, 0.0), axis=1, keepdims=True
            )


def norm_and_pack(values, small_ref, spot_ref, packing, experts, normed_ref, packed_refs):
    rows = values.shape[0]
    center = values - jnp.mean(values, axis=1, keepdims=True)
    spread = jnp.mean(center * center, axis=1, keepdims=True)
    normed = center * lax.rsqrt(spread + 1e-06) * small_ref[0:1, :] + small_ref[1:2, :]
    normed = normed.astype(jnp.bfloat16)
    normed_ref[...] = normed
    place = lax.broadcasted_iota(jnp.int32, (rows, experts * packing.rows), 1).astype(jnp.float32)
    packed = None
    for j in range(packing.chunks):
        at = place - float(j * packing.cap)
        into = jnp.where((at == spot_ref[:, 0:1]) | (at == spot_ref[:, 1:2]), 1.0, 0.0)
        term = jnp.dot(
            into.T.astype(jnp.bfloat16),
            normed[:, j * packing.width : (j + 1) * packing.width],
            preferred_element_type=jnp.float32,
        )
        packed = term if packed is None else packed + term
    for k in range(experts):
        packed_refs[k][...] = packed[k * packing.rows : (k + 1) * packing.rows].astype(
            jnp.bfloat16
        )


def prepare_kernel(packings, experts, after, ids_ref, small_ref, image_ref, *refs):
    image_spot, caption_spot, normed_ref = refs[after : after + 3]
    image_rows, caption_rows = image_spot.shape[0], caption_spot.shape[0]
    place(ids_ref[0:2, 0:image_rows], packings[0], experts, image_spot)
    place(ids_ref[2:4, 0:caption_rows], packings[1], experts, caption_spot)
    norm_and_pack(
        image_ref[...].astype(jnp.float32),
        small_ref,
        image_spot,
        packings[0],
        experts,
        normed_ref,
        refs[after + 3 :],
    )


def prepare(ids, small, image_rows, caption_rows, packings, experts, after):
    rows, features = image_rows.shape
    packed = jax.ShapeDtypeStruct((packings[0].rows, packings[0].width), jnp.bfloat16)
    results = pl.pallas_call(
        functools.partial(prepare_kernel, packings, experts, len(after)),
        out_shape=[
            jax.ShapeDtypeStruct((rows, 4), jnp.float32),
            jax.ShapeDtypeStruct((caption_rows, 4), jnp.float32),
            jax.ShapeDtypeStruct((rows, features), jnp.bfloat16),
        ]
        + [packed] * experts,
        in_specs=[VMEM] * 3 + [ANY] * len(after),
        out_specs=[VMEM] * (3 + experts),
        compiler_params=pltpu.CompilerParams(vmem_limit_bytes=8 << 20),
        name="prepare",
    )(ids, small, image_rows, *after)
    return results[:3], list(results[3:])


def tie_kernel(count, *refs):
    value = refs[0][...]
    for ref in refs[1:count]:
        value = value.astype(jnp.float32) + ref[...].astype(jnp.float32)
    refs[-1][...] = value


def tie(values, after, cost=0):
    kind = values[0].dtype if len(values) == 1 else jnp.float32
    return pl.pallas_call(
        functools.partial(tie_kernel, len(values)),
        out_shape=jax.ShapeDtypeStruct(values[0].shape, kind),
        in_specs=[VMEM] * len(values) + [ANY] * len(after),
        out_specs=VMEM,
        compiler_params=pltpu.CompilerParams(vmem_limit_bytes=8 << 20),
        cost_estimate=pl.CostEstimate(flops=cost, bytes_accessed=0, transcendentals=0),
        name="tie",
    )(*values, *after)


def modulate_kernel(packing, experts, count, spot_ref, small_ref, *refs):
    values = refs[0][...].astype(jnp.float32)
    for ref in refs[1:count]:
        values = values + ref[...].astype(jnp.float32)
    values = values.astype(jnp.bfloat16).astype(jnp.float32)
    norm_and_pack(
        values, small_ref, spot_ref, packing, experts, refs[count], refs[count + 1 :]
    )


def modulate(terms, spot, small, packing, experts):
    rows, features = terms[0].shape
    packed = jax.ShapeDtypeStruct((packing.rows, packing.width), jnp.bfloat16)
    results = pl.pallas_call(
        functools.partial(modulate_kernel, packing, experts, len(terms)),
        out_shape=[jax.ShapeDtypeStruct((rows, features), jnp.bfloat16)] + [packed] * experts,
        in_specs=[VMEM] * (2 + len(terms)),
        out_specs=[VMEM] * (1 + experts),
        compiler_params=pltpu.CompilerParams(vmem_limit_bytes=8 << 20),
        cost_estimate=pl.CostEstimate(flops=HINT, bytes_accessed=0, transcendentals=0),
        name="modulate",
    )(spot, small, *terms)
    return (results[0], list(results[1:]))


def route_kernel(spot_ref, normed_ref, small_ref, weight_ref):
    normed = normed_ref[...].astype(jnp.float32)
    logits = [
        jnp.sum(normed * small_ref[2 + k : 3 + k, :], axis=1, keepdims=True)
        for k in range(small_ref.shape[0] - 2)
    ]
    picked = []
    for t in range(2):
        logit = jnp.zeros_like(logits[0])
        for k, value in enumerate(logits):
            logit = jnp.where(spot_ref[:, 2 + t : 3 + t] == float(k), value, logit)
        picked.append(logit)
    weight_ref[:, 0:1] = jax.nn.sigmoid(picked[0] - picked[1])
    weight_ref[:, 1:2] = jax.nn.sigmoid(picked[1] - picked[0])


def route(normed, spot, small):
    return pl.pallas_call(
        route_kernel,
        out_shape=jax.ShapeDtypeStruct((spot.shape[0], 2), jnp.float32),
        in_specs=[VMEM] * 3,
        out_specs=VMEM,
        compiler_params=pltpu.CompilerParams(vmem_limit_bytes=8 << 20),
        name="route",
    )(spot, normed, small)


def cuts(units, part, parts):
    first, last = [units * p // parts // 16 * 16 for p in (part, part + 1)]
    edges = [first] + list(range(first + (256 if parts == 1 else 384), last - 255, 512)) + [last]
    return list(zip(edges[:-1], edges[1:]))


def expert_kernel(packing, unit_cuts, count, before, after, *refs):
    row_refs, before_refs = refs[:count], refs[count : count + before]
    gate_hbm, up_hbm, down_hbm = refs[count + before : count + before + 3]
    place = count + before + 3 + after
    out_refs = refs[place : place + count]
    gate_ref, up_ref, down_ref, rows_ref, total_ref, packed_ref, sems = refs[place + count :]
    rows = total_ref.shape[1]
    origin = unit_cuts[0][0]
    copies = []
    for i, (lo, hi) in enumerate(unit_cuts):
        for t, (source, target) in enumerate(
            ((gate_hbm, gate_ref), (up_hbm, up_ref), (down_hbm, down_ref))
        ):
            copies.append(
                pltpu.make_async_copy(
                    source.at[lo:hi], target.at[lo - origin : hi - origin], sems.at[3 * i + t]
                )
            )
    unit_cuts = [(lo - origin, hi - origin) for lo, hi in unit_cuts]
    for copy in copies[:6]:
        copy.start()

    cap, chunks, width, high = packing.cap, packing.chunks, packing.width, packing.rows
    per_ref = row_refs[0].shape[0] // high
    blocks = count * per_ref
    lanes = width // 128
    for i, ref in enumerate(row_refs):
        for c in range(lanes):
            packed_ref[c, i * per_ref * high : (i + 1) * per_ref * high, :] = ref[
                :, c * 128 : (c + 1) * 128
            ].astype(jnp.float32)
    spare = rows_ref.shape[1] - rows
    for j in range(chunks):
        for c in range(lanes):
            for slot in range(cap):
                total_ref[j * lanes + c, pl.ds(slot, blocks, stride=cap), :] = packed_ref[
                    c, pl.ds(j * cap + slot, blocks, stride=high), :
                ]
    for c in range(chunks * lanes):
        part = total_ref[c]
        if spare:
            part = jnp.concatenate([part, jnp.zeros((spare, 128), jnp.float32)], axis=0)
        rows_ref[c * 128 : (c + 1) * 128, :] = part.T.astype(jnp.bfloat16)

    def down(i, hidden):
        lo, hi = unit_cuts[i]
        term = jnp.dot(hidden, down_ref[lo:hi, :], preferred_element_type=jnp.float32)
        for c in range(chunks * lanes):
            if i == 0:
                total_ref[c] = term[:, c * 128 : (c + 1) * 128]
            else:
                total_ref[c] += term[:, c * 128 : (c + 1) * 128]

    features = gate_hbm.shape[1]
    middle = features // 256 * 128

    def product(weight_ref, lo, hi):
        return jnp.dot(
            weight_ref[lo:hi, :middle], rows_ref[:middle, :], preferred_element_type=jnp.float32
        ) + jnp.dot(
            weight_ref[lo:hi, middle:], rows_ref[middle:, :], preferred_element_type=jnp.float32
        )

    hidden = None
    for i, (lo, hi) in enumerate(unit_cuts):
        if i > 0:
            copies[3 * i - 1].wait()
        copies[3 * i].wait()
        copies[3 * i + 1].wait()
        for copy in copies[3 * (i + 2) : 3 * (i + 3)]:
            copy.start()
        gate = product(gate_ref, lo, hi)
        up = product(up_ref, lo, hi)
        if i > 0:
            down(i - 1, hidden)
        hidden = (gate * jax.nn.sigmoid(gate) * up).T[0:rows].astype(jnp.bfloat16)
    copies[-1].wait()
    down(len(unit_cuts) - 1, hidden)

    for c in range(lanes):
        for row in range(chunks * cap, high):
            packed_ref[c, pl.ds(row, blocks, stride=high), :] = jnp.zeros(
                (blocks, 128), jnp.float32
            )
        for j in range(chunks):
            for slot in range(cap):
                packed_ref[c, pl.ds(j * cap + slot, blocks, stride=high), :] = total_ref[
                    j * lanes + c, pl.ds(slot, blocks, stride=cap), :
                ]
    for i, ref in enumerate(out_refs):
        for c in range(lanes):
            columns = slice(c * 128, (c + 1) * 128)
            part = packed_ref[c, i * per_ref * high : (i + 1) * per_ref * high, :]
            if before:
                part = part + before_refs[i][:, columns].astype(jnp.float32)
            ref[:, columns] = part.astype(jnp.bfloat16)


def expert_rows(arrays, w_gate, w_up, w_down, packing, after, part=0, parts=1, before=()):
    features, units = w_gate.shape
    rows = len(arrays) * (arrays[0].shape[0] // packing.rows) * packing.cap
    unit_cuts = cuts(units, part, parts)
    own = unit_cuts[-1][1] - unit_cuts[0][0]
    return pl.pallas_call(
        functools.partial(
            expert_kernel, packing, unit_cuts, len(arrays), len(before), len(after)
        ),
        out_shape=[jax.ShapeDtypeStruct(arrays[0].shape, jnp.bfloat16)] * len(arrays),
        in_specs=[VMEM] * (len(arrays) + len(before)) + [HBM] * 3 + [ANY] * len(after),
        out_specs=[VMEM] * len(arrays),
        scratch_shapes=[
            pltpu.VMEM((own, features), jnp.bfloat16),
            pltpu.VMEM((own, features), jnp.bfloat16),
            pltpu.VMEM((own, features), jnp.bfloat16),
            pltpu.VMEM((features, -(-rows // 128) * 128), jnp.bfloat16),
            pltpu.VMEM((features // 128, rows, 128), jnp.float32),
            pltpu.VMEM((packing.width // 128, len(arrays) * arrays[0].shape[0], 128), jnp.float32),
            pltpu.SemaphoreType.DMA((3 * len(unit_cuts),)),
        ],
        compiler_params=pltpu.CompilerParams(vmem_limit_bytes=48 << 20),
        cost_estimate=pl.CostEstimate(
            flops=6 * rows * features * own,
            bytes_accessed=6 * features * own,
            transcendentals=rows * own,
        ),
        name="experts",
    )(*arrays, *before, w_gate.T, w_up.T, w_down, *after)


def combine_kernel(packing, spot_ref, weight_ref, *refs):
    block_refs, out_ref = refs[:-1], refs[-1]
    rows = out_ref.shape[0]
    blocks = jnp.concatenate([ref[...] for ref in block_refs], axis=0)
    place = lax.broadcasted_iota(jnp.int32, (rows, blocks.shape[0]), 1).astype(jnp.float32)
    picks = [
        jnp.where(place - float(j * packing.cap) == spot_ref[:, t : t + 1], 1.0, 0.0)
        for t in range(2)
        for j in range(packing.chunks)
    ]
    if rows % 16 == 0:
        table = jnp.concatenate(picks, axis=0).astype(jnp.bfloat16)
        picked = jnp.dot(table, blocks, preferred_element_type=jnp.float32)
        picked = [picked[i * rows : (i + 1) * rows] for i in range(len(picks))]
    else:
        picked = [
            jnp.dot(pick.astype(jnp.bfloat16), blocks, preferred_element_type=jnp.float32)
            for pick in picks
        ]
    for j in range(packing.chunks):
        out_ref[:, j * packing.width : (j + 1) * packing.width] = (
            weight_ref[:, 0:1] * picked[j] + weight_ref[:, 1:2] * picked[packing.chunks + j]
        ).astype(jnp.bfloat16)


def combine(spot, weights, blocks, packing, rows, features):
    return pl.pallas_call(
        functools.partial(combine_kernel, packing),
        out_shape=jax.ShapeDtypeStruct((rows, features), jnp.bfloat16),
        in_specs=[VMEM] * (2 + len(blocks)),
        out_specs=VMEM,
        compiler_params=pltpu.CompilerParams(vmem_limit_bytes=8 << 20),
        name="combine",
    )(spot, weights, *blocks)


def partial_captions(text_hidden, caption_weight, grid):
    groups = grid.pairs * 2
    rows = text_hidden.shape[0] // (grid.experts * groups)
    bits = (grid.experts * groups).bit_length() - 1
    text = text_hidden.reshape((2,) * bits + (rows, -1))
    for bit in range(bits):
        text = jnp.roll(text, (grid.index >> (bits - 1 - bit)) & 1, axis=bit)
    text = text.reshape(grid.experts, grid.pairs, 2, rows, -1)
    text = jnp.concatenate([text[:, 1:], text[:, :1]], axis=1)
    text = [
        jnp.transpose(text[:, :, c], (1, 0, 2, 3)).reshape(-1, text_hidden.shape[1])
        for c in (1, 0)
    ]
    other, own = [
        jnp.dot(text[c], caption_weight, preferred_element_type=jnp.float32).astype(kind)
        for c, kind in enumerate((jnp.bfloat16, jnp.float32))
    ]
    high = rows * grid.experts
    return [
        value[k * high : (k + 1) * high] for value in (other, own) for k in range(grid.pairs)
    ]


def local(
    image_rows,
    text_hidden,
    caption_weight,
    mod_scale,
    mod_shift,
    router_weight,
    image_experts,
    caption_experts,
    prompt_lengths,
    w_gate,
    w_up,
    w_down,
):
    devices = lax.axis_size("dev")
    features, experts = router_weight.shape
    grid = Grid(devices, experts)
    pairs = grid.pairs
    wide, narrow = jnp.float32, jnp.bfloat16
    image_packing = Packing(image_rows.shape[0] * 3 // 4, features)
    caption_packing = Packing(text_hidden.shape[0] // devices // 2 + 1, features)

    def split(value, count):
        rows = value.shape[0] // count
        return [value[k * rows : (k + 1) * rows] for k in range(count)]

    def to_experts(blocks):
        return [grid.swap(blocks[k], 0, k) for k in range(1, experts)]

    def to_pairs(first):
        return [first] + [grid.swap(first, 1, k) for k in range(1, pairs)]

    def over_cores(values):
        return [grid.swap(value, 2, 1) for value in values]

    def join_cores(results):
        own, other = results[:pairs], results[pairs:]
        sums = [None] * pairs
        for k in list(range(1, pairs)) + [0]:
            sums[k] = own[k].astype(wide) + grid.swap(other[k], 2, 1).astype(wide)
        return sums[0], [value.astype(narrow) for value in sums[1:]]

    def from_pairs(crossing):
        return [grid.swap(value, 1, k) for k, value in enumerate(crossing, 1)]

    def from_experts(kept, received):
        total = kept
        for value in received:
            total = total + value.astype(wide)
        parts = split(total.astype(narrow), experts)
        return [parts[0]] + [grid.swap(parts[k], 0, k) for k in range(1, experts)]

    partial = partial_captions(text_hidden, caption_weight, grid)
    sums = [
        partial[pairs + i] + grid.swap(partial[i], 2, 1).astype(wide) for i in range(pairs)
    ]
    crossing = [value.astype(narrow) for value in sums[:-1]]
    received = [grid.swap(value, 1, k) for k, value in enumerate(crossing, 1)]

    rows = text_hidden.shape[0] // devices
    position = grid.index * rows + jnp.arange(rows, dtype=jnp.int32)
    prompts = jnp.arange(prompt_lengths.shape[0], dtype=jnp.int32)
    lengths = jnp.where(position[:, None] // PLEN == prompts, prompt_lengths, 0).sum(axis=1)
    ids = jnp.where((position % PLEN < lengths)[None, :], caption_experts.T, -1)
    ids = jnp.pad(ids, ((0, 0), (0, image_rows.shape[0] - rows)))
    ids = jnp.concatenate([image_experts.T, ids], axis=0)
    small = jnp.concatenate([mod_scale[None], mod_shift[None], router_weight.T], axis=0)
    (image_spot, caption_spot, image_normed), blocks = prepare(
        ids, small, image_rows, rows, [image_packing, caption_packing], experts, crossing[:1]
    )
    image_first = [blocks[0]] + to_experts(blocks)

    received[0] = tie([received[0]], blocks[1:2], HINT)
    total = sums[-1]
    for value in received:
        total = total + value.astype(wide)
    parts = split(total, experts)
    sent = [part.astype(narrow) for part in parts[1:]]
    terms = parts[:1] + [grid.swap(part, 0, k) for k, part in enumerate(sent, 1)]
    image_first = jnp.concatenate([tie([image_first[0]], sent)] + image_first[1:], axis=0)
    image_own = to_pairs(image_first)
    weights = (w_gate, w_up, w_down)

    caption_normed, blocks = modulate(terms, caption_spot, small, caption_packing, experts)
    received = to_experts(blocks)
    image_own = image_own[:1] + [tie([value], blocks[1:2]) for value in image_own[1:]]
    image_arrays = image_own + over_cores(image_own)
    caption_first = jnp.concatenate([blocks[0]] + received, axis=0)
    caption_own = to_pairs(caption_first)

    image_weights = route(image_normed, image_spot, small)
    caption_weights = route(caption_normed, caption_spot, small)
    image_results = expert_rows(
        image_arrays, *weights, image_packing, [caption_first, image_weights]
    )
    caption_own = caption_own[:1] + [tie([value], image_results[:1]) for value in caption_own[1:]]
    image_results = list(image_results[:pairs]) + [
        tie([value], caption_own[1:2]) for value in image_results[pairs:]
    ]
    image_kept, image_crossing = join_cores(image_results)
    caption_results = expert_rows(
        caption_own + over_cores(caption_own),
        *weights,
        caption_packing,
        image_crossing[:1] + [caption_weights],
    )
    image_received = [
        tie([value], caption_results[:1]) for value in from_pairs(image_crossing)
    ]
    caption_results = list(caption_results[:pairs]) + [
        tie([value], image_received[:1]) for value in caption_results[pairs:]
    ]
    caption_kept, caption_crossing = join_cores(caption_results)
    image_received = [tie([value], caption_crossing[:1]) for value in image_received]
    image_blocks = from_experts(image_kept, image_received)
    caption_received = from_pairs(caption_crossing)
    caption_blocks = from_experts(caption_kept, caption_received)

    rows = image_rows.shape[0]
    image_out = combine(image_spot, image_weights, image_blocks, image_packing, rows, features)
    rows = text_hidden.shape[0] // devices
    caption_out = combine(
        caption_spot, caption_weights, caption_blocks, caption_packing, rows, features
    )
    return (image_out, caption_out)


def solution(mesh):
    in_specs = (
        P(("groups", "dev"), None),
        P("groups", "dev"),
        P("dev", None),
        P(),
        P(),
        P(),
        P(("groups", "dev"), None),
        P(("groups", "dev"), None),
        P("groups"),
        P(None, "dev"),
        P(None, "dev"),
        P("dev", None),
    )
    out_specs = (P(("groups", "dev"), None), P(("groups", "dev"), None))
    return jax.shard_map(local, mesh=mesh, in_specs=in_specs, out_specs=out_specs, check_vma=False)
```

```python
import functools

import jax
import jax.numpy as jnp
from jax import lax
from jax.experimental import pallas as pl
from jax.experimental.pallas import tpu as pltpu
from jax.sharding import PartitionSpec as P

PLEN = 128
HINT = 1 << 33
VMEM = pl.BlockSpec(memory_space=pltpu.VMEM)
SMEM = pl.BlockSpec(memory_space=pltpu.SMEM)
ANY = pl.BlockSpec(memory_space=pl.ANY)
HBM = pl.BlockSpec(memory_space=pltpu.HBM)


class Grid:
    def __init__(self, devices, experts):
        self.experts = experts
        self.pairs = devices // experts // 2
        index = lax.axis_index("dev")
        self.index = index
        self.expert = index // (self.pairs * 2)
        self.pair = (index // 2) % self.pairs
        self.core = index % 2

    def swap(self, value, axis, step):
        moves = []
        for expert in range(self.experts):
            for pair in range(self.pairs):
                for core in range(2):
                    to = [expert, pair, core]
                    to[axis] ^= step
                    moves.append(
                        (
                            (expert * self.pairs + pair) * 2 + core,
                            (to[0] * self.pairs + to[1]) * 2 + to[2],
                        )
                    )
        return lax.ppermute(value, "dev", moves)


class Packing:
    def __init__(self, cap, features):
        best = None
        for chunks in range(1, features // 128 + 1):
            if features % (128 * chunks):
                continue
            rows = -(-cap * chunks // 16) * 16
            cost = rows * (features // chunks)
            if best is None or cost < best[0]:
                best = (cost, chunks, rows)
        _, self.chunks, self.rows = best
        self.cap = cap
        self.width = features // self.chunks


def place(chosen, packing, experts, out_ref):
    index = lax.axis_index("dev")
    rows = chosen.shape[1]
    relative = chosen ^ (index // (lax.axis_size("dev") // experts))
    expert_at = lax.broadcasted_iota(jnp.int32, (experts, rows), 0)
    routed = (relative[0:1, :] == expert_at) | (relative[1:2, :] == expert_at)
    routed = routed & (chosen[0:1, :] >= 0)
    at = [lax.broadcasted_iota(jnp.int32, (rows, rows), d) for d in range(2)]
    before = (at[0] < at[1]).astype(jnp.float32)
    spot = jnp.dot(routed.astype(jnp.float32), before, preferred_element_type=jnp.float32)
    spot = spot + expert_at.astype(jnp.float32) * float(packing.rows)
    for t in range(2):
        own = jnp.where(relative[t : t + 1, :] == expert_at, spot, 0.0)
        own = jnp.sum(own, axis=0, keepdims=True)
        own = jnp.where(chosen[t : t + 1, :] >= 0, own, -65536.0)
        for column, value in ((t, own), (2 + t, chosen[t : t + 1, :].astype(jnp.float32))):
            out_ref[:, column : column + 1] = jnp.sum(
                jnp.where(at[0] == at[1], value, 0.0), axis=1, keepdims=True
            )


def norm_and_pack(values, small_ref, spot_ref, packing, experts, normed_ref, packed_refs):
    rows = values.shape[0]
    center = values - jnp.mean(values, axis=1, keepdims=True)
    spread = jnp.mean(center * center, axis=1, keepdims=True)
    normed = center * lax.rsqrt(spread + 1e-06) * small_ref[0:1, :] + small_ref[1:2, :]
    normed = normed.astype(jnp.bfloat16)
    normed_ref[...] = normed
    place = lax.broadcasted_iota(jnp.int32, (rows, experts * packing.rows), 1).astype(jnp.float32)
    packed = None
    for j in range(packing.chunks):
        at = place - float(j * packing.cap)
        into = jnp.where((at == spot_ref[:, 0:1]) | (at == spot_ref[:, 1:2]), 1.0, 0.0)
        term = jnp.dot(
            into.T.astype(jnp.bfloat16),
            normed[:, j * packing.width : (j + 1) * packing.width],
            preferred_element_type=jnp.float32,
        )
        packed = term if packed is None else packed + term
    for k in range(experts):
        packed_refs[k][...] = packed[k * packing.rows : (k + 1) * packing.rows].astype(
            jnp.bfloat16
        )


def prepare_kernel(packings, experts, after, ids_ref, small_ref, image_ref, *refs):
    image_spot, caption_spot, normed_ref = refs[after : after + 3]
    image_rows, caption_rows = image_spot.shape[0], caption_spot.shape[0]
    place(ids_ref[0:2, 0:image_rows], packings[0], experts, image_spot)
    place(ids_ref[2:4, 0:caption_rows], packings[1], experts, caption_spot)
    norm_and_pack(
        image_ref[...].astype(jnp.float32),
        small_ref,
        image_spot,
        packings[0],
        experts,
        normed_ref,
        refs[after + 3 :],
    )


def prepare(ids, small, image_rows, caption_rows, packings, experts, after):
    rows, features = image_rows.shape
    packed = jax.ShapeDtypeStruct((packings[0].rows, packings[0].width), jnp.bfloat16)
    results = pl.pallas_call(
        functools.partial(prepare_kernel, packings, experts, len(after)),
        out_shape=[
            jax.ShapeDtypeStruct((rows, 4), jnp.float32),
            jax.ShapeDtypeStruct((caption_rows, 4), jnp.float32),
            jax.ShapeDtypeStruct((rows, features), jnp.bfloat16),
        ]
        + [packed] * experts,
        in_specs=[VMEM] * 3 + [ANY] * len(after),
        out_specs=[VMEM] * (3 + experts),
        compiler_params=pltpu.CompilerParams(vmem_limit_bytes=8 << 20),
        name="prepare",
    )(ids, small, image_rows, *after)
    return results[:3], list(results[3:])


def tie_kernel(count, *refs):
    value = refs[0][...]
    for ref in refs[1:count]:
        value = value.astype(jnp.float32) + ref[...].astype(jnp.float32)
    refs[-1][...] = value


def tie(values, after, cost=0):
    kind = values[0].dtype if len(values) == 1 else jnp.float32
    return pl.pallas_call(
        functools.partial(tie_kernel, len(values)),
        out_shape=jax.ShapeDtypeStruct(values[0].shape, kind),
        in_specs=[VMEM] * len(values) + [ANY] * len(after),
        out_specs=VMEM,
        compiler_params=pltpu.CompilerParams(vmem_limit_bytes=8 << 20),
        cost_estimate=pl.CostEstimate(flops=cost, bytes_accessed=0, transcendentals=0),
        name="tie",
    )(*values, *after)


def modulate_kernel(packing, experts, count, spot_ref, small_ref, *refs):
    values = refs[0][...].astype(jnp.float32)
    for ref in refs[1:count]:
        values = values + ref[...].astype(jnp.float32)
    values = values.astype(jnp.bfloat16).astype(jnp.float32)
    norm_and_pack(
        values, small_ref, spot_ref, packing, experts, refs[count], refs[count + 1 :]
    )


def modulate(terms, spot, small, packing, experts):
    rows, features = terms[0].shape
    packed = jax.ShapeDtypeStruct((packing.rows, packing.width), jnp.bfloat16)
    results = pl.pallas_call(
        functools.partial(modulate_kernel, packing, experts, len(terms)),
        out_shape=[jax.ShapeDtypeStruct((rows, features), jnp.bfloat16)] + [packed] * experts,
        in_specs=[VMEM] * (2 + len(terms)),
        out_specs=[VMEM] * (1 + experts),
        compiler_params=pltpu.CompilerParams(vmem_limit_bytes=8 << 20),
        cost_estimate=pl.CostEstimate(flops=HINT, bytes_accessed=0, transcendentals=0),
        name="modulate",
    )(spot, small, *terms)
    return (results[0], list(results[1:]))


def route_kernel(spot_ref, normed_ref, small_ref, weight_ref):
    normed = normed_ref[...].astype(jnp.float32)
    logits = [
        jnp.sum(normed * small_ref[2 + k : 3 + k, :], axis=1, keepdims=True)
        for k in range(small_ref.shape[0] - 2)
    ]
    picked = []
    for t in range(2):
        logit = jnp.zeros_like(logits[0])
        for k, value in enumerate(logits):
            logit = jnp.where(spot_ref[:, 2 + t : 3 + t] == float(k), value, logit)
        picked.append(logit)
    weight_ref[:, 0:1] = jax.nn.sigmoid(picked[0] - picked[1])
    weight_ref[:, 1:2] = jax.nn.sigmoid(picked[1] - picked[0])


def route(normed, spot, small):
    return pl.pallas_call(
        route_kernel,
        out_shape=jax.ShapeDtypeStruct((spot.shape[0], 2), jnp.float32),
        in_specs=[VMEM] * 3,
        out_specs=VMEM,
        compiler_params=pltpu.CompilerParams(vmem_limit_bytes=8 << 20),
        name="route",
    )(spot, normed, small)


def cuts(units):
    edges = [0] + list(range(256, units - 255, 512)) + [units]
    return list(zip(edges[:-1], edges[1:]))


def expert_kernel(packing, unit_cuts, count, after, *refs):
    row_refs = refs[:count]
    gate_hbm, up_hbm, down_hbm = refs[count : count + 3]
    place = count + 3 + after
    out_refs = refs[place : place + count]
    gate_ref, up_ref, down_ref, rows_ref, total_ref, packed_ref, sems = refs[place + count :]
    copies = []
    for i, (lo, hi) in enumerate(unit_cuts):
        for t, (source, target) in enumerate(
            ((gate_hbm, gate_ref), (up_hbm, up_ref), (down_hbm, down_ref))
        ):
            copies.append(
                pltpu.make_async_copy(
                    source.at[lo:hi], target.at[lo:hi], sems.at[3 * i + t]
                )
            )
    for copy in copies[:6]:
        copy.start()

    cap, chunks, width, high = packing.cap, packing.chunks, packing.width, packing.rows
    per_ref = row_refs[0].shape[0] // high
    blocks = count * per_ref
    rows = blocks * cap
    lanes = width // 128
    for i, ref in enumerate(row_refs):
        for c in range(lanes):
            packed_ref[c, i * per_ref * high : (i + 1) * per_ref * high, :] = ref[
                :, c * 128 : (c + 1) * 128
            ].astype(jnp.float32)
    spare = rows_ref.shape[1] - rows
    for j in range(chunks):
        for c in range(lanes):
            for slot in range(cap):
                total_ref[j * lanes + c, pl.ds(slot, blocks, stride=cap), :] = packed_ref[
                    c, pl.ds(j * cap + slot, blocks, stride=high), :
                ]
    for c in range(chunks * lanes):
        part = total_ref[c, 0:rows, :]
        if spare:
            part = jnp.concatenate([part, jnp.zeros((spare, 128), jnp.float32)], axis=0)
        rows_ref[c * 128 : (c + 1) * 128, :] = part.astype(jnp.bfloat16).T

    def down(i, hidden):
        lo, hi = unit_cuts[i]
        term = jnp.dot(hidden, down_ref[lo:hi, :], preferred_element_type=jnp.float32)
        for c in range(chunks * lanes):
            if i == 0:
                total_ref[c, 0:rows, :] = term[:, c * 128 : (c + 1) * 128]
            else:
                total_ref[c, 0:rows, :] += term[:, c * 128 : (c + 1) * 128]

    features = gate_hbm.shape[1]
    middle = features // 256 * 128

    def product(weight_ref, lo, hi):
        return jnp.dot(
            weight_ref[lo:hi, :middle], rows_ref[:middle, :], preferred_element_type=jnp.float32
        ) + jnp.dot(
            weight_ref[lo:hi, middle:], rows_ref[middle:, :], preferred_element_type=jnp.float32
        )

    def gated(gate, up):
        return (gate * jax.nn.sigmoid(gate) * up).astype(jnp.bfloat16).T[0:rows]

    inner = None
    for i, (lo, hi) in enumerate(unit_cuts):
        if i > 0:
            copies[3 * i - 1].wait()
        copies[3 * i].wait()
        copies[3 * i + 1].wait()
        for copy in copies[3 * (i + 2) : 3 * (i + 3)]:
            copy.start()
        following = product(gate_ref, lo, hi), product(up_ref, lo, hi)
        if i > 0:
            down(i - 1, gated(*inner))
        inner = following
    copies[-1].wait()
    down(len(unit_cuts) - 1, gated(*inner))

    for c in range(lanes):
        for row in range(chunks * cap, high):
            packed_ref[c, pl.ds(row, blocks, stride=high), :] = jnp.zeros(
                (blocks, 128), jnp.float32
            )
        for j in range(chunks):
            for slot in range(cap):
                packed_ref[c, pl.ds(j * cap + slot, blocks, stride=high), :] = total_ref[
                    j * lanes + c, pl.ds(slot, blocks, stride=cap), :
                ]
    for i, ref in enumerate(out_refs):
        for c in range(lanes):
            columns = slice(c * 128, (c + 1) * 128)
            part = packed_ref[c, i * per_ref * high : (i + 1) * per_ref * high, :]
            ref[:, columns] = part.astype(jnp.bfloat16)


def expert_rows(arrays, w_gate, w_up, w_down, packing, after):
    features, units = w_gate.shape
    rows = len(arrays) * (arrays[0].shape[0] // packing.rows) * packing.cap
    unit_cuts = cuts(units)
    return pl.pallas_call(
        functools.partial(expert_kernel, packing, unit_cuts, len(arrays), len(after)),
        out_shape=[jax.ShapeDtypeStruct(arrays[0].shape, jnp.bfloat16)] * len(arrays),
        in_specs=[VMEM] * len(arrays) + [HBM] * 3 + [ANY] * len(after),
        out_specs=[VMEM] * len(arrays),
        scratch_shapes=[
            pltpu.VMEM((units, features), jnp.bfloat16),
            pltpu.VMEM((units, features), jnp.bfloat16),
            pltpu.VMEM((units, features), jnp.bfloat16),
            pltpu.VMEM((features, -(-rows // 128) * 128), jnp.bfloat16),
            pltpu.VMEM((features // 128, rows + 16, 128), jnp.float32),
            pltpu.VMEM(
                (packing.width // 128, len(arrays) * arrays[0].shape[0] + packing.rows, 128),
                jnp.float32,
            ),
            pltpu.SemaphoreType.DMA((3 * len(unit_cuts),)),
        ],
        compiler_params=pltpu.CompilerParams(vmem_limit_bytes=48 << 20),
        cost_estimate=pl.CostEstimate(
            flops=6 * rows * features * units,
            bytes_accessed=6 * features * units,
            transcendentals=rows * units,
        ),
        name="experts",
    )(*arrays, w_gate.T, w_up.T, w_down, *after)


def combine_kernel(packing, spot_ref, weight_ref, *refs):
    block_refs, out_ref = refs[:-1], refs[-1]
    rows = out_ref.shape[0]
    blocks = jnp.concatenate([ref[...] for ref in block_refs], axis=0)
    place = lax.broadcasted_iota(jnp.int32, (rows, blocks.shape[0]), 1).astype(jnp.float32)
    picks = [
        jnp.where(place - float(j * packing.cap) == spot_ref[:, t : t + 1], 1.0, 0.0)
        for t in range(2)
        for j in range(packing.chunks)
    ]
    if rows % 16 == 0:
        table = jnp.concatenate(picks, axis=0).astype(jnp.bfloat16)
        picked = jnp.dot(table, blocks, preferred_element_type=jnp.float32)
        picked = [picked[i * rows : (i + 1) * rows] for i in range(len(picks))]
    else:
        picked = [
            jnp.dot(pick.astype(jnp.bfloat16), blocks, preferred_element_type=jnp.float32)
            for pick in picks
        ]
    for j in range(packing.chunks):
        out_ref[:, j * packing.width : (j + 1) * packing.width] = (
            weight_ref[:, 0:1] * picked[j] + weight_ref[:, 1:2] * picked[packing.chunks + j]
        ).astype(jnp.bfloat16)


def combine(spot, weights, blocks, packing, rows, features):
    return pl.pallas_call(
        functools.partial(combine_kernel, packing),
        out_shape=jax.ShapeDtypeStruct((rows, features), jnp.bfloat16),
        in_specs=[VMEM] * (2 + len(blocks)),
        out_specs=VMEM,
        compiler_params=pltpu.CompilerParams(vmem_limit_bytes=8 << 20),
        name="combine",
    )(spot, weights, *blocks)


def partial_captions(text_hidden, caption_weight, grid):
    groups = grid.pairs * 2
    rows = text_hidden.shape[0] // (grid.experts * groups)
    bits = (grid.experts * groups).bit_length() - 1
    text = text_hidden.reshape((2,) * bits + (rows, -1))
    for bit in range(bits):
        text = jnp.roll(text, (grid.index >> (bits - 1 - bit)) & 1, axis=bit)
    text = text.reshape(grid.experts, grid.pairs, 2, rows, -1)
    text = jnp.concatenate([text[:, 1:], text[:, :1]], axis=1)
    text = [
        jnp.transpose(text[:, :, c], (1, 0, 2, 3)).reshape(-1, text_hidden.shape[1])
        for c in (1, 0)
    ]
    other, own = [
        jnp.dot(text[c], caption_weight, preferred_element_type=jnp.float32).astype(kind)
        for c, kind in enumerate((jnp.bfloat16, jnp.float32))
    ]
    high = rows * grid.experts
    return [
        value[k * high : (k + 1) * high] for value in (other, own) for k in range(grid.pairs)
    ]


def local(
    image_rows,
    text_hidden,
    caption_weight,
    mod_scale,
    mod_shift,
    router_weight,
    image_experts,
    caption_experts,
    prompt_lengths,
    w_gate,
    w_up,
    w_down,
):
    devices = lax.axis_size("dev")
    features, experts = router_weight.shape
    grid = Grid(devices, experts)
    pairs = grid.pairs
    wide, narrow = jnp.float32, jnp.bfloat16
    image_packing = Packing(image_rows.shape[0] * 3 // 4, features)
    caption_packing = Packing(text_hidden.shape[0] // devices // 2 + 1, features)

    def split(value, count):
        rows = value.shape[0] // count
        return [value[k * rows : (k + 1) * rows] for k in range(count)]

    def to_experts(blocks):
        return [grid.swap(blocks[k], 0, k) for k in range(1, experts)]

    def to_pairs(first):
        return [first] + [grid.swap(first, 1, k) for k in range(1, pairs)]

    def over_cores(values):
        return [grid.swap(value, 2, 1) for value in values]

    def join_cores(results):
        own, other = results[:pairs], results[pairs:]
        sums = [None] * pairs
        for k in list(range(1, pairs)) + [0]:
            sums[k] = own[k].astype(wide) + grid.swap(other[k], 2, 1).astype(wide)
        return sums[0], [value.astype(narrow) for value in sums[1:]]

    def from_pairs(crossing):
        return [grid.swap(value, 1, k) for k, value in enumerate(crossing, 1)]

    def from_experts(kept, received):
        total = kept
        for value in received:
            total = total + value.astype(wide)
        parts = split(total.astype(narrow), experts)
        return [parts[0]] + [grid.swap(parts[k], 0, k) for k in range(1, experts)]

    partial = partial_captions(text_hidden, caption_weight, grid)
    sums = [
        partial[pairs + i] + grid.swap(partial[i], 2, 1).astype(wide) for i in range(pairs)
    ]
    crossing = [value.astype(narrow) for value in sums[:-1]]
    received = [grid.swap(value, 1, k) for k, value in enumerate(crossing, 1)]

    rows = text_hidden.shape[0] // devices
    position = grid.index * rows + jnp.arange(rows, dtype=jnp.int32)
    prompts = jnp.arange(prompt_lengths.shape[0], dtype=jnp.int32)
    lengths = jnp.where(position[:, None] // PLEN == prompts, prompt_lengths, 0).sum(axis=1)
    ids = jnp.where((position % PLEN < lengths)[None, :], caption_experts.T, -1)
    ids = jnp.pad(ids, ((0, 0), (0, image_rows.shape[0] - rows)))
    ids = jnp.concatenate([image_experts.T, ids], axis=0)
    small = jnp.concatenate([mod_scale[None], mod_shift[None], router_weight.T], axis=0)
    (image_spot, caption_spot, image_normed), blocks = prepare(
        ids, small, image_rows, rows, [image_packing, caption_packing], experts, crossing[:1]
    )
    image_first = [blocks[0]] + to_experts(blocks)

    received[0] = tie([received[0]], blocks[1:2], HINT)
    total = sums[-1]
    for value in received:
        total = total + value.astype(wide)
    parts = split(total, experts)
    sent = [part.astype(narrow) for part in parts[1:]]
    terms = parts[:1] + [grid.swap(part, 0, k) for k, part in enumerate(sent, 1)]
    image_first = jnp.concatenate([tie([image_first[0]], sent)] + image_first[1:], axis=0)
    image_own = to_pairs(image_first)
    weights = (w_gate, w_up, w_down)

    caption_normed, blocks = modulate(terms, caption_spot, small, caption_packing, experts)
    received = to_experts(blocks)
    image_own = image_own[:1] + [tie([value], blocks[1:2]) for value in image_own[1:]]
    image_arrays = image_own + over_cores(image_own)
    caption_first = jnp.concatenate([blocks[0]] + received, axis=0)
    caption_own = to_pairs(caption_first)

    image_weights = route(image_normed, image_spot, small)
    caption_weights = route(caption_normed, caption_spot, small)
    image_results = expert_rows(
        image_arrays, *weights, image_packing, [caption_first, image_weights]
    )
    caption_own = caption_own[:1] + [tie([value], image_results[:1]) for value in caption_own[1:]]
    image_results = list(image_results[:pairs]) + [
        tie([value], caption_own[1:2]) for value in image_results[pairs:]
    ]
    image_kept, image_crossing = join_cores(image_results)
    caption_results = expert_rows(
        caption_own + over_cores(caption_own),
        *weights,
        caption_packing,
        image_crossing[:1] + [caption_weights],
    )
    image_received = [
        tie([value], caption_results[:1]) for value in from_pairs(image_crossing)
    ]
    caption_results = list(caption_results[:pairs]) + [
        tie([value], image_received[:1]) for value in caption_results[pairs:]
    ]
    caption_kept, caption_crossing = join_cores(caption_results)
    image_received = [tie([value], caption_crossing[:1]) for value in image_received]
    image_blocks = from_experts(image_kept, image_received)
    caption_received = from_pairs(caption_crossing)
    caption_blocks = from_experts(caption_kept, caption_received)

    rows = image_rows.shape[0]
    image_out = combine(image_spot, image_weights, image_blocks, image_packing, rows, features)
    rows = text_hidden.shape[0] // devices
    caption_out = combine(
        caption_spot, caption_weights, caption_blocks, caption_packing, rows, features
    )
    return (image_out, caption_out)


def solution(mesh):
    in_specs = (
        P(("groups", "dev"), None),
        P("groups", "dev"),
        P("dev", None),
        P(),
        P(),
        P(),
        P(("groups", "dev"), None),
        P(("groups", "dev"), None),
        P("groups"),
        P(None, "dev"),
        P(None, "dev"),
        P("dev", None),
    )
    out_specs = (P(("groups", "dev"), None), P(("groups", "dev"), None))
    return jax.shard_map(local, mesh=mesh, in_specs=in_specs, out_specs=out_specs, check_vma=False)
```

```python
import functools

import jax
import jax.numpy as jnp
from jax import lax
from jax.experimental import pallas as pl
from jax.experimental.pallas import tpu as pltpu
from jax.sharding import PartitionSpec as P

PLEN = 128
HINT = 1 << 33
VMEM = pl.BlockSpec(memory_space=pltpu.VMEM)
SMEM = pl.BlockSpec(memory_space=pltpu.SMEM)
ANY = pl.BlockSpec(memory_space=pl.ANY)
HBM = pl.BlockSpec(memory_space=pltpu.HBM)


class Grid:
    def __init__(self, devices, experts):
        self.experts = experts
        self.pairs = devices // experts // 2
        index = lax.axis_index("dev")
        self.index = index
        self.expert = index // (self.pairs * 2)
        self.pair = (index // 2) % self.pairs
        self.core = index % 2

    def swap(self, value, axis, step):
        moves = []
        for expert in range(self.experts):
            for pair in range(self.pairs):
                for core in range(2):
                    to = [expert, pair, core]
                    to[axis] ^= step
                    moves.append(
                        (
                            (expert * self.pairs + pair) * 2 + core,
                            (to[0] * self.pairs + to[1]) * 2 + to[2],
                        )
                    )
        return lax.ppermute(value, "dev", moves)


class Packing:
    def __init__(self, cap, features):
        best = None
        for chunks in range(1, features // 128 + 1):
            if features % (128 * chunks):
                continue
            rows = -(-cap * chunks // 16) * 16
            cost = rows * (features // chunks)
            if best is None or cost < best[0]:
                best = (cost, chunks, rows)
        _, self.chunks, self.rows = best
        self.cap = cap
        self.width = features // self.chunks


def place(chosen, packing, experts, out_ref):
    index = lax.axis_index("dev")
    rows = chosen.shape[1]
    relative = chosen ^ (index // (lax.axis_size("dev") // experts))
    expert_at = lax.broadcasted_iota(jnp.int32, (experts, rows), 0)
    routed = (relative[0:1, :] == expert_at) | (relative[1:2, :] == expert_at)
    routed = routed & (chosen[0:1, :] >= 0)
    at = [lax.broadcasted_iota(jnp.int32, (rows, rows), d) for d in range(2)]
    before = (at[0] < at[1]).astype(jnp.float32)
    spot = jnp.dot(routed.astype(jnp.float32), before, preferred_element_type=jnp.float32)
    spot = spot + expert_at.astype(jnp.float32) * float(packing.rows)
    for t in range(2):
        own = jnp.where(relative[t : t + 1, :] == expert_at, spot, 0.0)
        own = jnp.sum(own, axis=0, keepdims=True)
        own = jnp.where(chosen[t : t + 1, :] >= 0, own, -65536.0)
        for column, value in ((t, own), (2 + t, chosen[t : t + 1, :].astype(jnp.float32))):
            out_ref[:, column : column + 1] = jnp.sum(
                jnp.where(at[0] == at[1], value, 0.0), axis=1, keepdims=True
            )


def norm_and_pack(values, small_ref, spot_ref, packing, experts, normed_ref, packed_refs):
    rows = values.shape[0]
    center = values - jnp.mean(values, axis=1, keepdims=True)
    spread = jnp.mean(center * center, axis=1, keepdims=True)
    normed = center * lax.rsqrt(spread + 1e-06) * small_ref[0:1, :] + small_ref[1:2, :]
    normed = normed.astype(jnp.bfloat16)
    normed_ref[...] = normed
    place = lax.broadcasted_iota(jnp.int32, (rows, experts * packing.rows), 1).astype(jnp.float32)
    packed = None
    for j in range(packing.chunks):
        at = place - float(j * packing.cap)
        into = jnp.where((at == spot_ref[:, 0:1]) | (at == spot_ref[:, 1:2]), 1.0, 0.0)
        term = jnp.dot(
            into.T.astype(jnp.bfloat16),
            normed[:, j * packing.width : (j + 1) * packing.width],
            preferred_element_type=jnp.float32,
        )
        packed = term if packed is None else packed + term
    for k in range(experts):
        packed_refs[k][...] = packed[k * packing.rows : (k + 1) * packing.rows].astype(
            jnp.bfloat16
        )


def prepare_kernel(packings, experts, after, ids_ref, small_ref, image_ref, *refs):
    image_spot, caption_spot, normed_ref = refs[after : after + 3]
    image_rows, caption_rows = image_spot.shape[0], caption_spot.shape[0]
    place(ids_ref[0:2, 0:image_rows], packings[0], experts, image_spot)
    place(ids_ref[2:4, 0:caption_rows], packings[1], experts, caption_spot)
    norm_and_pack(
        image_ref[...].astype(jnp.float32),
        small_ref,
        image_spot,
        packings[0],
        experts,
        normed_ref,
        refs[after + 3 :],
    )


def prepare(ids, small, image_rows, caption_rows, packings, experts, after):
    rows, features = image_rows.shape
    packed = jax.ShapeDtypeStruct((packings[0].rows, packings[0].width), jnp.bfloat16)
    results = pl.pallas_call(
        functools.partial(prepare_kernel, packings, experts, len(after)),
        out_shape=[
            jax.ShapeDtypeStruct((rows, 4), jnp.float32),
            jax.ShapeDtypeStruct((caption_rows, 4), jnp.float32),
            jax.ShapeDtypeStruct((rows, features), jnp.bfloat16),
        ]
        + [packed] * experts,
        in_specs=[VMEM] * 3 + [ANY] * len(after),
        out_specs=[VMEM] * (3 + experts),
        compiler_params=pltpu.CompilerParams(vmem_limit_bytes=8 << 20),
        name="prepare",
    )(ids, small, image_rows, *after)
    return results[:3], list(results[3:])


def tie_kernel(count, *refs):
    value = refs[0][...]
    for ref in refs[1:count]:
        value = value.astype(jnp.float32) + ref[...].astype(jnp.float32)
    refs[-1][...] = value


def tie(values, after, cost=0):
    kind = values[0].dtype if len(values) == 1 else jnp.float32
    return pl.pallas_call(
        functools.partial(tie_kernel, len(values)),
        out_shape=jax.ShapeDtypeStruct(values[0].shape, kind),
        in_specs=[VMEM] * len(values) + [ANY] * len(after),
        out_specs=VMEM,
        compiler_params=pltpu.CompilerParams(vmem_limit_bytes=8 << 20),
        cost_estimate=pl.CostEstimate(flops=cost, bytes_accessed=0, transcendentals=0),
        name="tie",
    )(*values, *after)


def modulate_kernel(packing, experts, count, spot_ref, small_ref, *refs):
    values = refs[0][...].astype(jnp.float32)
    for ref in refs[1:count]:
        values = values + ref[...].astype(jnp.float32)
    values = values.astype(jnp.bfloat16).astype(jnp.float32)
    norm_and_pack(
        values, small_ref, spot_ref, packing, experts, refs[count], refs[count + 1 :]
    )


def modulate(terms, spot, small, packing, experts):
    rows, features = terms[0].shape
    packed = jax.ShapeDtypeStruct((packing.rows, packing.width), jnp.bfloat16)
    results = pl.pallas_call(
        functools.partial(modulate_kernel, packing, experts, len(terms)),
        out_shape=[jax.ShapeDtypeStruct((rows, features), jnp.bfloat16)] + [packed] * experts,
        in_specs=[VMEM] * (2 + len(terms)),
        out_specs=[VMEM] * (1 + experts),
        compiler_params=pltpu.CompilerParams(vmem_limit_bytes=8 << 20),
        cost_estimate=pl.CostEstimate(flops=HINT, bytes_accessed=0, transcendentals=0),
        name="modulate",
    )(spot, small, *terms)
    return (results[0], list(results[1:]))


def route_kernel(spot_ref, normed_ref, small_ref, weight_ref):
    normed = normed_ref[...].astype(jnp.float32)
    logits = [
        jnp.sum(normed * small_ref[2 + k : 3 + k, :], axis=1, keepdims=True)
        for k in range(small_ref.shape[0] - 2)
    ]
    picked = []
    for t in range(2):
        logit = jnp.zeros_like(logits[0])
        for k, value in enumerate(logits):
            logit = jnp.where(spot_ref[:, 2 + t : 3 + t] == float(k), value, logit)
        picked.append(logit)
    weight_ref[:, 0:1] = jax.nn.sigmoid(picked[0] - picked[1])
    weight_ref[:, 1:2] = jax.nn.sigmoid(picked[1] - picked[0])


def route(normed, spot, small):
    return pl.pallas_call(
        route_kernel,
        out_shape=jax.ShapeDtypeStruct((spot.shape[0], 2), jnp.float32),
        in_specs=[VMEM] * 3,
        out_specs=VMEM,
        compiler_params=pltpu.CompilerParams(vmem_limit_bytes=8 << 20),
        name="route",
    )(spot, normed, small)


def cuts(units):
    edges = [0] + list(range(256, units - 255, 512)) + [units]
    if edges[-1] - edges[-2] > 256 and len(edges) > 2:
        edges.insert(-1, edges[-2] + 256)
    return list(zip(edges[:-1], edges[1:]))


def expert_kernel(packing, unit_cuts, count, after, *refs):
    row_refs = refs[:count]
    gate_hbm, up_hbm, down_hbm = refs[count : count + 3]
    place = count + 3 + after
    out_refs = refs[place : place + count]
    gate_ref, up_ref, down_ref, rows_ref, total_ref, packed_ref, sems = refs[place + count :]
    copies = []
    for i, (lo, hi) in enumerate(unit_cuts):
        for t, (source, target) in enumerate(
            ((gate_hbm, gate_ref), (up_hbm, up_ref), (down_hbm, down_ref))
        ):
            copies.append(
                pltpu.make_async_copy(
                    source.at[lo:hi], target.at[lo:hi], sems.at[3 * i + t]
                )
            )
    for copy in copies[:2]:
        copy.start()

    cap, chunks, width, high = packing.cap, packing.chunks, packing.width, packing.rows
    per_ref = row_refs[0].shape[0] // high
    blocks = count * per_ref
    rows = blocks * cap
    lanes = width // 128
    for i, ref in enumerate(row_refs):
        for c in range(lanes):
            packed_ref[c, i * per_ref * high : (i + 1) * per_ref * high, :] = ref[
                :, c * 128 : (c + 1) * 128
            ].astype(jnp.float32)
    spare = rows_ref.shape[1] - rows
    for j in range(chunks):
        for c in range(lanes):
            for slot in range(cap):
                total_ref[j * lanes + c, pl.ds(slot, blocks, stride=cap), :] = packed_ref[
                    c, pl.ds(j * cap + slot, blocks, stride=high), :
                ]
    for copy in copies[2:6]:
        copy.start()
    for c in range(chunks * lanes):
        part = total_ref[c, 0:rows, :]
        if spare:
            part = jnp.concatenate([part, jnp.zeros((spare, 128), jnp.float32)], axis=0)
        rows_ref[c * 128 : (c + 1) * 128, :] = part.astype(jnp.bfloat16).T

    def down(i, hidden):
        lo, hi = unit_cuts[i]
        term = jnp.dot(hidden, down_ref[lo:hi, :], preferred_element_type=jnp.float32)
        for c in range(chunks * lanes):
            if i == 0:
                total_ref[c, 0:rows, :] = term[:, c * 128 : (c + 1) * 128]
            else:
                total_ref[c, 0:rows, :] += term[:, c * 128 : (c + 1) * 128]

    features = gate_hbm.shape[1]
    middle = features // 256 * 128

    def product(weight_ref, lo, hi):
        return jnp.dot(
            weight_ref[lo:hi, :middle], rows_ref[:middle, :], preferred_element_type=jnp.float32
        ) + jnp.dot(
            weight_ref[lo:hi, middle:], rows_ref[middle:, :], preferred_element_type=jnp.float32
        )

    def gated(gate, up):
        return (gate * jax.nn.sigmoid(gate) * up).astype(jnp.bfloat16).T[0:rows]

    inner = None
    for i, (lo, hi) in enumerate(unit_cuts):
        if i > 0:
            copies[3 * i - 1].wait()
        copies[3 * i].wait()
        copies[3 * i + 1].wait()
        for copy in copies[3 * (i + 2) : 3 * (i + 3)]:
            copy.start()
        following = product(gate_ref, lo, hi), product(up_ref, lo, hi)
        if i > 0:
            down(i - 1, gated(*inner))
        inner = following
    copies[-1].wait()
    down(len(unit_cuts) - 1, gated(*inner))

    for c in range(lanes):
        for row in range(chunks * cap, high):
            packed_ref[c, pl.ds(row, blocks, stride=high), :] = jnp.zeros(
                (blocks, 128), jnp.float32
            )
        for j in range(chunks):
            for slot in range(cap):
                packed_ref[c, pl.ds(j * cap + slot, blocks, stride=high), :] = total_ref[
                    j * lanes + c, pl.ds(slot, blocks, stride=cap), :
                ]
    for i, ref in enumerate(out_refs):
        for c in range(lanes):
            columns = slice(c * 128, (c + 1) * 128)
            part = packed_ref[c, i * per_ref * high : (i + 1) * per_ref * high, :]
            ref[:, columns] = part.astype(jnp.bfloat16)


def expert_rows(arrays, w_gate, w_up, w_down, packing, after):
    features, units = w_gate.shape
    rows = len(arrays) * (arrays[0].shape[0] // packing.rows) * packing.cap
    unit_cuts = cuts(units)
    return pl.pallas_call(
        functools.partial(expert_kernel, packing, unit_cuts, len(arrays), len(after)),
        out_shape=[jax.ShapeDtypeStruct(arrays[0].shape, jnp.bfloat16)] * len(arrays),
        in_specs=[VMEM] * len(arrays) + [HBM] * 3 + [ANY] * len(after),
        out_specs=[VMEM] * len(arrays),
        scratch_shapes=[
            pltpu.VMEM((units, features), jnp.bfloat16),
            pltpu.VMEM((units, features), jnp.bfloat16),
            pltpu.VMEM((units, features), jnp.bfloat16),
            pltpu.VMEM((features, -(-rows // 128) * 128), jnp.bfloat16),
            pltpu.VMEM((features // 128, rows + 16, 128), jnp.float32),
            pltpu.VMEM(
                (packing.width // 128, len(arrays) * arrays[0].shape[0] + packing.rows, 128),
                jnp.float32,
            ),
            pltpu.SemaphoreType.DMA((3 * len(unit_cuts),)),
        ],
        compiler_params=pltpu.CompilerParams(vmem_limit_bytes=48 << 20),
        cost_estimate=pl.CostEstimate(
            flops=6 * rows * features * units,
            bytes_accessed=6 * features * units,
            transcendentals=rows * units,
        ),
        name="experts",
    )(*arrays, w_gate.T, w_up.T, w_down, *after)


def combine_kernel(packing, spot_ref, weight_ref, *refs):
    block_refs, out_ref = refs[:-1], refs[-1]
    rows = out_ref.shape[0]
    blocks = jnp.concatenate([ref[...] for ref in block_refs], axis=0)
    place = lax.broadcasted_iota(jnp.int32, (rows, blocks.shape[0]), 1).astype(jnp.float32)
    picks = [
        jnp.where(place - float(j * packing.cap) == spot_ref[:, t : t + 1], 1.0, 0.0)
        for t in range(2)
        for j in range(packing.chunks)
    ]
    if rows % 16 == 0:
        table = jnp.concatenate(picks, axis=0).astype(jnp.bfloat16)
        picked = jnp.dot(table, blocks, preferred_element_type=jnp.float32)
        picked = [picked[i * rows : (i + 1) * rows] for i in range(len(picks))]
    else:
        picked = [
            jnp.dot(pick.astype(jnp.bfloat16), blocks, preferred_element_type=jnp.float32)
            for pick in picks
        ]
    for j in range(packing.chunks):
        out_ref[:, j * packing.width : (j + 1) * packing.width] = (
            weight_ref[:, 0:1] * picked[j] + weight_ref[:, 1:2] * picked[packing.chunks + j]
        ).astype(jnp.bfloat16)


def combine(spot, weights, blocks, packing, rows, features):
    return pl.pallas_call(
        functools.partial(combine_kernel, packing),
        out_shape=jax.ShapeDtypeStruct((rows, features), jnp.bfloat16),
        in_specs=[VMEM] * (2 + len(blocks)),
        out_specs=VMEM,
        compiler_params=pltpu.CompilerParams(vmem_limit_bytes=8 << 20),
        name="combine",
    )(spot, weights, *blocks)


def partial_captions(text_hidden, caption_weight, grid):
    groups = grid.pairs * 2
    rows = text_hidden.shape[0] // (grid.experts * groups)
    bits = (grid.experts * groups).bit_length() - 1
    text = text_hidden.reshape((2,) * bits + (rows, -1))
    for bit in range(bits):
        text = jnp.roll(text, (grid.index >> (bits - 1 - bit)) & 1, axis=bit)
    text = text.reshape(grid.experts, grid.pairs, 2, rows, -1)
    text = jnp.concatenate([text[:, 1:], text[:, :1]], axis=1)
    text = [
        jnp.transpose(text[:, :, c], (1, 0, 2, 3)).reshape(-1, text_hidden.shape[1])
        for c in (1, 0)
    ]
    other, own = [
        jnp.dot(text[c], caption_weight, preferred_element_type=jnp.float32).astype(kind)
        for c, kind in enumerate((jnp.bfloat16, jnp.float32))
    ]
    high = rows * grid.experts
    return [
        value[k * high : (k + 1) * high] for value in (other, own) for k in range(grid.pairs)
    ]


def local(
    image_rows,
    text_hidden,
    caption_weight,
    mod_scale,
    mod_shift,
    router_weight,
    image_experts,
    caption_experts,
    prompt_lengths,
    w_gate,
    w_up,
    w_down,
):
    devices = lax.axis_size("dev")
    features, experts = router_weight.shape
    grid = Grid(devices, experts)
    pairs = grid.pairs
    wide, narrow = jnp.float32, jnp.bfloat16
    image_packing = Packing(image_rows.shape[0] * 3 // 4, features)
    caption_packing = Packing(text_hidden.shape[0] // devices // 2 + 1, features)

    def split(value, count):
        rows = value.shape[0] // count
        return [value[k * rows : (k + 1) * rows] for k in range(count)]

    def to_experts(blocks):
        return [grid.swap(blocks[k], 0, k) for k in range(1, experts)]

    def to_pairs(first):
        return [first] + [grid.swap(first, 1, k) for k in range(1, pairs)]

    def over_cores(values):
        return [grid.swap(value, 2, 1) for value in values]

    def join_cores(results):
        own, other = results[:pairs], results[pairs:]
        sums = [None] * pairs
        for k in list(range(1, pairs)) + [0]:
            sums[k] = own[k].astype(wide) + grid.swap(other[k], 2, 1).astype(wide)
        return sums[0], [value.astype(narrow) for value in sums[1:]]

    def from_pairs(crossing):
        return [grid.swap(value, 1, k) for k, value in enumerate(crossing, 1)]

    def from_experts(kept, received):
        total = kept
        for value in received:
            total = total + value.astype(wide)
        parts = split(total.astype(narrow), experts)
        return [parts[0]] + [grid.swap(parts[k], 0, k) for k in range(1, experts)]

    partial = partial_captions(text_hidden, caption_weight, grid)
    sums = [
        partial[pairs + i] + grid.swap(partial[i], 2, 1).astype(wide) for i in range(pairs)
    ]
    crossing = [value.astype(narrow) for value in sums[:-1]]
    received = [grid.swap(value, 1, k) for k, value in enumerate(crossing, 1)]

    rows = text_hidden.shape[0] // devices
    position = grid.index * rows + jnp.arange(rows, dtype=jnp.int32)
    prompts = jnp.arange(prompt_lengths.shape[0], dtype=jnp.int32)
    lengths = jnp.where(position[:, None] // PLEN == prompts, prompt_lengths, 0).sum(axis=1)
    ids = jnp.where((position % PLEN < lengths)[None, :], caption_experts.T, -1)
    ids = jnp.pad(ids, ((0, 0), (0, image_rows.shape[0] - rows)))
    ids = jnp.concatenate([image_experts.T, ids], axis=0)
    small = jnp.concatenate([mod_scale[None], mod_shift[None], router_weight.T], axis=0)
    (image_spot, caption_spot, image_normed), blocks = prepare(
        ids, small, image_rows, rows, [image_packing, caption_packing], experts, crossing[:1]
    )
    image_first = [blocks[0]] + to_experts(blocks)

    received[0] = tie([received[0]], blocks[1:2], HINT)
    total = sums[-1]
    for value in received:
        total = total + value.astype(wide)
    parts = split(total, experts)
    sent = [part.astype(narrow) for part in parts[1:]]
    terms = parts[:1] + [grid.swap(part, 0, k) for k, part in enumerate(sent, 1)]
    image_first = jnp.concatenate([tie([image_first[0]], sent)] + image_first[1:], axis=0)
    image_own = to_pairs(image_first)
    weights = (w_gate, w_up, w_down)

    caption_normed, blocks = modulate(terms, caption_spot, small, caption_packing, experts)
    received = to_experts(blocks)
    image_own = image_own[:1] + [tie([value], blocks[1:2]) for value in image_own[1:]]
    image_arrays = image_own + over_cores(image_own)
    caption_first = jnp.concatenate([blocks[0]] + received, axis=0)
    caption_own = to_pairs(caption_first)

    image_weights = route(image_normed, image_spot, small)
    caption_weights = route(caption_normed, caption_spot, small)
    image_results = expert_rows(
        image_arrays, *weights, image_packing, [caption_first, image_weights]
    )
    caption_own = caption_own[:1] + [tie([value], image_results[:1]) for value in caption_own[1:]]
    image_results = list(image_results[:pairs]) + [
        tie([value], caption_own[1:2]) for value in image_results[pairs:]
    ]
    image_kept, image_crossing = join_cores(image_results)
    caption_results = expert_rows(
        caption_own + over_cores(caption_own),
        *weights,
        caption_packing,
        image_crossing[:1] + [caption_weights],
    )
    image_received = [
        tie([value], caption_results[:1]) for value in from_pairs(image_crossing)
    ]
    caption_results = list(caption_results[:pairs]) + [
        tie([value], image_received[:1]) for value in caption_results[pairs:]
    ]
    caption_kept, caption_crossing = join_cores(caption_results)
    image_received = [tie([value], caption_crossing[:1]) for value in image_received]
    image_blocks = from_experts(image_kept, image_received)
    caption_received = from_pairs(caption_crossing)
    caption_blocks = from_experts(caption_kept, caption_received)

    rows = image_rows.shape[0]
    image_out = combine(image_spot, image_weights, image_blocks, image_packing, rows, features)
    rows = text_hidden.shape[0] // devices
    caption_out = combine(
        caption_spot, caption_weights, caption_blocks, caption_packing, rows, features
    )
    return (image_out, caption_out)


def solution(mesh):
    in_specs = (
        P(("groups", "dev"), None),
        P("groups", "dev"),
        P("dev", None),
        P(),
        P(),
        P(),
        P(("groups", "dev"), None),
        P(("groups", "dev"), None),
        P("groups"),
        P(None, "dev"),
        P(None, "dev"),
        P("dev", None),
    )
    out_specs = (P(("groups", "dev"), None), P(("groups", "dev"), None))
    return jax.shard_map(local, mesh=mesh, in_specs=in_specs, out_specs=out_specs, check_vma=False)
```

```python
import functools

import jax
import jax.numpy as jnp
from jax import lax
from jax.experimental import pallas as pl
from jax.experimental.pallas import tpu as pltpu
from jax.sharding import PartitionSpec as P

PLEN = 128
HINT = 1 << 33
STRIP = 512
VMEM = pl.BlockSpec(memory_space=pltpu.VMEM)
SMEM = pl.BlockSpec(memory_space=pltpu.SMEM)
ANY = pl.BlockSpec(memory_space=pl.ANY)
HBM = pl.BlockSpec(memory_space=pltpu.HBM)


class Grid:
    def __init__(self, devices, experts):
        self.experts = experts
        self.pairs = devices // experts // 2
        index = lax.axis_index("dev")
        self.index = index
        self.expert = index // (self.pairs * 2)
        self.pair = (index // 2) % self.pairs
        self.core = index % 2

    def swap(self, value, axis, step):
        moves = []
        for expert in range(self.experts):
            for pair in range(self.pairs):
                for core in range(2):
                    to = [expert, pair, core]
                    to[axis] ^= step
                    moves.append(
                        (
                            (expert * self.pairs + pair) * 2 + core,
                            (to[0] * self.pairs + to[1]) * 2 + to[2],
                        )
                    )
        return lax.ppermute(value, "dev", moves)


class Packing:
    def __init__(self, cap, features):
        best = None
        for chunks in range(1, features // 128 + 1):
            if features % (128 * chunks):
                continue
            rows = -(-cap * chunks // 16) * 16
            cost = rows * (features // chunks)
            if best is None or cost < best[0]:
                best = (cost, chunks, rows)
        _, self.chunks, self.rows = best
        self.cap = cap
        self.width = features // self.chunks


def place(chosen, packing, experts, out_ref):
    index = lax.axis_index("dev")
    rows = chosen.shape[1]
    relative = chosen ^ (index // (lax.axis_size("dev") // experts))
    expert_at = lax.broadcasted_iota(jnp.int32, (experts, rows), 0)
    routed = (relative[0:1, :] == expert_at) | (relative[1:2, :] == expert_at)
    routed = routed & (chosen[0:1, :] >= 0)
    at = [lax.broadcasted_iota(jnp.int32, (rows, rows), d) for d in range(2)]
    before = (at[0] < at[1]).astype(jnp.float32)
    spot = jnp.dot(routed.astype(jnp.float32), before, preferred_element_type=jnp.float32)
    spot = spot + expert_at.astype(jnp.float32) * float(packing.rows)
    for t in range(2):
        own = jnp.where(relative[t : t + 1, :] == expert_at, spot, 0.0)
        own = jnp.sum(own, axis=0, keepdims=True)
        own = jnp.where(chosen[t : t + 1, :] >= 0, own, -65536.0)
        for column, value in ((t, own), (2 + t, chosen[t : t + 1, :].astype(jnp.float32))):
            out_ref[:, column : column + 1] = jnp.sum(
                jnp.where(at[0] == at[1], value, 0.0), axis=1, keepdims=True
            )


def norm_and_pack(values, small_ref, spot_ref, packing, experts, normed_ref, packed_refs):
    rows = values.shape[0]
    center = values - jnp.mean(values, axis=1, keepdims=True)
    spread = jnp.mean(center * center, axis=1, keepdims=True)
    normed = center * lax.rsqrt(spread + 1e-06) * small_ref[0:1, :] + small_ref[1:2, :]
    normed = normed.astype(jnp.bfloat16)
    normed_ref[...] = normed
    place = lax.broadcasted_iota(jnp.int32, (rows, experts * packing.rows), 1).astype(jnp.float32)
    packed = None
    for j in range(packing.chunks):
        at = place - float(j * packing.cap)
        into = jnp.where((at == spot_ref[:, 0:1]) | (at == spot_ref[:, 1:2]), 1.0, 0.0)
        term = jnp.dot(
            into.T.astype(jnp.bfloat16),
            normed[:, j * packing.width : (j + 1) * packing.width],
            preferred_element_type=jnp.float32,
        )
        packed = term if packed is None else packed + term
    for k in range(experts):
        packed_refs[k][...] = packed[k * packing.rows : (k + 1) * packing.rows].astype(
            jnp.bfloat16
        )


def prepare_kernel(packings, experts, after, ids_ref, small_ref, image_ref, *refs):
    image_spot, caption_spot, normed_ref = refs[after : after + 3]
    image_rows, caption_rows = image_spot.shape[0], caption_spot.shape[0]
    place(ids_ref[0:2, 0:image_rows], packings[0], experts, image_spot)
    place(ids_ref[2:4, 0:caption_rows], packings[1], experts, caption_spot)
    norm_and_pack(
        image_ref[...].astype(jnp.float32),
        small_ref,
        image_spot,
        packings[0],
        experts,
        normed_ref,
        refs[after + 3 :],
    )


def prepare(ids, small, image_rows, caption_rows, packings, experts, after):
    rows, features = image_rows.shape
    packed = jax.ShapeDtypeStruct((packings[0].rows, packings[0].width), jnp.bfloat16)
    results = pl.pallas_call(
        functools.partial(prepare_kernel, packings, experts, len(after)),
        out_shape=[
            jax.ShapeDtypeStruct((rows, 4), jnp.float32),
            jax.ShapeDtypeStruct((caption_rows, 4), jnp.float32),
            jax.ShapeDtypeStruct((rows, features), jnp.bfloat16),
        ]
        + [packed] * experts,
        in_specs=[VMEM] * 3 + [ANY] * len(after),
        out_specs=[VMEM] * (3 + experts),
        compiler_params=pltpu.CompilerParams(vmem_limit_bytes=8 << 20),
        name="prepare",
    )(ids, small, image_rows, *after)
    return results[:3], list(results[3:])


def tie_kernel(count, *refs):
    value = refs[0][...]
    for ref in refs[1:count]:
        value = value.astype(jnp.float32) + ref[...].astype(jnp.float32)
    refs[-1][...] = value


def tie(values, after, cost=0):
    kind = values[0].dtype if len(values) == 1 else jnp.float32
    return pl.pallas_call(
        functools.partial(tie_kernel, len(values)),
        out_shape=jax.ShapeDtypeStruct(values[0].shape, kind),
        in_specs=[VMEM] * len(values) + [ANY] * len(after),
        out_specs=VMEM,
        compiler_params=pltpu.CompilerParams(vmem_limit_bytes=8 << 20),
        cost_estimate=pl.CostEstimate(flops=cost, bytes_accessed=0, transcendentals=0),
        name="tie",
    )(*values, *after)


def modulate_kernel(packing, experts, count, spot_ref, small_ref, *refs):
    values = refs[0][...].astype(jnp.float32)
    for ref in refs[1:count]:
        values = values + ref[...].astype(jnp.float32)
    values = values.astype(jnp.bfloat16).astype(jnp.float32)
    norm_and_pack(
        values, small_ref, spot_ref, packing, experts, refs[count], refs[count + 1 :]
    )


def modulate(terms, spot, small, packing, experts):
    rows, features = terms[0].shape
    packed = jax.ShapeDtypeStruct((packing.rows, packing.width), jnp.bfloat16)
    results = pl.pallas_call(
        functools.partial(modulate_kernel, packing, experts, len(terms)),
        out_shape=[jax.ShapeDtypeStruct((rows, features), jnp.bfloat16)] + [packed] * experts,
        in_specs=[VMEM] * (2 + len(terms)),
        out_specs=[VMEM] * (1 + experts),
        compiler_params=pltpu.CompilerParams(vmem_limit_bytes=8 << 20),
        cost_estimate=pl.CostEstimate(flops=HINT, bytes_accessed=0, transcendentals=0),
        name="modulate",
    )(spot, small, *terms)
    return (results[0], list(results[1:]))


def route_kernel(spot_ref, normed_ref, small_ref, weight_ref):
    normed = normed_ref[...].astype(jnp.float32)
    logits = [
        jnp.sum(normed * small_ref[2 + k : 3 + k, :], axis=1, keepdims=True)
        for k in range(small_ref.shape[0] - 2)
    ]
    picked = []
    for t in range(2):
        logit = jnp.zeros_like(logits[0])
        for k, value in enumerate(logits):
            logit = jnp.where(spot_ref[:, 2 + t : 3 + t] == float(k), value, logit)
        picked.append(logit)
    weight_ref[:, 0:1] = jax.nn.sigmoid(picked[0] - picked[1])
    weight_ref[:, 1:2] = jax.nn.sigmoid(picked[1] - picked[0])


def route(normed, spot, small):
    return pl.pallas_call(
        route_kernel,
        out_shape=jax.ShapeDtypeStruct((spot.shape[0], 2), jnp.float32),
        in_specs=[VMEM] * 3,
        out_specs=VMEM,
        compiler_params=pltpu.CompilerParams(vmem_limit_bytes=8 << 20),
        name="route",
    )(spot, normed, small)


def cuts(units):
    edges = [0] + list(range(256, units - 255, 512)) + [units]
    return list(zip(edges[:-1], edges[1:]))


def expert_kernel(packing, unit_cuts, count, after, *refs):
    row_refs = refs[:count]
    gate_hbm, up_hbm, down_hbm = refs[count : count + 3]
    place = count + 3 + after
    out_refs = refs[place : place + count]
    gate_ref, up_ref, down_ref, rows_ref, total_ref, packed_ref, sems = refs[place + count :]
    copies = []
    for i, (lo, hi) in enumerate(unit_cuts):
        for t, (source, target) in enumerate(
            ((gate_hbm, gate_ref), (up_hbm, up_ref), (down_hbm, down_ref))
        ):
            copies.append(
                pltpu.make_async_copy(
                    source.at[lo:hi], target.at[lo:hi], sems.at[3 * i + t]
                )
            )
    for copy in copies[:2]:
        copy.start()

    cap, chunks, width, high = packing.cap, packing.chunks, packing.width, packing.rows
    per_ref = row_refs[0].shape[0] // high
    blocks = count * per_ref
    rows = blocks * cap
    lanes = width // 128
    for i, ref in enumerate(row_refs):
        for c in range(lanes):
            packed_ref[c, i * per_ref * high : (i + 1) * per_ref * high, :] = ref[
                :, c * 128 : (c + 1) * 128
            ].astype(jnp.float32)
    spare = rows_ref.shape[1] - rows
    for j in range(chunks):
        for c in range(lanes):
            for slot in range(cap):
                total_ref[j * lanes + c, pl.ds(slot, blocks, stride=cap), :] = packed_ref[
                    c, pl.ds(j * cap + slot, blocks, stride=high), :
                ]
    for copy in copies[2:6]:
        copy.start()
    for c in range(chunks * lanes):
        part = total_ref[c, 0:rows, :]
        if spare:
            part = jnp.concatenate([part, jnp.zeros((spare, 128), jnp.float32)], axis=0)
        rows_ref[c * 128 : (c + 1) * 128, :] = part.astype(jnp.bfloat16).T

    def down(i, hidden):
        lo, hi = unit_cuts[i]
        term = jnp.dot(hidden, down_ref[lo:hi, :], preferred_element_type=jnp.float32)
        for c in range(chunks * lanes):
            if i == 0:
                total_ref[c, 0:rows, :] = term[:, c * 128 : (c + 1) * 128]
            else:
                total_ref[c, 0:rows, :] += term[:, c * 128 : (c + 1) * 128]

    features = gate_hbm.shape[1]

    def product(weight_ref, lo, hi):
        terms = [
            jnp.dot(
                weight_ref[lo:hi, strip : strip + STRIP],
                rows_ref[strip : strip + STRIP, :],
                preferred_element_type=jnp.float32,
            )
            for strip in range(0, features, STRIP)
        ]
        return functools.reduce(jnp.add, terms)

    def gated(gate, up):
        return (gate * jax.nn.sigmoid(gate) * up).astype(jnp.bfloat16).T[0:rows]

    inner = None
    for i, (lo, hi) in enumerate(unit_cuts):
        if i > 0:
            copies[3 * i - 1].wait()
        copies[3 * i].wait()
        copies[3 * i + 1].wait()
        for copy in copies[3 * (i + 2) : 3 * (i + 3)]:
            copy.start()
        following = product(gate_ref, lo, hi), product(up_ref, lo, hi)
        if i > 0:
            down(i - 1, gated(*inner))
        inner = following
    copies[-1].wait()
    down(len(unit_cuts) - 1, gated(*inner))

    for c in range(lanes):
        for row in range(chunks * cap, high):
            packed_ref[c, pl.ds(row, blocks, stride=high), :] = jnp.zeros(
                (blocks, 128), jnp.float32
            )
        for j in range(chunks):
            for slot in range(cap):
                packed_ref[c, pl.ds(j * cap + slot, blocks, stride=high), :] = total_ref[
                    j * lanes + c, pl.ds(slot, blocks, stride=cap), :
                ]
    for i, ref in enumerate(out_refs):
        for c in range(lanes):
            columns = slice(c * 128, (c + 1) * 128)
            part = packed_ref[c, i * per_ref * high : (i + 1) * per_ref * high, :]
            ref[:, columns] = part.astype(jnp.bfloat16)


def expert_rows(arrays, w_gate, w_up, w_down, packing, after):
    features, units = w_gate.shape
    rows = len(arrays) * (arrays[0].shape[0] // packing.rows) * packing.cap
    unit_cuts = cuts(units)
    return pl.pallas_call(
        functools.partial(expert_kernel, packing, unit_cuts, len(arrays), len(after)),
        out_shape=[jax.ShapeDtypeStruct(arrays[0].shape, jnp.bfloat16)] * len(arrays),
        in_specs=[VMEM] * len(arrays) + [HBM] * 3 + [ANY] * len(after),
        out_specs=[VMEM] * len(arrays),
        scratch_shapes=[
            pltpu.VMEM((units, features), jnp.bfloat16),
            pltpu.VMEM((units, features), jnp.bfloat16),
            pltpu.VMEM((units, features), jnp.bfloat16),
            pltpu.VMEM((features, -(-rows // 128) * 128), jnp.bfloat16),
            pltpu.VMEM((features // 128, rows + 16, 128), jnp.float32),
            pltpu.VMEM(
                (packing.width // 128, len(arrays) * arrays[0].shape[0] + packing.rows, 128),
                jnp.float32,
            ),
            pltpu.SemaphoreType.DMA((3 * len(unit_cuts),)),
        ],
        compiler_params=pltpu.CompilerParams(vmem_limit_bytes=48 << 20),
        cost_estimate=pl.CostEstimate(
            flops=6 * rows * features * units,
            bytes_accessed=6 * features * units,
            transcendentals=rows * units,
        ),
        name="experts",
    )(*arrays, w_gate.T, w_up.T, w_down, *after)


def combine_kernel(packing, spot_ref, weight_ref, *refs):
    block_refs, out_ref = refs[:-1], refs[-1]
    rows = out_ref.shape[0]
    blocks = jnp.concatenate([ref[...] for ref in block_refs], axis=0)
    place = lax.broadcasted_iota(jnp.int32, (rows, blocks.shape[0]), 1).astype(jnp.float32)
    picks = [
        jnp.where(place - float(j * packing.cap) == spot_ref[:, t : t + 1], 1.0, 0.0)
        for t in range(2)
        for j in range(packing.chunks)
    ]
    if rows % 16 == 0:
        table = jnp.concatenate(picks, axis=0).astype(jnp.bfloat16)
        picked = jnp.dot(table, blocks, preferred_element_type=jnp.float32)
        picked = [picked[i * rows : (i + 1) * rows] for i in range(len(picks))]
    else:
        picked = [
            jnp.dot(pick.astype(jnp.bfloat16), blocks, preferred_element_type=jnp.float32)
            for pick in picks
        ]
    for j in range(packing.chunks):
        out_ref[:, j * packing.width : (j + 1) * packing.width] = (
            weight_ref[:, 0:1] * picked[j] + weight_ref[:, 1:2] * picked[packing.chunks + j]
        ).astype(jnp.bfloat16)


def combine(spot, weights, blocks, packing, rows, features):
    return pl.pallas_call(
        functools.partial(combine_kernel, packing),
        out_shape=jax.ShapeDtypeStruct((rows, features), jnp.bfloat16),
        in_specs=[VMEM] * (2 + len(blocks)),
        out_specs=VMEM,
        compiler_params=pltpu.CompilerParams(vmem_limit_bytes=8 << 20),
        name="combine",
    )(spot, weights, *blocks)


def partial_captions(text_hidden, caption_weight, grid):
    groups = grid.pairs * 2
    rows = text_hidden.shape[0] // (grid.experts * groups)
    bits = (grid.experts * groups).bit_length() - 1
    text = text_hidden.reshape((2,) * bits + (rows, -1))
    for bit in range(bits):
        text = jnp.roll(text, (grid.index >> (bits - 1 - bit)) & 1, axis=bit)
    text = text.reshape(grid.experts, grid.pairs, 2, rows, -1)
    text = jnp.concatenate([text[:, 1:], text[:, :1]], axis=1)
    text = [
        jnp.transpose(text[:, :, c], (1, 0, 2, 3)).reshape(-1, text_hidden.shape[1])
        for c in (1, 0)
    ]
    other, own = [
        jnp.dot(text[c], caption_weight, preferred_element_type=jnp.float32).astype(kind)
        for c, kind in enumerate((jnp.bfloat16, jnp.float32))
    ]
    high = rows * grid.experts
    return [
        value[k * high : (k + 1) * high] for value in (other, own) for k in range(grid.pairs)
    ]


def local(
    image_rows,
    text_hidden,
    caption_weight,
    mod_scale,
    mod_shift,
    router_weight,
    image_experts,
    caption_experts,
    prompt_lengths,
    w_gate,
    w_up,
    w_down,
):
    devices = lax.axis_size("dev")
    features, experts = router_weight.shape
    grid = Grid(devices, experts)
    pairs = grid.pairs
    wide, narrow = jnp.float32, jnp.bfloat16
    image_packing = Packing(image_rows.shape[0] * 3 // 4, features)
    caption_packing = Packing(text_hidden.shape[0] // devices // 2 + 1, features)

    def split(value, count):
        rows = value.shape[0] // count
        return [value[k * rows : (k + 1) * rows] for k in range(count)]

    def to_experts(blocks):
        return [grid.swap(blocks[k], 0, k) for k in range(1, experts)]

    def to_pairs(first):
        return [first] + [grid.swap(first, 1, k) for k in range(1, pairs)]

    def over_cores(values):
        return [grid.swap(value, 2, 1) for value in values]

    def join_cores(results):
        own, other = results[:pairs], results[pairs:]
        sums = [None] * pairs
        for k in list(range(1, pairs)) + [0]:
            sums[k] = own[k].astype(wide) + grid.swap(other[k], 2, 1).astype(wide)
        return sums[0], [value.astype(narrow) for value in sums[1:]]

    def from_pairs(crossing):
        return [grid.swap(value, 1, k) for k, value in enumerate(crossing, 1)]

    def from_experts(kept, received):
        total = kept
        for value in received:
            total = total + value.astype(wide)
        parts = split(total.astype(narrow), experts)
        return [parts[0]] + [grid.swap(parts[k], 0, k) for k in range(1, experts)]

    partial = partial_captions(text_hidden, caption_weight, grid)
    sums = [
        partial[pairs + i] + grid.swap(partial[i], 2, 1).astype(wide) for i in range(pairs)
    ]
    crossing = [value.astype(narrow) for value in sums[:-1]]
    received = [grid.swap(value, 1, k) for k, value in enumerate(crossing, 1)]

    rows = text_hidden.shape[0] // devices
    position = grid.index * rows + jnp.arange(rows, dtype=jnp.int32)
    prompts = jnp.arange(prompt_lengths.shape[0], dtype=jnp.int32)
    lengths = jnp.where(position[:, None] // PLEN == prompts, prompt_lengths, 0).sum(axis=1)
    ids = jnp.where((position % PLEN < lengths)[None, :], caption_experts.T, -1)
    ids = jnp.pad(ids, ((0, 0), (0, image_rows.shape[0] - rows)))
    ids = jnp.concatenate([image_experts.T, ids], axis=0)
    small = jnp.concatenate([mod_scale[None], mod_shift[None], router_weight.T], axis=0)
    (image_spot, caption_spot, image_normed), blocks = prepare(
        ids, small, image_rows, rows, [image_packing, caption_packing], experts, crossing[:1]
    )
    image_first = [blocks[0]] + to_experts(blocks)

    received[0] = tie([received[0]], blocks[1:2], HINT)
    total = sums[-1]
    for value in received:
        total = total + value.astype(wide)
    parts = split(total, experts)
    sent = [part.astype(narrow) for part in parts[1:]]
    terms = parts[:1] + [grid.swap(part, 0, k) for k, part in enumerate(sent, 1)]
    image_first = jnp.concatenate([tie([image_first[0]], sent)] + image_first[1:], axis=0)
    image_own = to_pairs(image_first)
    weights = (w_gate, w_up, w_down)

    caption_normed, blocks = modulate(terms, caption_spot, small, caption_packing, experts)
    received = to_experts(blocks)
    image_own = image_own[:1] + [tie([value], blocks[1:2]) for value in image_own[1:]]
    image_arrays = image_own + over_cores(image_own)
    caption_first = jnp.concatenate([blocks[0]] + received, axis=0)
    caption_own = to_pairs(caption_first)

    image_weights = route(image_normed, image_spot, small)
    caption_weights = route(caption_normed, caption_spot, small)
    image_results = expert_rows(
        image_arrays, *weights, image_packing, [caption_first, image_weights]
    )
    caption_own = caption_own[:1] + [tie([value], image_results[:1]) for value in caption_own[1:]]
    image_results = list(image_results[:pairs]) + [
        tie([value], caption_own[1:2]) for value in image_results[pairs:]
    ]
    image_kept, image_crossing = join_cores(image_results)
    caption_results = expert_rows(
        caption_own + over_cores(caption_own),
        *weights,
        caption_packing,
        image_crossing[:1] + [caption_weights],
    )
    image_received = [
        tie([value], caption_results[:1]) for value in from_pairs(image_crossing)
    ]
    caption_results = list(caption_results[:pairs]) + [
        tie([value], image_received[:1]) for value in caption_results[pairs:]
    ]
    caption_kept, caption_crossing = join_cores(caption_results)
    image_received = [tie([value], caption_crossing[:1]) for value in image_received]
    image_blocks = from_experts(image_kept, image_received)
    caption_received = from_pairs(caption_crossing)
    caption_blocks = from_experts(caption_kept, caption_received)

    rows = image_rows.shape[0]
    image_out = combine(image_spot, image_weights, image_blocks, image_packing, rows, features)
    rows = text_hidden.shape[0] // devices
    caption_out = combine(
        caption_spot, caption_weights, caption_blocks, caption_packing, rows, features
    )
    return (image_out, caption_out)


def solution(mesh):
    in_specs = (
        P(("groups", "dev"), None),
        P("groups", "dev"),
        P("dev", None),
        P(),
        P(),
        P(),
        P(("groups", "dev"), None),
        P(("groups", "dev"), None),
        P("groups"),
        P(None, "dev"),
        P(None, "dev"),
        P("dev", None),
    )
    out_specs = (P(("groups", "dev"), None), P(("groups", "dev"), None))
    return jax.shard_map(local, mesh=mesh, in_specs=in_specs, out_specs=out_specs, check_vma=False)
```

```python
import functools

import jax
import jax.numpy as jnp
from jax import lax
from jax.experimental import pallas as pl
from jax.experimental.pallas import tpu as pltpu
from jax.sharding import PartitionSpec as P

PLEN = 128
HINT = 1 << 33
STRIP = 512
LIMIT = 24 << 20
VMEM = pl.BlockSpec(memory_space=pltpu.VMEM)
SMEM = pl.BlockSpec(memory_space=pltpu.SMEM)
ANY = pl.BlockSpec(memory_space=pl.ANY)
HBM = pl.BlockSpec(memory_space=pltpu.HBM)


class Grid:
    def __init__(self, devices, experts):
        self.experts = experts
        self.pairs = devices // experts // 2
        index = lax.axis_index("dev")
        self.index = index
        self.expert = index // (self.pairs * 2)
        self.pair = (index // 2) % self.pairs
        self.core = index % 2

    def swap(self, value, axis, step):
        moves = []
        for expert in range(self.experts):
            for pair in range(self.pairs):
                for core in range(2):
                    to = [expert, pair, core]
                    to[axis] ^= step
                    moves.append(
                        (
                            (expert * self.pairs + pair) * 2 + core,
                            (to[0] * self.pairs + to[1]) * 2 + to[2],
                        )
                    )
        return lax.ppermute(value, "dev", moves)


class Packing:
    def __init__(self, cap, features):
        best = None
        for chunks in range(1, features // 128 + 1):
            if features % (128 * chunks):
                continue
            rows = -(-cap * chunks // 16) * 16
            cost = rows * (features // chunks)
            if best is None or cost < best[0]:
                best = (cost, chunks, rows)
        _, self.chunks, self.rows = best
        self.cap = cap
        self.width = features // self.chunks


def place(chosen, packing, experts, out_ref):
    index = lax.axis_index("dev")
    rows = chosen.shape[1]
    relative = chosen ^ (index // (lax.axis_size("dev") // experts))
    expert_at = lax.broadcasted_iota(jnp.int32, (experts, rows), 0)
    routed = (relative[0:1, :] == expert_at) | (relative[1:2, :] == expert_at)
    routed = routed & (chosen[0:1, :] >= 0)
    at = [lax.broadcasted_iota(jnp.int32, (rows, rows), d) for d in range(2)]
    before = (at[0] < at[1]).astype(jnp.float32)
    spot = jnp.dot(routed.astype(jnp.float32), before, preferred_element_type=jnp.float32)
    spot = spot + expert_at.astype(jnp.float32) * float(packing.rows)
    for t in range(2):
        own = jnp.where(relative[t : t + 1, :] == expert_at, spot, 0.0)
        own = jnp.sum(own, axis=0, keepdims=True)
        own = jnp.where(chosen[t : t + 1, :] >= 0, own, -65536.0)
        for column, value in ((t, own), (2 + t, chosen[t : t + 1, :].astype(jnp.float32))):
            out_ref[:, column : column + 1] = jnp.sum(
                jnp.where(at[0] == at[1], value, 0.0), axis=1, keepdims=True
            )


def norm_and_pack(values, small_ref, spot_ref, packing, experts, normed_ref, packed_refs):
    rows = values.shape[0]
    center = values - jnp.mean(values, axis=1, keepdims=True)
    spread = jnp.mean(center * center, axis=1, keepdims=True)
    normed = center * lax.rsqrt(spread + 1e-06) * small_ref[0:1, :] + small_ref[1:2, :]
    normed = normed.astype(jnp.bfloat16)
    normed_ref[...] = normed
    place = lax.broadcasted_iota(jnp.int32, (rows, experts * packing.rows), 1).astype(jnp.float32)
    packed = None
    for j in range(packing.chunks):
        at = place - float(j * packing.cap)
        into = jnp.where((at == spot_ref[:, 0:1]) | (at == spot_ref[:, 1:2]), 1.0, 0.0)
        term = jnp.dot(
            into.T.astype(jnp.bfloat16),
            normed[:, j * packing.width : (j + 1) * packing.width],
            preferred_element_type=jnp.float32,
        )
        packed = term if packed is None else packed + term
    for k in range(experts):
        packed_refs[k][...] = packed[k * packing.rows : (k + 1) * packing.rows].astype(
            jnp.bfloat16
        )


def prepare_kernel(packings, experts, after, ids_ref, small_ref, image_ref, *refs):
    image_spot, caption_spot, normed_ref = refs[after : after + 3]
    image_rows, caption_rows = image_spot.shape[0], caption_spot.shape[0]
    place(ids_ref[0:2, 0:image_rows], packings[0], experts, image_spot)
    place(ids_ref[2:4, 0:caption_rows], packings[1], experts, caption_spot)
    norm_and_pack(
        image_ref[...].astype(jnp.float32),
        small_ref,
        image_spot,
        packings[0],
        experts,
        normed_ref,
        refs[after + 3 :],
    )


def prepare(ids, small, image_rows, caption_rows, packings, experts, after):
    rows, features = image_rows.shape
    packed = jax.ShapeDtypeStruct((packings[0].rows, packings[0].width), jnp.bfloat16)
    results = pl.pallas_call(
        functools.partial(prepare_kernel, packings, experts, len(after)),
        out_shape=[
            jax.ShapeDtypeStruct((rows, 4), jnp.float32),
            jax.ShapeDtypeStruct((caption_rows, 4), jnp.float32),
            jax.ShapeDtypeStruct((rows, features), jnp.bfloat16),
        ]
        + [packed] * experts,
        in_specs=[VMEM] * 3 + [ANY] * len(after),
        out_specs=[VMEM] * (3 + experts),
        compiler_params=pltpu.CompilerParams(vmem_limit_bytes=8 << 20),
        name="prepare",
    )(ids, small, image_rows, *after)
    return results[:3], list(results[3:])


def tie_kernel(count, *refs):
    value = refs[0][...]
    for ref in refs[1:count]:
        value = value.astype(jnp.float32) + ref[...].astype(jnp.float32)
    refs[-1][...] = value.astype(refs[-1].dtype)


def tie(values, after, cost=0, kind=None):
    kind = kind or values[0].dtype
    return pl.pallas_call(
        functools.partial(tie_kernel, len(values)),
        out_shape=jax.ShapeDtypeStruct(values[0].shape, kind),
        in_specs=[VMEM] * len(values) + [ANY] * len(after),
        out_specs=VMEM,
        compiler_params=pltpu.CompilerParams(vmem_limit_bytes=8 << 20),
        cost_estimate=pl.CostEstimate(flops=cost, bytes_accessed=0, transcendentals=0),
        name="tie",
    )(*values, *after)


def modulate_kernel(packing, experts, count, spot_ref, small_ref, *refs):
    values = refs[0][...].astype(jnp.float32)
    for ref in refs[1:count]:
        values = values + ref[...].astype(jnp.float32)
    values = values.astype(jnp.bfloat16).astype(jnp.float32)
    norm_and_pack(
        values, small_ref, spot_ref, packing, experts, refs[count], refs[count + 1 :]
    )


def modulate(terms, spot, small, packing, experts):
    rows, features = terms[0].shape
    packed = jax.ShapeDtypeStruct((packing.rows, packing.width), jnp.bfloat16)
    results = pl.pallas_call(
        functools.partial(modulate_kernel, packing, experts, len(terms)),
        out_shape=[jax.ShapeDtypeStruct((rows, features), jnp.bfloat16)] + [packed] * experts,
        in_specs=[VMEM] * (2 + len(terms)),
        out_specs=[VMEM] * (1 + experts),
        compiler_params=pltpu.CompilerParams(vmem_limit_bytes=8 << 20),
        cost_estimate=pl.CostEstimate(flops=HINT, bytes_accessed=0, transcendentals=0),
        name="modulate",
    )(spot, small, *terms)
    return (results[0], list(results[1:]))


def route_kernel(spot_ref, normed_ref, small_ref, weight_ref):
    normed = normed_ref[...].astype(jnp.float32)
    logits = [
        jnp.sum(normed * small_ref[2 + k : 3 + k, :], axis=1, keepdims=True)
        for k in range(small_ref.shape[0] - 2)
    ]
    picked = []
    for t in range(2):
        logit = jnp.zeros_like(logits[0])
        for k, value in enumerate(logits):
            logit = jnp.where(spot_ref[:, 2 + t : 3 + t] == float(k), value, logit)
        picked.append(logit)
    weight_ref[:, 0:1] = jax.nn.sigmoid(picked[0] - picked[1])
    weight_ref[:, 1:2] = jax.nn.sigmoid(picked[1] - picked[0])


def route(normed, spot, small):
    return pl.pallas_call(
        route_kernel,
        out_shape=jax.ShapeDtypeStruct((spot.shape[0], 2), jnp.float32),
        in_specs=[VMEM] * 3,
        out_specs=VMEM,
        compiler_params=pltpu.CompilerParams(vmem_limit_bytes=8 << 20),
        name="route",
    )(spot, normed, small)


def cuts(units):
    edges = [0] + list(range(256, units - 255, 512)) + [units]
    return list(zip(edges[:-1], edges[1:]))


def expert_kernel(packing, unit_cuts, count, after, fetch, *refs):
    row_refs = refs[:count]
    gate_hbm, up_hbm, down_hbm = refs[count : count + 3]
    place = count + 3 + after
    out_refs = refs[place : place + count]
    if fetch:
        gate_ref, up_ref, down_ref, rows_ref, total_ref, packed_ref, sems = refs[place + count :]
    else:
        gate_ref, up_ref, down_ref = gate_hbm, up_hbm, down_hbm
        rows_ref, total_ref, packed_ref = refs[place + count :]
    copies = []
    for i, (lo, hi) in enumerate(unit_cuts):
        for t, (source, target) in enumerate(
            ((gate_hbm, gate_ref), (up_hbm, up_ref), (down_hbm, down_ref))
        ):
            if fetch:
                copies.append(
                    pltpu.make_async_copy(source.at[lo:hi], target.at[lo:hi], sems.at[3 * i + t])
                )
    for copy in copies[:2]:
        copy.start()

    cap, chunks, width, high = packing.cap, packing.chunks, packing.width, packing.rows
    per_ref = row_refs[0].shape[0] // high
    blocks = count * per_ref
    rows = blocks * cap
    lanes = width // 128
    for i, ref in enumerate(row_refs):
        for c in range(lanes):
            packed_ref[c, i * per_ref * high : (i + 1) * per_ref * high, :] = ref[
                :, c * 128 : (c + 1) * 128
            ].astype(jnp.float32)
    spare = rows_ref.shape[1] - rows
    for j in range(chunks):
        for c in range(lanes):
            for slot in range(cap):
                total_ref[j * lanes + c, pl.ds(slot, blocks, stride=cap), :] = packed_ref[
                    c, pl.ds(j * cap + slot, blocks, stride=high), :
                ]
    for copy in copies[2:6]:
        copy.start()
    for c in range(chunks * lanes):
        part = total_ref[c, 0:rows, :]
        if spare:
            part = jnp.concatenate([part, jnp.zeros((spare, 128), jnp.float32)], axis=0)
        rows_ref[c * 128 : (c + 1) * 128, :] = part.astype(jnp.bfloat16).T

    def down(i, hidden):
        lo, hi = unit_cuts[i]
        term = jnp.dot(hidden, down_ref[lo:hi, :], preferred_element_type=jnp.float32)
        for c in range(chunks * lanes):
            if i == 0:
                total_ref[c, 0:rows, :] = term[:, c * 128 : (c + 1) * 128]
            else:
                total_ref[c, 0:rows, :] += term[:, c * 128 : (c + 1) * 128]

    features = gate_hbm.shape[1]

    def product(weight_ref, lo, hi):
        terms = [
            jnp.dot(
                weight_ref[lo:hi, strip : strip + STRIP],
                rows_ref[strip : strip + STRIP, :],
                preferred_element_type=jnp.float32,
            )
            for strip in range(0, features, STRIP)
        ]
        return functools.reduce(jnp.add, terms)

    def gated(gate, up):
        return (gate * jax.nn.sigmoid(gate) * up).astype(jnp.bfloat16).T[0:rows]

    inner = None
    for i, (lo, hi) in enumerate(unit_cuts):
        for copy in copies[max(3 * i - 1, 0) : 3 * i + 2]:
            copy.wait()
        for copy in copies[3 * (i + 2) : 3 * (i + 3)]:
            copy.start()
        following = product(gate_ref, lo, hi), product(up_ref, lo, hi)
        if i > 0:
            down(i - 1, gated(*inner))
        inner = following
    for copy in copies[-1:]:
        copy.wait()
    down(len(unit_cuts) - 1, gated(*inner))

    for c in range(lanes):
        for row in range(chunks * cap, high):
            packed_ref[c, pl.ds(row, blocks, stride=high), :] = jnp.zeros(
                (blocks, 128), jnp.float32
            )
        for j in range(chunks):
            for slot in range(cap):
                packed_ref[c, pl.ds(j * cap + slot, blocks, stride=high), :] = total_ref[
                    j * lanes + c, pl.ds(slot, blocks, stride=cap), :
                ]
    for i, ref in enumerate(out_refs):
        for c in range(lanes):
            columns = slice(c * 128, (c + 1) * 128)
            part = packed_ref[c, i * per_ref * high : (i + 1) * per_ref * high, :]
            ref[:, columns] = part.astype(jnp.bfloat16)


def expert_rows(arrays, w_gate, w_up, w_down, packing, after, fetch):
    units, features = w_down.shape
    rows = len(arrays) * (arrays[0].shape[0] // packing.rows) * packing.cap
    unit_cuts = cuts(units)
    weight = jax.ShapeDtypeStruct((units, features), jnp.bfloat16)
    kept = 3 if fetch else 0
    results = pl.pallas_call(
        functools.partial(expert_kernel, packing, unit_cuts, len(arrays), len(after), fetch),
        out_shape=[jax.ShapeDtypeStruct(arrays[0].shape, jnp.bfloat16)] * len(arrays)
        + [weight] * kept,
        in_specs=[VMEM] * len(arrays) + [HBM if fetch else VMEM] * 3 + [ANY] * len(after),
        out_specs=[VMEM] * (len(arrays) + kept),
        scratch_shapes=[
            pltpu.VMEM((features, -(-rows // 128) * 128), jnp.bfloat16),
            pltpu.VMEM((features // 128, rows + 16, 128), jnp.float32),
            pltpu.VMEM(
                (packing.width // 128, len(arrays) * arrays[0].shape[0] + packing.rows, 128),
                jnp.float32,
            ),
        ]
        + [pltpu.SemaphoreType.DMA((3 * len(unit_cuts),))] * (kept // 3),
        compiler_params=pltpu.CompilerParams(vmem_limit_bytes=LIMIT),
        cost_estimate=pl.CostEstimate(
            flops=6 * rows * features * units,
            bytes_accessed=6 * features * units,
            transcendentals=rows * units,
        ),
        name="experts",
    )(*arrays, w_gate, w_up, w_down, *after)
    return list(results[: len(arrays)]), list(results[len(arrays) :])


def combine_kernel(packing, spot_ref, weight_ref, *refs):
    block_refs, out_ref = refs[:-1], refs[-1]
    rows = out_ref.shape[0]
    blocks = jnp.concatenate([ref[...] for ref in block_refs], axis=0)
    place = lax.broadcasted_iota(jnp.int32, (rows, blocks.shape[0]), 1).astype(jnp.float32)
    picks = [
        jnp.where(place - float(j * packing.cap) == spot_ref[:, t : t + 1], 1.0, 0.0)
        for t in range(2)
        for j in range(packing.chunks)
    ]
    if rows % 16 == 0:
        table = jnp.concatenate(picks, axis=0).astype(jnp.bfloat16)
        picked = jnp.dot(table, blocks, preferred_element_type=jnp.float32)
        picked = [picked[i * rows : (i + 1) * rows] for i in range(len(picks))]
    else:
        picked = [
            jnp.dot(pick.astype(jnp.bfloat16), blocks, preferred_element_type=jnp.float32)
            for pick in picks
        ]
    for j in range(packing.chunks):
        out_ref[:, j * packing.width : (j + 1) * packing.width] = (
            weight_ref[:, 0:1] * picked[j] + weight_ref[:, 1:2] * picked[packing.chunks + j]
        ).astype(jnp.bfloat16)


def combine(spot, weights, blocks, packing, rows, features):
    return pl.pallas_call(
        functools.partial(combine_kernel, packing),
        out_shape=jax.ShapeDtypeStruct((rows, features), jnp.bfloat16),
        in_specs=[VMEM] * (2 + len(blocks)),
        out_specs=VMEM,
        compiler_params=pltpu.CompilerParams(vmem_limit_bytes=8 << 20),
        name="combine",
    )(spot, weights, *blocks)


def partial_captions(text_hidden, caption_weight, grid):
    groups = grid.pairs * 2
    rows = text_hidden.shape[0] // (grid.experts * groups)
    bits = (grid.experts * groups).bit_length() - 1
    text = text_hidden.reshape((2,) * bits + (rows, -1))
    for bit in range(bits):
        text = jnp.roll(text, (grid.index >> (bits - 1 - bit)) & 1, axis=bit)
    text = text.reshape(grid.experts, grid.pairs, 2, rows, -1)
    text = jnp.concatenate([text[:, 1:], text[:, :1]], axis=1)
    text = [
        jnp.transpose(text[:, :, c], (1, 0, 2, 3)).reshape(-1, text_hidden.shape[1])
        for c in (1, 0)
    ]
    other, own = [
        jnp.dot(text[c], caption_weight, preferred_element_type=jnp.float32).astype(kind)
        for c, kind in enumerate((jnp.bfloat16, jnp.float32))
    ]
    high = rows * grid.experts
    return [
        value[k * high : (k + 1) * high] for value in (other, own) for k in range(grid.pairs)
    ]


def local(
    image_rows,
    text_hidden,
    caption_weight,
    mod_scale,
    mod_shift,
    router_weight,
    image_experts,
    caption_experts,
    prompt_lengths,
    w_gate,
    w_up,
    w_down,
):
    devices = lax.axis_size("dev")
    features, experts = router_weight.shape
    grid = Grid(devices, experts)
    pairs = grid.pairs
    wide, narrow = jnp.float32, jnp.bfloat16
    image_packing = Packing(image_rows.shape[0] * 3 // 4, features)
    caption_packing = Packing(text_hidden.shape[0] // devices // 2 + 1, features)

    def split(value, count):
        rows = value.shape[0] // count
        return [value[k * rows : (k + 1) * rows] for k in range(count)]

    def to_experts(blocks):
        return [grid.swap(blocks[k], 0, k) for k in range(1, experts)]

    def to_pairs(first):
        return [first] + [grid.swap(first, 1, k) for k in range(1, pairs)]

    def over_cores(values):
        return [grid.swap(value, 2, 1) for value in values]

    def join_cores(results):
        own, other = results[:pairs], results[pairs:]
        crossing = [
            tie([own[k], grid.swap(other[k], 2, 1)], [], 0, narrow) for k in range(1, pairs)
        ]
        return own[0].astype(wide) + grid.swap(other[0], 2, 1).astype(wide), crossing

    def from_pairs(crossing):
        return [grid.swap(value, 1, k) for k, value in enumerate(crossing, 1)]

    def from_experts(kept, received):
        total = kept
        for value in received:
            total = total + value.astype(wide)
        parts = split(total.astype(narrow), experts)
        return [parts[0]] + [grid.swap(parts[k], 0, k) for k in range(1, experts)]

    partial = partial_captions(text_hidden, caption_weight, grid)
    sums = [
        partial[pairs + i] + grid.swap(partial[i], 2, 1).astype(wide) for i in range(pairs)
    ]
    crossing = [value.astype(narrow) for value in sums[:-1]]
    received = [grid.swap(value, 1, k) for k, value in enumerate(crossing, 1)]

    rows = text_hidden.shape[0] // devices
    position = grid.index * rows + jnp.arange(rows, dtype=jnp.int32)
    prompts = jnp.arange(prompt_lengths.shape[0], dtype=jnp.int32)
    lengths = jnp.where(position[:, None] // PLEN == prompts, prompt_lengths, 0).sum(axis=1)
    ids = jnp.where((position % PLEN < lengths)[None, :], caption_experts.T, -1)
    ids = jnp.pad(ids, ((0, 0), (0, image_rows.shape[0] - rows)))
    ids = jnp.concatenate([image_experts.T, ids], axis=0)
    small = jnp.concatenate([mod_scale[None], mod_shift[None], router_weight.T], axis=0)
    (image_spot, caption_spot, image_normed), blocks = prepare(
        ids, small, image_rows, rows, [image_packing, caption_packing], experts, crossing[:1]
    )
    image_first = [blocks[0]] + to_experts(blocks)

    received[0] = tie([received[0]], blocks[1:2], HINT)
    total = sums[-1]
    for value in received:
        total = total + value.astype(wide)
    parts = split(total, experts)
    sent = [part.astype(narrow) for part in parts[1:]]
    terms = parts[:1] + [grid.swap(part, 0, k) for k, part in enumerate(sent, 1)]
    image_first = jnp.concatenate([tie([image_first[0]], sent)] + image_first[1:], axis=0)
    image_own = to_pairs(image_first)
    weights = (w_gate.T, w_up.T, w_down)

    caption_normed, blocks = modulate(terms, caption_spot, small, caption_packing, experts)
    received = to_experts(blocks)
    image_own = image_own[:1] + [tie([value], blocks[1:2]) for value in image_own[1:]]
    image_arrays = image_own + over_cores(image_own)
    caption_first = jnp.concatenate([blocks[0]] + received, axis=0)
    caption_own = to_pairs(caption_first)

    image_weights = route(image_normed, image_spot, small)
    caption_weights = route(caption_normed, caption_spot, small)
    image_results, weights = expert_rows(
        image_arrays, *weights, image_packing, [caption_first, image_weights], True
    )
    caption_own = caption_own[:1] + [tie([value], image_results[:1]) for value in caption_own[1:]]
    image_results = image_results[:pairs] + [
        tie([value], caption_own[1:2]) for value in image_results[pairs:]
    ]
    image_kept, image_crossing = join_cores(image_results)
    caption_results, _ = expert_rows(
        caption_own + over_cores(caption_own),
        *weights,
        caption_packing,
        image_crossing[:1] + [caption_weights],
        False,
    )
    image_received = [
        tie([value], caption_results[:1]) for value in from_pairs(image_crossing)
    ]
    caption_results = caption_results[:pairs] + [
        tie([value], image_received[:1]) for value in caption_results[pairs:]
    ]
    caption_kept, caption_crossing = join_cores(caption_results)
    image_received = [tie([value], caption_crossing[:1]) for value in image_received]
    image_blocks = from_experts(image_kept, image_received)
    caption_received = from_pairs(caption_crossing)
    caption_blocks = from_experts(caption_kept, caption_received)

    rows = image_rows.shape[0]
    image_out = combine(image_spot, image_weights, image_blocks, image_packing, rows, features)
    rows = text_hidden.shape[0] // devices
    caption_out = combine(
        caption_spot, caption_weights, caption_blocks, caption_packing, rows, features
    )
    return (image_out, caption_out)


def solution(mesh):
    in_specs = (
        P(("groups", "dev"), None),
        P("groups", "dev"),
        P("dev", None),
        P(),
        P(),
        P(),
        P(("groups", "dev"), None),
        P(("groups", "dev"), None),
        P("groups"),
        P(None, "dev"),
        P(None, "dev"),
        P("dev", None),
    )
    out_specs = (P(("groups", "dev"), None), P(("groups", "dev"), None))
    return jax.shard_map(local, mesh=mesh, in_specs=in_specs, out_specs=out_specs, check_vma=False)
```

```python
import functools

import jax
import jax.numpy as jnp
from jax import lax
from jax.experimental import pallas as pl
from jax.experimental.pallas import tpu as pltpu
from jax.sharding import PartitionSpec as P

PLEN = 128
HINT = 1 << 33
STRIP = 512
LIMIT = 8 << 20
VMEM = pl.BlockSpec(memory_space=pltpu.VMEM)
SMEM = pl.BlockSpec(memory_space=pltpu.SMEM)
ANY = pl.BlockSpec(memory_space=pl.ANY)
HBM = pl.BlockSpec(memory_space=pltpu.HBM)


class Grid:
    def __init__(self, devices, experts):
        self.experts = experts
        self.pairs = devices // experts // 2
        index = lax.axis_index("dev")
        self.index = index
        self.expert = index // (self.pairs * 2)
        self.pair = (index // 2) % self.pairs
        self.core = index % 2

    def swap(self, value, axis, step):
        moves = []
        for expert in range(self.experts):
            for pair in range(self.pairs):
                for core in range(2):
                    to = [expert, pair, core]
                    to[axis] ^= step
                    moves.append(
                        (
                            (expert * self.pairs + pair) * 2 + core,
                            (to[0] * self.pairs + to[1]) * 2 + to[2],
                        )
                    )
        return lax.ppermute(value, "dev", moves)


class Packing:
    def __init__(self, cap, features):
        best = None
        for chunks in range(1, features // 128 + 1):
            if features % (128 * chunks):
                continue
            rows = -(-cap * chunks // 16) * 16
            cost = rows * (features // chunks)
            if best is None or cost < best[0]:
                best = (cost, chunks, rows)
        _, self.chunks, self.rows = best
        self.cap = cap
        self.width = features // self.chunks


def place(chosen, packing, experts, out_ref):
    index = lax.axis_index("dev")
    rows = chosen.shape[1]
    relative = chosen ^ (index // (lax.axis_size("dev") // experts))
    expert_at = lax.broadcasted_iota(jnp.int32, (experts, rows), 0)
    routed = (relative[0:1, :] == expert_at) | (relative[1:2, :] == expert_at)
    routed = routed & (chosen[0:1, :] >= 0)
    at = [lax.broadcasted_iota(jnp.int32, (rows, rows), d) for d in range(2)]
    before = (at[0] < at[1]).astype(jnp.float32)
    spot = jnp.dot(routed.astype(jnp.float32), before, preferred_element_type=jnp.float32)
    spot = spot + expert_at.astype(jnp.float32) * float(packing.rows)
    for t in range(2):
        own = jnp.where(relative[t : t + 1, :] == expert_at, spot, 0.0)
        own = jnp.sum(own, axis=0, keepdims=True)
        own = jnp.where(chosen[t : t + 1, :] >= 0, own, -65536.0)
        for column, value in ((t, own), (2 + t, chosen[t : t + 1, :].astype(jnp.float32))):
            out_ref[:, column : column + 1] = jnp.sum(
                jnp.where(at[0] == at[1], value, 0.0), axis=1, keepdims=True
            )


def norm_and_pack(values, small_ref, spot_ref, packing, experts, normed_ref, packed_refs):
    rows = values.shape[0]
    center = values - jnp.mean(values, axis=1, keepdims=True)
    spread = jnp.mean(center * center, axis=1, keepdims=True)
    normed = center * lax.rsqrt(spread + 1e-06) * small_ref[0:1, :] + small_ref[1:2, :]
    normed = normed.astype(jnp.bfloat16)
    normed_ref[...] = normed
    place = lax.broadcasted_iota(jnp.int32, (rows, experts * packing.rows), 1).astype(jnp.float32)
    packed = None
    for j in range(packing.chunks):
        at = place - float(j * packing.cap)
        into = jnp.where((at == spot_ref[:, 0:1]) | (at == spot_ref[:, 1:2]), 1.0, 0.0)
        term = jnp.dot(
            into.T.astype(jnp.bfloat16),
            normed[:, j * packing.width : (j + 1) * packing.width],
            preferred_element_type=jnp.float32,
        )
        packed = term if packed is None else packed + term
    for k in range(experts):
        packed_refs[k][...] = packed[k * packing.rows : (k + 1) * packing.rows].astype(
            jnp.bfloat16
        )


def prepare_kernel(packings, experts, after, ids_ref, small_ref, image_ref, *refs):
    image_spot, caption_spot, normed_ref = refs[after : after + 3]
    image_rows, caption_rows = image_spot.shape[0], caption_spot.shape[0]
    place(ids_ref[0:2, 0:image_rows], packings[0], experts, image_spot)
    place(ids_ref[2:4, 0:caption_rows], packings[1], experts, caption_spot)
    norm_and_pack(
        image_ref[...].astype(jnp.float32),
        small_ref,
        image_spot,
        packings[0],
        experts,
        normed_ref,
        refs[after + 3 :],
    )


def prepare(ids, small, image_rows, caption_rows, packings, experts, after):
    rows, features = image_rows.shape
    packed = jax.ShapeDtypeStruct((packings[0].rows, packings[0].width), jnp.bfloat16)
    results = pl.pallas_call(
        functools.partial(prepare_kernel, packings, experts, len(after)),
        out_shape=[
            jax.ShapeDtypeStruct((rows, 4), jnp.float32),
            jax.ShapeDtypeStruct((caption_rows, 4), jnp.float32),
            jax.ShapeDtypeStruct((rows, features), jnp.bfloat16),
        ]
        + [packed] * experts,
        in_specs=[VMEM] * 3 + [ANY] * len(after),
        out_specs=[VMEM] * (3 + experts),
        compiler_params=pltpu.CompilerParams(vmem_limit_bytes=8 << 20),
        name="prepare",
    )(ids, small, image_rows, *after)
    return results[:3], list(results[3:])


def tie_kernel(count, *refs):
    value = refs[0][...]
    for ref in refs[1:count]:
        value = value.astype(jnp.float32) + ref[...].astype(jnp.float32)
    refs[-1][...] = value.astype(refs[-1].dtype)


def tie(values, after, cost=0, kind=None):
    kind = kind or values[0].dtype
    return pl.pallas_call(
        functools.partial(tie_kernel, len(values)),
        out_shape=jax.ShapeDtypeStruct(values[0].shape, kind),
        in_specs=[VMEM] * len(values) + [ANY] * len(after),
        out_specs=VMEM,
        compiler_params=pltpu.CompilerParams(vmem_limit_bytes=8 << 20),
        cost_estimate=pl.CostEstimate(flops=cost, bytes_accessed=0, transcendentals=0),
        name="tie",
    )(*values, *after)


def modulate_kernel(packing, experts, count, spot_ref, small_ref, *refs):
    values = refs[0][...].astype(jnp.float32)
    for ref in refs[1:count]:
        values = values + ref[...].astype(jnp.float32)
    values = values.astype(jnp.bfloat16).astype(jnp.float32)
    norm_and_pack(
        values, small_ref, spot_ref, packing, experts, refs[count], refs[count + 1 :]
    )


def modulate(terms, spot, small, packing, experts):
    rows, features = terms[0].shape
    packed = jax.ShapeDtypeStruct((packing.rows, packing.width), jnp.bfloat16)
    results = pl.pallas_call(
        functools.partial(modulate_kernel, packing, experts, len(terms)),
        out_shape=[jax.ShapeDtypeStruct((rows, features), jnp.bfloat16)] + [packed] * experts,
        in_specs=[VMEM] * (2 + len(terms)),
        out_specs=[VMEM] * (1 + experts),
        compiler_params=pltpu.CompilerParams(vmem_limit_bytes=8 << 20),
        cost_estimate=pl.CostEstimate(flops=HINT, bytes_accessed=0, transcendentals=0),
        name="modulate",
    )(spot, small, *terms)
    return (results[0], list(results[1:]))


def route_kernel(spot_ref, normed_ref, small_ref, weight_ref):
    normed = normed_ref[...].astype(jnp.float32)
    logits = [
        jnp.sum(normed * small_ref[2 + k : 3 + k, :], axis=1, keepdims=True)
        for k in range(small_ref.shape[0] - 2)
    ]
    picked = []
    for t in range(2):
        logit = jnp.zeros_like(logits[0])
        for k, value in enumerate(logits):
            logit = jnp.where(spot_ref[:, 2 + t : 3 + t] == float(k), value, logit)
        picked.append(logit)
    weight_ref[:, 0:1] = jax.nn.sigmoid(picked[0] - picked[1])
    weight_ref[:, 1:2] = jax.nn.sigmoid(picked[1] - picked[0])


def route(normed, spot, small):
    return pl.pallas_call(
        route_kernel,
        out_shape=jax.ShapeDtypeStruct((spot.shape[0], 2), jnp.float32),
        in_specs=[VMEM] * 3,
        out_specs=VMEM,
        compiler_params=pltpu.CompilerParams(vmem_limit_bytes=8 << 20),
        name="route",
    )(spot, normed, small)


def cuts(units):
    edges = [0] + list(range(256, units - 255, 512)) + [units]
    return list(zip(edges[:-1], edges[1:]))


def concat_kernel(count, *refs):
    refs[-1][...] = jnp.concatenate([ref[...] for ref in refs[:count]], axis=0)


def concat(values, after):
    rows, columns = values[0].shape
    return pl.pallas_call(
        functools.partial(concat_kernel, len(values)),
        out_shape=jax.ShapeDtypeStruct((rows * len(values), columns), values[0].dtype),
        in_specs=[VMEM] * len(values) + [ANY] * len(after),
        out_specs=VMEM,
        compiler_params=pltpu.CompilerParams(vmem_limit_bytes=8 << 20),
        name="concat",
    )(*values, *after)


def expert_kernel(packing, unit_cuts, count, after, held, *refs):
    row_refs, sources = refs[:count], refs[count : count + 3]
    place = count + 3 + after
    out_refs, refs = refs[place : place + count], refs[place + count :]
    weight_refs = sources[:held] + refs[: 3 - held]
    gate_ref, up_ref, down_ref = weight_refs
    rows_ref, total_ref, packed_ref = refs[3 - held : 6 - held]
    copies = [[] for _ in unit_cuts]
    for i, (lo, hi) in enumerate(unit_cuts):
        for t in range(held, 3):
            copies[i].append(
                pltpu.make_async_copy(
                    sources[t].at[lo:hi], weight_refs[t].at[lo:hi], refs[-1].at[3 * i + t]
                )
            )

    def start(i):
        for copy in copies[i] if i < len(copies) else []:
            copy.start()

    start(0)

    cap, chunks, width, high = packing.cap, packing.chunks, packing.width, packing.rows
    per_ref = row_refs[0].shape[0] // high
    blocks = count * per_ref
    rows = blocks * cap
    lanes = width // 128
    for i, ref in enumerate(row_refs):
        for c in range(lanes):
            packed_ref[c, i * per_ref * high : (i + 1) * per_ref * high, :] = ref[
                :, c * 128 : (c + 1) * 128
            ].astype(jnp.float32)
    spare = rows_ref.shape[1] - rows
    for j in range(chunks):
        for c in range(lanes):
            for slot in range(cap):
                total_ref[j * lanes + c, pl.ds(slot, blocks, stride=cap), :] = packed_ref[
                    c, pl.ds(j * cap + slot, blocks, stride=high), :
                ]
    start(1)
    for c in range(chunks * lanes):
        part = total_ref[c, 0:rows, :]
        if spare:
            part = jnp.concatenate([part, jnp.zeros((spare, 128), jnp.float32)], axis=0)
        rows_ref[c * 128 : (c + 1) * 128, :] = part.astype(jnp.bfloat16).T

    def down(i, hidden):
        lo, hi = unit_cuts[i]
        term = jnp.dot(hidden, down_ref[lo:hi, :], preferred_element_type=jnp.float32)
        for c in range(chunks * lanes):
            if i == 0:
                total_ref[c, 0:rows, :] = term[:, c * 128 : (c + 1) * 128]
            else:
                total_ref[c, 0:rows, :] += term[:, c * 128 : (c + 1) * 128]

    features = gate_ref.shape[1]

    def product(weight_ref, lo, hi):
        terms = [
            jnp.dot(
                weight_ref[lo:hi, strip : strip + STRIP],
                rows_ref[strip : strip + STRIP, :],
                preferred_element_type=jnp.float32,
            )
            for strip in range(0, features, STRIP)
        ]
        return functools.reduce(jnp.add, terms)

    def gated(gate, up):
        return (gate * jax.nn.sigmoid(gate) * up).astype(jnp.bfloat16).T[0:rows]

    inner = None
    for i, (lo, hi) in enumerate(unit_cuts):
        for copy in copies[i - 1][-1:] if i > 0 else []:
            copy.wait()
        for copy in copies[i][:-1]:
            copy.wait()
        start(i + 2)
        following = product(gate_ref, lo, hi), product(up_ref, lo, hi)
        if i > 0:
            down(i - 1, gated(*inner))
        inner = following
    for copy in copies[-1][-1:]:
        copy.wait()
    down(len(unit_cuts) - 1, gated(*inner))

    for c in range(lanes):
        for row in range(chunks * cap, high):
            packed_ref[c, pl.ds(row, blocks, stride=high), :] = jnp.zeros(
                (blocks, 128), jnp.float32
            )
        for j in range(chunks):
            for slot in range(cap):
                packed_ref[c, pl.ds(j * cap + slot, blocks, stride=high), :] = total_ref[
                    j * lanes + c, pl.ds(slot, blocks, stride=cap), :
                ]
    for i, ref in enumerate(out_refs):
        for c in range(lanes):
            columns = slice(c * 128, (c + 1) * 128)
            part = packed_ref[c, i * per_ref * high : (i + 1) * per_ref * high, :]
            ref[:, columns] = part.astype(jnp.bfloat16)


def expert_rows(arrays, weights, packing, after, held):
    units, features = weights[2].shape
    rows = len(arrays) * (arrays[0].shape[0] // packing.rows) * packing.cap
    unit_cuts = cuts(units)
    weight = jax.ShapeDtypeStruct((units, features), jnp.bfloat16)
    kept = 3 - held
    results = pl.pallas_call(
        functools.partial(expert_kernel, packing, unit_cuts, len(arrays), len(after), held),
        out_shape=[jax.ShapeDtypeStruct(arrays[0].shape, jnp.bfloat16)] * len(arrays)
        + [weight] * kept,
        in_specs=[VMEM] * (len(arrays) + held) + [HBM] * kept + [ANY] * len(after),
        out_specs=[VMEM] * (len(arrays) + kept),
        scratch_shapes=[
            pltpu.VMEM((features, -(-rows // 128) * 128), jnp.bfloat16),
            pltpu.VMEM((features // 128, rows + 16, 128), jnp.float32),
            pltpu.VMEM(
                (packing.width // 128, len(arrays) * arrays[0].shape[0] + packing.rows, 128),
                jnp.float32,
            ),
        ]
        + [pltpu.SemaphoreType.DMA((3 * len(unit_cuts),))] * (kept > 0),
        compiler_params=pltpu.CompilerParams(vmem_limit_bytes=(8 << 20) + 12 * rows * features),
        cost_estimate=pl.CostEstimate(
            flops=6 * rows * features * units,
            bytes_accessed=6 * features * units,
            transcendentals=rows * units,
        ),
        name="experts",
    )(*arrays, *weights, *after)
    results = list(results)
    return results[: len(arrays)], list(weights[:held]) + results[len(arrays) :]


def combine_kernel(packing, spot_ref, weight_ref, *refs):
    block_refs, out_ref = refs[:-1], refs[-1]
    rows = out_ref.shape[0]
    blocks = jnp.concatenate([ref[...] for ref in block_refs], axis=0)
    place = lax.broadcasted_iota(jnp.int32, (rows, blocks.shape[0]), 1).astype(jnp.float32)
    picks = [
        jnp.where(place - float(j * packing.cap) == spot_ref[:, t : t + 1], 1.0, 0.0)
        for t in range(2)
        for j in range(packing.chunks)
    ]
    if rows % 16 == 0:
        table = jnp.concatenate(picks, axis=0).astype(jnp.bfloat16)
        picked = jnp.dot(table, blocks, preferred_element_type=jnp.float32)
        picked = [picked[i * rows : (i + 1) * rows] for i in range(len(picks))]
    else:
        picked = [
            jnp.dot(pick.astype(jnp.bfloat16), blocks, preferred_element_type=jnp.float32)
            for pick in picks
        ]
    for j in range(packing.chunks):
        out_ref[:, j * packing.width : (j + 1) * packing.width] = (
            weight_ref[:, 0:1] * picked[j] + weight_ref[:, 1:2] * picked[packing.chunks + j]
        ).astype(jnp.bfloat16)


def combine(spot, weights, blocks, packing, rows, features):
    return pl.pallas_call(
        functools.partial(combine_kernel, packing),
        out_shape=jax.ShapeDtypeStruct((rows, features), jnp.bfloat16),
        in_specs=[VMEM] * (2 + len(blocks)),
        out_specs=VMEM,
        compiler_params=pltpu.CompilerParams(vmem_limit_bytes=8 << 20),
        name="combine",
    )(spot, weights, *blocks)


def partial_captions(text_hidden, caption_weight, grid):
    groups = grid.pairs * 2
    rows = text_hidden.shape[0] // (grid.experts * groups)
    bits = (grid.experts * groups).bit_length() - 1
    text = text_hidden.reshape((2,) * bits + (rows, -1))
    for bit in range(bits):
        text = jnp.roll(text, (grid.index >> (bits - 1 - bit)) & 1, axis=bit)
    text = text.reshape(grid.experts, grid.pairs, 2, rows, -1)
    text = jnp.concatenate([text[:, 1:], text[:, :1]], axis=1)
    text = [
        jnp.transpose(text[:, :, c], (1, 0, 2, 3)).reshape(-1, text_hidden.shape[1])
        for c in (1, 0)
    ]
    other, own = [
        jnp.dot(text[c], caption_weight, preferred_element_type=jnp.float32).astype(kind)
        for c, kind in enumerate((jnp.bfloat16, jnp.float32))
    ]
    high = rows * grid.experts
    return [
        value[k * high : (k + 1) * high] for value in (other, own) for k in range(grid.pairs)
    ]


def local(
    image_rows,
    text_hidden,
    caption_weight,
    mod_scale,
    mod_shift,
    router_weight,
    image_experts,
    caption_experts,
    prompt_lengths,
    w_gate,
    w_up,
    w_down,
):
    devices = lax.axis_size("dev")
    features, experts = router_weight.shape
    grid = Grid(devices, experts)
    pairs = grid.pairs
    wide, narrow = jnp.float32, jnp.bfloat16
    image_packing = Packing(image_rows.shape[0] * 3 // 4, features)
    caption_packing = Packing(text_hidden.shape[0] // devices // 2 + 1, features)

    def split(value, count):
        rows = value.shape[0] // count
        return [value[k * rows : (k + 1) * rows] for k in range(count)]

    def to_experts(blocks):
        return [grid.swap(blocks[k], 0, k) for k in range(1, experts)]

    def to_pairs(first):
        return [first] + [grid.swap(first, 1, k) for k in range(1, pairs)]

    def over_cores(values):
        return [grid.swap(value, 2, 1) for value in values]

    def join_cores(results):
        own, other = results[:pairs], results[pairs:]
        crossing = [
            tie([own[k], grid.swap(other[k], 2, 1)], [], 0, narrow) for k in range(1, pairs)
        ]
        return own[0].astype(wide) + grid.swap(other[0], 2, 1).astype(wide), crossing

    def from_pairs(crossing):
        return [grid.swap(value, 1, k) for k, value in enumerate(crossing, 1)]

    def from_experts(kept, received):
        total = kept
        for value in received:
            total = total + value.astype(wide)
        parts = split(total.astype(narrow), experts)
        return [parts[0]] + [grid.swap(parts[k], 0, k) for k in range(1, experts)]

    partial = partial_captions(text_hidden, caption_weight, grid)
    sums = [
        partial[pairs + i] + grid.swap(partial[i], 2, 1).astype(wide) for i in range(pairs)
    ]
    crossing = [value.astype(narrow) for value in sums[:-1]]
    received = [grid.swap(value, 1, k) for k, value in enumerate(crossing, 1)]

    rows = text_hidden.shape[0] // devices
    position = grid.index * rows + jnp.arange(rows, dtype=jnp.int32)
    prompts = jnp.arange(prompt_lengths.shape[0], dtype=jnp.int32)
    lengths = jnp.where(position[:, None] // PLEN == prompts, prompt_lengths, 0).sum(axis=1)
    ids = jnp.where((position % PLEN < lengths)[None, :], caption_experts.T, -1)
    ids = jnp.pad(ids, ((0, 0), (0, image_rows.shape[0] - rows)))
    ids = jnp.concatenate([image_experts.T, ids], axis=0)
    small = jnp.concatenate([mod_scale[None], mod_shift[None], router_weight.T], axis=0)
    (image_spot, caption_spot, image_normed), blocks = prepare(
        ids, small, image_rows, rows, [image_packing, caption_packing], experts, crossing[:1]
    )
    image_first = [blocks[0]] + to_experts(blocks)

    received[0] = tie([received[0]], blocks[1:2], HINT)
    total = sums[-1]
    for value in received:
        total = total + value.astype(wide)
    parts = split(total, experts)
    sent = [part.astype(narrow) for part in parts[1:]]
    terms = parts[:1] + [grid.swap(part, 0, k) for k, part in enumerate(sent, 1)]
    image_first = jnp.concatenate([tie([image_first[0]], sent)] + image_first[1:], axis=0)
    image_own = to_pairs(image_first)
    weights = (w_gate.T, w_up.T, w_down)

    caption_normed, blocks = modulate(terms, caption_spot, small, caption_packing, experts)
    received = to_experts(blocks)
    image_own = image_own[:1] + [tie([value], blocks[1:2]) for value in image_own[1:]]
    image_arrays = image_own + over_cores(image_own)
    caption_first = concat([blocks[0]] + received, [])
    caption_own = to_pairs(caption_first)

    image_weights = route(image_normed, image_spot, small)
    caption_weights = route(caption_normed, caption_spot, small)
    image_results, weights = expert_rows(
        image_arrays, weights, image_packing, [caption_first, image_weights], 3
    )
    caption_own = caption_own[:1] + [tie([value], image_results[:1]) for value in caption_own[1:]]
    image_results = image_results[:pairs] + [
        tie([value], caption_own[1:2]) for value in image_results[pairs:]
    ]
    image_kept, image_crossing = join_cores(image_results)
    caption_results, _ = expert_rows(
        caption_own + over_cores(caption_own),
        weights,
        caption_packing,
        image_crossing[:1] + [caption_weights],
        3,
    )
    image_received = [
        tie([value], caption_results[:1]) for value in from_pairs(image_crossing)
    ]
    caption_results = caption_results[:pairs] + [
        tie([value], image_received[:1]) for value in caption_results[pairs:]
    ]
    caption_kept, caption_crossing = join_cores(caption_results)
    image_received = [tie([value], caption_crossing[:1]) for value in image_received]
    image_blocks = from_experts(image_kept, image_received)
    caption_received = from_pairs(caption_crossing)
    caption_blocks = from_experts(caption_kept, caption_received)

    rows = image_rows.shape[0]
    image_out = combine(image_spot, image_weights, image_blocks, image_packing, rows, features)
    rows = text_hidden.shape[0] // devices
    caption_out = combine(
        caption_spot, caption_weights, caption_blocks, caption_packing, rows, features
    )
    return (image_out, caption_out)


def solution(mesh):
    in_specs = (
        P(("groups", "dev"), None),
        P("groups", "dev"),
        P("dev", None),
        P(),
        P(),
        P(),
        P(("groups", "dev"), None),
        P(("groups", "dev"), None),
        P("groups"),
        P(None, "dev"),
        P(None, "dev"),
        P("dev", None),
    )
    out_specs = (P(("groups", "dev"), None), P(("groups", "dev"), None))
    return jax.shard_map(local, mesh=mesh, in_specs=in_specs, out_specs=out_specs, check_vma=False)
```
